32 devices in a mesh: ctx: 16 (over z, y, x), fsdp: 2 (over core).
Axes of the slice: x: 2, y: 2, z: 4, core: 2. Of those that a mesh axis runs over, the one named last changes fastest.
Arguments:
- features: bfloat16 [3, 2048, 6144], P(None, 'ctx', 'fsdp'), may hold values from -6 to 6
- cotangent: bfloat16 [2048, 6144], P('ctx', 'fsdp'), may hold values from -6 to 6
- master_filters: float32 [4, 7, 384], P(None, None, 'fsdp'), may hold values from -2 to 2
Outputs:
- mixed: bfloat16 [2048, 6144], P('ctx', 'fsdp')
- feature_grads: bfloat16 [3, 2048, 6144], P(None, 'ctx', 'fsdp')
- filter_grads: float32 [4, 7, 384], P(None, None, 'fsdp')
The draws below stay inside these ranges and needn't reach their ends.
All inputs are finite; a program needn't handle non-finite values.
Results may differ from the reference program's by a relative error of at most 0.007.
Values may be sent and summed in bfloat16 or wider, within the bound.
No kernel may reach another device: no remote copies, remote signals or barrier semaphores. Data moves between devices by JAX's collectives and lax.ppermute only.
A program may use at most 64 MiB of HBM per device.

```python
import math
import jax
import jax.numpy as jnp
from jax import lax

C = 6144
G = 384
TAPS = 7
L = 2048


def block_levels(stream_key, dims, split, low, largest):
    def one(dim, parts):
        draws = jax.random.uniform(jax.random.fold_in(jax.random.fold_in(stream_key, 6), dim), (parts,), jnp.float32, low / len(split), largest / len(split))
        return jnp.repeat(jnp.exp(draws), dims[dim] // parts).reshape((-1,) + (1,) * (len(dims) - dim - 1))

    loudness = one(*split[0])
    for cut in split[1:]:
        loudness = loudness * one(*cut)
    return loudness


def bell_draw(key, extent, deviation, most, split=(), kind=jnp.bfloat16):
    level = block_levels(key, extent, split, -0.22, 0.18) if split else 1.0
    values = jax.random.normal(key, extent, jnp.float32) * deviation * level
    return jnp.minimum(jnp.maximum(values, -most), most).astype(kind)


def setup_inputs(seed: int = 0) -> dict:
    arg_keys = jax.random.split(jax.random.key(seed), 4)
    return {
        "features": bell_draw(arg_keys[0], (3, L, C), 1.0, 6.0, ((1, 16), (2, 2))),
        "cotangent": bell_draw(arg_keys[1], (L, C), 1.0, 6.0, ((0, 16), (1, 2))),
        "master_filters": bell_draw(arg_keys[2], (4, TAPS, G), TAPS ** -0.5, 2.0, ((2, 2),), jnp.float32),
    }


def causal(extended, weights):
    reach = weights.shape[0] - 1
    length = extended.shape[0] - reach
    result = weights[0] * extended[reach:reach + length]
    for lag in range(1, weights.shape[0]):
        result = result + weights[lag] * extended[reach - lag:reach - lag + length]
    return result

def anticausal(extended, weights):
    reach = weights.shape[0] - 1
    length = extended.shape[0] - reach
    result = weights[0] * extended[0:length]
    for lag in range(1, weights.shape[0]):
        result = result + weights[lag] * extended[lag:lag + length]
    return result

def reference(features, cotangent, master_filters):
    length = features.shape[1]
    channels = features.shape[2]
    groups = master_filters.shape[2]
    reach = master_filters.shape[1] - 1
    repeats = channels // groups
    rounded = master_filters.astype(jnp.bfloat16).astype(jnp.float32)
    weights = jnp.tile(rounded, (1, 1, repeats))
    width = math.gcd(channels, 512)
    count = channels // width

    def front(values):
        return jnp.pad(values, ((reach, 0), (0, 0)))

    def back(values):
        return jnp.pad(values, ((0, reach), (0, 0)))

    def one_slab(offset):
        inputs = lax.dynamic_slice_in_dim(features, offset, width, 2).astype(jnp.float32)
        upstream = lax.dynamic_slice_in_dim(cotangent, offset, width, 1).astype(jnp.float32)
        local_w = lax.dynamic_slice_in_dim(weights, offset, width, 2)
        padded = [front(inputs[i]) for i in range(3)]
        q_conv = causal(padded[0], local_w[0])
        k_conv = causal(padded[1], local_w[1])
        v_conv = causal(padded[2], local_w[2])
        product = k_conv * v_conv
        product_pad = front(product)
        mixer = causal(product_pad, local_w[3])
        mixed = (q_conv * mixer).astype(jnp.bfloat16)
        grad_qconv = upstream * mixer
        grad_mixer = upstream * q_conv
        grad_product = anticausal(back(grad_mixer), local_w[3])
        grad_kconv = grad_product * v_conv
        grad_vconv = grad_product * k_conv
        grad_q = anticausal(back(grad_qconv), local_w[0])
        grad_k = anticausal(back(grad_kconv), local_w[1])
        grad_v = anticausal(back(grad_vconv), local_w[2])
        feature_grads = jnp.stack([grad_q, grad_k, grad_v]).astype(jnp.bfloat16)
        pairs = ((grad_qconv, padded[0]), (grad_kconv, padded[1]), (grad_vconv, padded[2]), (grad_mixer, product_pad))
        rows_out = []
        for grad_term, source in pairs:
            rows_out.append(jnp.stack([lax.optimization_barrier(jnp.sum(grad_term * source[reach - lag:reach - lag + length], axis=0)) for lag in range(reach + 1)]))
        return (mixed, feature_grads, jnp.stack(rows_out))
    offsets = (jnp.arange(count) * width).astype(jnp.int32)
    mixed_b, grads_b, filt_b = lax.map(one_slab, offsets)
    mixed = jnp.transpose(mixed_b, (1, 0, 2)).reshape(length, channels)
    feature_grads = jnp.transpose(grads_b, (1, 2, 0, 3)).reshape(3, length, channels)
    per_channel = jnp.transpose(filt_b, (1, 2, 0, 3)).reshape(4, reach + 1, channels)
    summed = lax.optimization_barrier(jnp.sum(per_channel.reshape(4, reach + 1, repeats, groups), axis=2))
    factor = 1.0 / math.sqrt(length * repeats)
    return (mixed, feature_grads, summed * factor)
```

```python
import functools
import math

import jax
import jax.numpy as jnp
from jax import lax
from jax.experimental import pallas as pl
from jax.experimental.pallas import tpu as pltpu
from jax.sharding import PartitionSpec as P

LANES = 128
PAD = 16
STEP = 16


def shift_rows(value, axis, by):
    size = lax.axis_size(axis)
    pairs = [(i, i + by) for i in range(size) if 0 <= i + by < size]
    return lax.ppermute(value, axis, pairs)


def gather_filters(shard, axis):
    size = lax.axis_size(axis)
    if size != 2:
        return lax.all_gather(shard, axis, axis=2, tiled=True)
    other = lax.ppermute(shard, axis, [(0, 1), (1, 0)])
    first = lax.axis_index(axis) == 0
    return jnp.concatenate(
        [jnp.where(first, shard, other), jnp.where(first, other, shard)], axis=2
    )


def sum_over(value, axis):
    size = lax.axis_size(axis)
    if size & (size - 1):
        return lax.psum(value, axis)
    hop = 1
    while hop < size:
        value = value + lax.ppermute(value, axis, [(i, i ^ hop) for i in range(size)])
        hop *= 2
    return value


def sum_scatter(value, axis):
    size = lax.axis_size(axis)
    portion = value.shape[-1] // size
    if size != 2:
        total = sum_over(value, axis)
        return lax.dynamic_slice_in_dim(
            total, lax.axis_index(axis) * portion, portion, value.ndim - 1
        )
    first = lax.axis_index(axis) == 0
    low, high = value[..., :portion], value[..., portion:]
    sent = lax.ppermute(jnp.where(first, high, low), axis, [(0, 1), (1, 0)])
    return jnp.where(first, low, high) + sent


def kernel(
    taps,
    features_ref,
    cotangent_ref,
    weights_ref,
    before_ref,
    after_ref,
    mixed_ref,
    grads_ref,
    sums_ref,
    q_s,
    k_s,
    v_s,
    c_s,
    kc_s,
    vc_s,
    p_s,
    gq_s,
    gm_s,
    gk_s,
    gv_s,
    b_s,
    a_s,
):
    reach = taps - 1
    length = cotangent_ref.shape[0]
    columns = cotangent_ref.shape[1] // LANES

    @pl.when(pl.program_id(0) == 0)
    def _():
        sums_ref[...] = jnp.zeros_like(sums_ref)

    def causal(ref, w, start):
        total = None
        for lag in range(taps):
            term = w[lag] * ref[pl.ds(PAD + start - lag, STEP), :]
            total = term if total is None else total + term
        return total

    def anticausal(ref, w, start, source):
        total = None
        products = []
        for lag in range(taps):
            piece = ref[pl.ds(PAD + start + lag, STEP), :]
            term = w[lag] * piece
            total = term if total is None else total + term
            if source is not None:
                both = source * piece
                products.append(both[:8] + both[8:])
        return total, products

    def column(index, carry):
        lanes = pl.ds(pl.multiple_of(index * LANES, LANES), LANES)

        def weights(bank):
            return [weights_ref[bank, pl.ds(lag, 1), lanes] for lag in range(taps)]

        for bank, ref in enumerate((q_s, k_s, v_s)):
            ref[PAD : PAD + length, :] = features_ref[bank, :, lanes].astype(jnp.float32)
        c_s[PAD : PAD + length, :] = cotangent_ref[:, lanes].astype(jnp.float32)
        b_s[...] = before_ref[:, lanes].astype(jnp.float32)
        a_s[...] = after_ref[:, lanes].astype(jnp.float32)
        q_s[PAD - reach : PAD, :] = b_s[0:reach, :]
        k_s[PAD - 2 * reach : PAD, :] = b_s[reach : 3 * reach, :]
        v_s[PAD - 2 * reach : PAD, :] = b_s[3 * reach : 5 * reach, :]
        end = PAD + length
        q_s[end : end + 2 * reach, :] = a_s[0 : 2 * reach, :]
        c_s[end : end + 2 * reach, :] = a_s[2 * reach : 4 * reach, :]
        k_s[end : end + reach, :] = a_s[4 * reach : 5 * reach, :]
        v_s[end : end + reach, :] = a_s[5 * reach : 6 * reach, :]

        wk, wv = weights(1), weights(2)
        for start in range(-8, length + 8, STEP):
            rows = pl.ds(PAD + start, STEP)
            kc = causal(k_s, wk, start)
            vc = causal(v_s, wv, start)
            kc_s[rows, :] = kc
            vc_s[rows, :] = vc
            p_s[rows, :] = kc * vc
        wq, wm = weights(0), weights(3)
        for start in range(0, length + PAD, STEP):
            rows = pl.ds(PAD + start, STEP)
            upstream = c_s[rows, :]
            qc = causal(q_s, wq, start)
            gm_s[rows, :] = upstream * qc
            if start < length:
                mixer = causal(p_s, wm, start)
                mixed_ref[pl.ds(start, STEP), lanes] = (qc * mixer).astype(mixed_ref.dtype)
                gq_s[rows, :] = upstream * mixer
            else:
                rows = pl.ds(PAD + start, 8)
                mixer = None
                for lag in range(taps):
                    term = wm[lag] * p_s[pl.ds(PAD + start - lag, 8), :]
                    mixer = term if mixer is None else mixer + term
                gq_s[rows, :] = upstream[:8] * mixer
        sums = [[None] * taps for _ in range(4)]

        def collect(bank, products):
            for lag, value in enumerate(products):
                old = sums[bank][lag]
                sums[bank][lag] = value if old is None else old + value

        for start in range(0, length, STEP):
            rows = pl.ds(PAD + start, STEP)
            gp, products = anticausal(gm_s, wm, start, p_s[rows, :])
            collect(3, products)
            gk_s[rows, :] = gp * vc_s[rows, :]
            gv_s[rows, :] = gp * kc_s[rows, :]
        rows = pl.ds(PAD + length, 8)
        gp = None
        for lag in range(taps):
            term = wm[lag] * gm_s[pl.ds(PAD + length + lag, 8), :]
            gp = term if gp is None else gp + term
        gk_s[rows, :] = gp * vc_s[rows, :]
        gv_s[rows, :] = gp * kc_s[rows, :]
        for bank, (grad, source, w) in enumerate(
            ((gq_s, q_s, wq), (gk_s, k_s, wk), (gv_s, v_s, wv))
        ):
            for start in range(0, length, STEP):
                rows = pl.ds(PAD + start, STEP)
                value, products = anticausal(grad, w, start, source[rows, :])
                collect(bank, products)
                grads_ref[bank, pl.ds(start, STEP), lanes] = value.astype(grads_ref.dtype)
        for bank in range(4):
            for lag in range(taps):
                sums_ref[bank, lag, :, lanes] += sums[bank][lag]
        return carry

    lax.fori_loop(0, columns, column, 0)


def local_work(features, cotangent, weights, before, after):
    banks, length, channels = features.shape
    taps, groups = weights.shape[1:]
    repeats = channels // groups
    room = length + 2 * PAD
    scratch = [pltpu.VMEM((room, LANES), jnp.float32) for _ in range(11)]
    scratch += [
        pltpu.VMEM((before.shape[0], LANES), jnp.float32),
        pltpu.VMEM((after.shape[0], LANES), jnp.float32),
    ]
    return pl.pallas_call(
        functools.partial(kernel, taps),
        grid=(repeats,),
        out_shape=(
            jax.ShapeDtypeStruct(cotangent.shape, cotangent.dtype),
            jax.ShapeDtypeStruct(features.shape, features.dtype),
            jax.ShapeDtypeStruct((4, taps, 8, groups), jnp.float32),
        ),
        in_specs=[
            pl.BlockSpec((banks, length, groups), lambda i: (0, 0, i)),
            pl.BlockSpec((length, groups), lambda i: (0, i)),
            pl.BlockSpec(weights.shape, lambda i: (0, 0, 0)),
            pl.BlockSpec((before.shape[0], groups), lambda i: (0, i)),
            pl.BlockSpec((after.shape[0], groups), lambda i: (0, i)),
        ],
        out_specs=(
            pl.BlockSpec((length, groups), lambda i: (0, i)),
            pl.BlockSpec((banks, length, groups), lambda i: (0, 0, i)),
            pl.BlockSpec((4, taps, 8, groups), lambda i: (0, 0, 0, 0)),
        ),
        scratch_shapes=scratch,
        compiler_params=pltpu.CompilerParams(vmem_limit_bytes=32 * 1024 * 1024),
        name="local_work",
    )(features, cotangent, weights, before, after)


def per_device(features, cotangent, master_filters):
    reach = master_filters.shape[1] - 1
    length = features.shape[1]
    weights = gather_filters(master_filters.astype(jnp.bfloat16), "fsdp").astype(jnp.float32)
    tail = jnp.concatenate(
        [
            features[0, length - reach :],
            features[1, length - 2 * reach :],
            features[2, length - 2 * reach :],
        ],
        axis=0,
    )
    head = jnp.concatenate(
        [features[0, : 2 * reach], cotangent[: 2 * reach], features[1, :reach], features[2, :reach]],
        axis=0,
    )
    before = shift_rows(tail, "ctx", 1)
    after = shift_rows(head, "ctx", -1)
    mixed, feature_grads, sums = local_work(features, cotangent, weights, before, after)
    partial_sum = jnp.sum(sums, axis=2)
    repeats = features.shape[2] // weights.shape[2]
    count_all = length * lax.axis_size("ctx") * repeats * lax.axis_size("fsdp")
    factor = 1.0 / math.sqrt(count_all)
    filter_grads = sum_over(sum_scatter(partial_sum, "fsdp"), "ctx") * factor
    return (mixed, feature_grads, filter_grads)


def solution(mesh):
    return jax.shard_map(
        per_device,
        mesh=mesh,
        in_specs=(P(None, "ctx", "fsdp"), P("ctx", "fsdp"), P(None, None, "fsdp")),
        out_specs=(P("ctx", "fsdp"), P(None, "ctx", "fsdp"), P(None, None, "fsdp")),
        check_vma=False,
    )
```

```python
import functools
import math

import jax
import jax.numpy as jnp
from jax import lax
from jax.experimental import pallas as pl
from jax.experimental.pallas import tpu as pltpu
from jax.sharding import PartitionSpec as P

LANES = 128
TILE = 8
PAD = 16
PIECES = 2
F32 = jnp.float32


def shift_rows(value, axis, by):
    size = lax.axis_size(axis)
    pairs = [(i, i + by) for i in range(size) if 0 <= i + by < size]
    return lax.ppermute(value, axis, pairs)


def gather_filters(shard, axis):
    size = lax.axis_size(axis)
    if size != 2:
        return lax.all_gather(shard, axis, axis=2, tiled=True)
    other = lax.ppermute(shard, axis, [(0, 1), (1, 0)])
    first = lax.axis_index(axis) == 0
    return jnp.concatenate(
        [jnp.where(first, shard, other), jnp.where(first, other, shard)], axis=2
    )


def sum_over(value, axis):
    size = lax.axis_size(axis)
    if size & (size - 1):
        return lax.psum(value, axis)
    hop = 1
    while hop < size:
        value = value + lax.ppermute(value, axis, [(i, i ^ hop) for i in range(size)])
        hop *= 2
    return value


def sum_scatter(value, axis):
    size = lax.axis_size(axis)
    portion = value.shape[-1] // size
    if size != 2:
        total = sum_over(value, axis)
        return lax.dynamic_slice_in_dim(
            total, lax.axis_index(axis) * portion, portion, value.ndim - 1
        )
    first = lax.axis_index(axis) == 0
    low, high = value[..., :portion], value[..., portion:]
    sent = lax.ppermute(jnp.where(first, high, low), axis, [(0, 1), (1, 0)])
    return jnp.where(first, low, high) + sent


def column_loop(ref, body):
    def step(index, carry):
        body(pl.ds(pl.multiple_of(index * LANES, LANES), LANES), index)
        return carry

    lax.fori_loop(0, ref.shape[-1] // LANES, step, 0)


def weight_rows(ref, bank, lanes):
    return [ref[bank, pl.ds(lag, 1), lanes] for lag in range(ref.shape[1])]


def dot_taps(weights, pieces):
    total = weights[0] * pieces[0]
    for weight, piece in zip(weights[1:], pieces[1:]):
        total = total + weight * piece
    return total


def back(ref, start, taps, rows=TILE):
    return [ref[pl.ds(PAD + start - lag, rows), :] for lag in range(taps)]


def ahead(ref, start, taps, rows=TILE):
    return [ref[pl.ds(PAD + start + lag, rows), :] for lag in range(taps)]


class Sums:
    def __init__(self, taps):
        self.taps = taps
        self.held = [[None] * taps for _ in range(4)]

    def add(self, bank, grad, pieces):
        for lag, piece in enumerate(pieces):
            term = grad * piece
            old = self.held[bank][lag]
            self.held[bank][lag] = term if old is None else old + term

    def store(self, ref, lanes):
        for bank in range(4):
            for lag in range(self.taps):
                ref[bank, lag, :, lanes] += self.held[bank][lag]


def pack_kernel(reach, tail_ref, head_ref, upstream_ref, before_ref, after_ref, b_s, a_s):
    def column(lanes, _):
        def rows(ref, bank, start, stop):
            return ref[bank, :, lanes].astype(F32)[start:stop]

        b_s[0:reach, :] = rows(tail_ref, 0, PAD - reach, PAD)
        b_s[reach : 3 * reach, :] = rows(tail_ref, 1, PAD - 2 * reach, PAD)
        b_s[3 * reach : 5 * reach, :] = rows(tail_ref, 2, PAD - 2 * reach, PAD)
        before_ref[:, lanes] = b_s[...].astype(before_ref.dtype)
        a_s[0 : 2 * reach, :] = rows(head_ref, 0, 0, 2 * reach)
        a_s[2 * reach : 4 * reach, :] = upstream_ref[:, lanes].astype(F32)[: 2 * reach]
        a_s[4 * reach : 5 * reach, :] = rows(head_ref, 1, 0, reach)
        a_s[5 * reach : 6 * reach, :] = rows(head_ref, 2, 0, reach)
        after_ref[:, lanes] = a_s[...].astype(after_ref.dtype)

    column_loop(before_ref, column)


def pack(features, cotangent, reach):
    banks, length, channels = features.shape
    last = length // PAD - 1
    kind = features.dtype
    return pl.pallas_call(
        functools.partial(pack_kernel, reach),
        grid=(1,),
        out_shape=(
            jax.ShapeDtypeStruct((5 * reach, channels), kind),
            jax.ShapeDtypeStruct((6 * reach, channels), kind),
        ),
        in_specs=[
            pl.BlockSpec((banks, PAD, channels), lambda i: (0, last, 0)),
            pl.BlockSpec((banks, PAD, channels), lambda i: (0, 0, 0)),
            pl.BlockSpec((PAD, channels), lambda i: (0, 0)),
        ],
        out_specs=(
            pl.BlockSpec((5 * reach, channels), lambda i: (0, 0)),
            pl.BlockSpec((6 * reach, channels), lambda i: (0, 0)),
        ),
        scratch_shapes=[
            pltpu.VMEM((5 * reach, LANES), F32),
            pltpu.VMEM((6 * reach, LANES), F32),
        ],
        cost_estimate=pl.CostEstimate(flops=10**6, bytes_accessed=10**6, transcendentals=0),
        compiler_params=pltpu.CompilerParams(vmem_limit_bytes=8 * 1024 * 1024),
        name="pack_halos",
    )(features, features, cotangent)


def interior_kernel(
    taps,
    features_ref,
    cotangent_ref,
    weights_ref,
    mixed_ref,
    grads_ref,
    sums_ref,
    q_s,
    k_s,
    v_s,
    kc_s,
    vc_s,
    p_s,
    gm_s,
):
    length = cotangent_ref.shape[0]

    @pl.when(pl.program_id(0) == 0)
    def _():
        sums_ref[...] = jnp.zeros_like(sums_ref)

    def column(lanes, _):
        for bank, ref in enumerate((q_s, k_s, v_s)):
            ref[PAD : PAD + length, :] = features_ref[bank, :, lanes].astype(F32)
        wq, wk, wv, wm = (weight_rows(weights_ref, bank, lanes) for bank in range(4))
        for start in range(TILE, length, TILE):
            rows = pl.ds(PAD + start, TILE)
            kc = dot_taps(wk, back(k_s, start, taps))
            vc = dot_taps(wv, back(v_s, start, taps))
            kc_s[rows, :] = kc
            vc_s[rows, :] = vc
            p_s[rows, :] = kc * vc
        sums = Sums(taps)
        rows = pl.ds(PAD + TILE, TILE)
        upstream = cotangent_ref[0:PAD, lanes].astype(F32)[TILE:]
        gm_s[rows, :] = upstream * dot_taps(wq, back(q_s, TILE, taps))
        for start in range(PAD, length, PAD):
            upstream = cotangent_ref[pl.ds(start, PAD), lanes].astype(F32)
            parts = []
            for half in (0, TILE):
                rows = pl.ds(PAD + start + half, TILE)
                up = upstream[half : half + TILE]
                sources = back(q_s, start + half, taps)
                products = back(p_s, start + half, taps)
                qc = dot_taps(wq, sources)
                mixer = dot_taps(wm, products)
                gq = up * mixer
                gm = up * qc
                parts.append(qc * mixer)
                gm_s[rows, :] = gm
                grads_ref[0, pl.ds(start + half, TILE), lanes] = gq
                sums.add(0, gq, sources)
                sums.add(3, gm, products)
            mixed_ref[pl.ds(start, PAD), lanes] = jnp.concatenate(parts, axis=0).astype(
                mixed_ref.dtype
            )
        for start in range(TILE, length - TILE, TILE):
            rows = pl.ds(PAD + start, TILE)
            gp = dot_taps(wm, ahead(gm_s, start, taps))
            gk = gp * vc_s[rows, :]
            gv = gp * kc_s[rows, :]
            grads_ref[1, pl.ds(start, TILE), lanes] = gk
            grads_ref[2, pl.ds(start, TILE), lanes] = gv
            sums.add(1, gk, back(k_s, start, taps))
            sums.add(2, gv, back(v_s, start, taps))
        sums.store(sums_ref, lanes)

    column_loop(cotangent_ref, column)


def interior(features, cotangent, weights):
    banks, length, channels = features.shape
    taps, groups = weights.shape[1:]
    repeats = channels // groups
    room = length + 2 * PAD
    work = length * channels * taps * 2
    return pl.pallas_call(
        functools.partial(interior_kernel, taps),
        grid=(repeats,),
        out_shape=(
            jax.ShapeDtypeStruct(cotangent.shape, cotangent.dtype),
            jax.ShapeDtypeStruct(features.shape, F32),
            jax.ShapeDtypeStruct((4, taps, TILE, groups), F32),
        ),
        in_specs=[
            pl.BlockSpec((banks, length, groups), lambda i: (0, 0, i)),
            pl.BlockSpec((length, groups), lambda i: (0, i)),
            pl.BlockSpec(weights.shape, lambda i: (0, 0, 0)),
        ],
        out_specs=(
            pl.BlockSpec((length, groups), lambda i: (0, i)),
            pl.BlockSpec((banks, length, groups), lambda i: (0, 0, i)),
            pl.BlockSpec((4, taps, TILE, groups), lambda i: (0, 0, 0, 0)),
        ),
        scratch_shapes=[pltpu.VMEM((room, LANES), F32) for _ in range(7)],
        cost_estimate=pl.CostEstimate(
            flops=9 * work, bytes_accessed=26 * length * channels, transcendentals=0
        ),
        compiler_params=pltpu.CompilerParams(vmem_limit_bytes=24 * 1024 * 1024),
        name="interior",
    )(features, cotangent, weights)


def edge_kernel(
    taps,
    length,
    groups,
    tail_ref,
    head_ref,
    up_tail_ref,
    up_head_ref,
    weights_ref,
    before_ref,
    after_ref,
    sums_in_ref,
    _mixed_in_ref,
    mixed_ref,
    ghead_ref,
    gtail_ref,
    sums_ref,
    acc,
    b_s,
    a_s,
    qh,
    kh,
    vh,
    ph,
    gmh,
    qt,
    kt,
    vt,
    gmt,
):
    reach = taps - 1
    columns = groups // LANES

    @pl.when(pl.program_id(0) == 0)
    def _():
        acc[...] = sums_in_ref[...]

    def column(lanes, index):
        part = pl.ds(pl.multiple_of(lax.rem(index, columns) * LANES, LANES), LANES)
        wq, wk, wv, wm = (weight_rows(weights_ref, bank, part) for bank in range(4))
        b_s[...] = before_ref[:, lanes].astype(F32)
        a_s[...] = after_ref[:, lanes].astype(F32)
        for bank, (ref, first) in enumerate(((qh, 0), (kh, reach), (vh, 3 * reach))):
            count = reach if bank == 0 else 2 * reach
            ref[PAD - count : PAD, :] = b_s[first : first + count, :]
            ref[PAD : 2 * PAD, :] = head_ref[bank, :, lanes].astype(F32)
        for bank, ref in enumerate((qt, kt, vt)):
            ref[0:PAD, :] = tail_ref[bank, :, lanes].astype(F32)
        qt[PAD : PAD + 2 * reach, :] = a_s[0 : 2 * reach, :]
        sums = Sums(taps)
        conv_k, conv_v = {}, {}
        for start in range(-TILE, PAD, TILE):
            conv_k[start] = dot_taps(wk, back(kh, start, taps))
            conv_v[start] = dot_taps(wv, back(vh, start, taps))
            ph[pl.ds(PAD + start, TILE), :] = conv_k[start] * conv_v[start]
        upstream = up_head_ref[:, lanes].astype(F32)
        parts = []
        for start in range(0, PAD, TILE):
            up = upstream[start : start + TILE]
            sources = back(qh, start, taps)
            products = back(ph, start, taps)
            qc = dot_taps(wq, sources)
            mixer = dot_taps(wm, products)
            gq = up * mixer
            gm = up * qc
            parts.append(qc * mixer)
            gmh[pl.ds(PAD + start, TILE), :] = gm
            ghead_ref[0, pl.ds(start, TILE), lanes] = gq
            sums.add(0, gq, sources)
            sums.add(3, gm, products)
        mixed_ref[:, lanes] = jnp.concatenate(parts, axis=0).astype(mixed_ref.dtype)
        gp = dot_taps(wm, ahead(gmh, 0, taps))
        gk = gp * conv_v[0]
        gv = gp * conv_k[0]
        ghead_ref[1, 0:TILE, lanes] = gk
        ghead_ref[2, 0:TILE, lanes] = gv
        sums.add(1, gk, back(kh, 0, taps))
        sums.add(2, gv, back(vh, 0, taps))
        qc = dot_taps(wq, back(qt, -TILE, taps))
        gmt[PAD - TILE : PAD, :] = up_tail_ref[:, lanes].astype(F32)[TILE:] * qc
        qc = dot_taps(wq, back(qt, 0, taps))
        gmt[PAD : PAD + TILE, :] = a_s[2 * reach : 2 * reach + TILE, :] * qc
        gp = dot_taps(wm, ahead(gmt, -TILE, taps))
        sources_k = back(kt, -TILE, taps)
        sources_v = back(vt, -TILE, taps)
        gk = gp * dot_taps(wv, sources_v)
        gv = gp * dot_taps(wk, sources_k)
        gtail_ref[0, :, lanes] = gk
        gtail_ref[1, :, lanes] = gv
        sums.add(1, gk, sources_k)
        sums.add(2, gv, sources_v)
        sums.store(acc, part)

    column_loop(mixed_ref, column)

    @pl.when(pl.program_id(0) == pl.num_programs(0) - 1)
    def _():
        sums_ref[...] = jnp.sum(acc[...], axis=2)


def edge(features, cotangent, weights, before, after, sums, mixed):
    banks, length, channels = features.shape
    taps, groups = weights.shape[1:]
    last = length // PAD - 1
    steps = 2 if channels % (2 * groups) == 0 else 1
    wide = channels // steps
    room = 2 * PAD + TILE
    work = TILE * channels * taps * 2
    return pl.pallas_call(
        functools.partial(edge_kernel, taps, length, groups),
        grid=(steps,),
        out_shape=(
            jax.ShapeDtypeStruct(mixed.shape, mixed.dtype),
            jax.ShapeDtypeStruct((banks, PAD, channels), F32),
            jax.ShapeDtypeStruct((banks - 1, TILE, channels), F32),
            jax.ShapeDtypeStruct((4, taps, groups), F32),
        ),
        in_specs=[
            pl.BlockSpec((banks, PAD, wide), lambda i: (0, last, i)),
            pl.BlockSpec((banks, PAD, wide), lambda i: (0, 0, i)),
            pl.BlockSpec((PAD, wide), lambda i: (last, i)),
            pl.BlockSpec((PAD, wide), lambda i: (0, i)),
            pl.BlockSpec(weights.shape, lambda i: (0, 0, 0)),
            pl.BlockSpec((before.shape[0], wide), lambda i: (0, i)),
            pl.BlockSpec((after.shape[0], wide), lambda i: (0, i)),
            pl.BlockSpec(sums.shape, lambda i: (0, 0, 0, 0)),
            pl.BlockSpec(memory_space=pl.ANY),
        ],
        out_specs=(
            pl.BlockSpec((PAD, wide), lambda i: (0, i)),
            pl.BlockSpec((banks, PAD, wide), lambda i: (0, 0, i)),
            pl.BlockSpec((banks - 1, TILE, wide), lambda i: (0, 0, i)),
            pl.BlockSpec((4, taps, groups), lambda i: (0, 0, 0)),
        ),
        scratch_shapes=[
            pltpu.VMEM(sums.shape, F32),
            pltpu.VMEM((before.shape[0], LANES), F32),
            pltpu.VMEM((after.shape[0], LANES), F32),
        ]
        + [pltpu.VMEM((room, LANES), F32) for _ in range(9)],
        input_output_aliases={8: 0},
        cost_estimate=pl.CostEstimate(
            flops=24 * work, bytes_accessed=2 * 10**6, transcendentals=0
        ),
        compiler_params=pltpu.CompilerParams(vmem_limit_bytes=16 * 1024 * 1024),
        name="edge",
    )(features, features, cotangent, cotangent, weights, before, after, sums, mixed)


def grads_kernel(
    taps,
    grads_ref,
    ghead_ref,
    gtail_ref,
    tail_ref,
    after_ref,
    weights_ref,
    *refs,
):
    out_ref, a_s, gq, gk, gv, q_s, k_s, v_s, p_s, gm_s = refs[-10:]
    reach = taps - 1
    length = grads_ref.shape[1]

    def column(lanes, _):
        wq, wk, wv, wm = (weight_rows(weights_ref, bank, lanes) for bank in range(4))
        a_s[...] = after_ref[:, lanes].astype(F32)
        for bank, ref in enumerate((q_s, k_s, v_s)):
            ref[0:PAD, :] = tail_ref[bank, :, lanes].astype(F32)
        q_s[PAD : PAD + 2 * reach, :] = a_s[0 : 2 * reach, :]
        k_s[PAD : PAD + reach, :] = a_s[4 * reach : 5 * reach, :]
        v_s[PAD : PAD + reach, :] = a_s[5 * reach : 6 * reach, :]
        for start in (-TILE, 0):
            kc = dot_taps(wk, back(k_s, start, taps))
            vc = dot_taps(wv, back(v_s, start, taps))
            p_s[pl.ds(PAD + start, TILE), :] = kc * vc
        first, second = (
            a_s[2 * reach : 2 * reach + TILE, :],
            a_s[2 * reach + TILE : 2 * reach + 2 * TILE, :],
        )
        gm_s[PAD : PAD + TILE, :] = first * dot_taps(wq, back(q_s, 0, taps))
        gm_s[PAD + TILE : 2 * PAD, :] = second * dot_taps(wq, back(q_s, TILE, taps))
        end = pl.ds(PAD + length, TILE)
        gq[end, :] = first * dot_taps(wm, back(p_s, 0, taps))
        gp = dot_taps(wm, ahead(gm_s, 0, taps))
        gk[end, :] = gp * vc
        gv[end, :] = gp * kc
        gq[PAD : 2 * PAD, :] = ghead_ref[0, :, lanes]
        gq[2 * PAD : PAD + length, :] = grads_ref[0, PAD:length, lanes]
        for bank, ref in ((1, gk), (2, gv)):
            ref[PAD : PAD + TILE, :] = ghead_ref[bank, 0:TILE, lanes]
            ref[PAD + TILE : PAD + length - TILE, :] = grads_ref[
                bank, TILE : length - TILE, lanes
            ]
            ref[PAD + length - TILE : PAD + length, :] = gtail_ref[bank - 1, :, lanes]
        for bank, (ref, weights) in enumerate(((gq, wq), (gk, wk), (gv, wv))):
            for start in range(0, length, PAD):
                out_ref[bank, pl.ds(start, PAD), lanes] = dot_taps(
                    weights, ahead(ref, start, taps, PAD)
                ).astype(out_ref.dtype)

    column_loop(grads_ref, column)


def feature_gradients(piece, pieces, features, grads, ghead, gtail, after, weights, earlier):
    banks, length, channels = features.shape
    taps, groups = weights.shape[1:]
    last = length // PAD - 1
    steps = channels // groups // pieces
    first = piece * steps
    room = length + 2 * PAD
    operands = [grads, ghead, gtail, features, after, weights]
    in_specs = [
        pl.BlockSpec((banks, length, groups), lambda i: (0, 0, first + i)),
        pl.BlockSpec((banks, PAD, groups), lambda i: (0, 0, first + i)),
        pl.BlockSpec((banks - 1, TILE, groups), lambda i: (0, 0, first + i)),
        pl.BlockSpec((banks, PAD, groups), lambda i: (0, last, first + i)),
        pl.BlockSpec((after.shape[0], groups), lambda i: (0, first + i)),
        pl.BlockSpec(weights.shape, lambda i: (0, 0, 0)),
    ]
    aliases = {}
    if earlier is not None:
        aliases = {len(operands): 0}
        operands.append(earlier)
        in_specs.append(pl.BlockSpec(memory_space=pl.ANY))
    work = length * channels * taps * 2 // pieces
    return pl.pallas_call(
        functools.partial(grads_kernel, taps),
        grid=(steps,),
        out_shape=jax.ShapeDtypeStruct(features.shape, features.dtype),
        in_specs=in_specs,
        out_specs=pl.BlockSpec((banks, length, groups), lambda i: (0, 0, first + i)),
        scratch_shapes=[pltpu.VMEM((after.shape[0], LANES), F32)]
        + [pltpu.VMEM((room, LANES), F32) for _ in range(3)]
        + [pltpu.VMEM((3 * PAD, LANES), F32) for _ in range(5)],
        input_output_aliases=aliases,
        cost_estimate=pl.CostEstimate(
            flops=4 * work,
            bytes_accessed=18 * length * channels // pieces,
            transcendentals=0,
        ),
        compiler_params=pltpu.CompilerParams(vmem_limit_bytes=16 * 1024 * 1024),
        name="feature_gradients",
    )(*operands)


def per_device(features, cotangent, master_filters):
    reach = master_filters.shape[1] - 1
    length = features.shape[1]
    tail, head = pack(features, cotangent, reach)
    before = shift_rows(tail, "ctx", 1)
    after = shift_rows(head, "ctx", -1)
    weights = gather_filters(master_filters.astype(jnp.bfloat16), "fsdp").astype(F32)
    mixed, grads, sums = interior(features, cotangent, weights)
    mixed, ghead, gtail, sums = edge(
        features, cotangent, weights, before, after, sums, mixed
    )
    repeats = features.shape[2] // weights.shape[2]
    pieces = PIECES if repeats % PIECES == 0 else 1
    feature_grads = None
    for piece in range(pieces):
        feature_grads = feature_gradients(
            piece, pieces, features, grads, ghead, gtail, after, weights, feature_grads
        )
    count_all = length * lax.axis_size("ctx") * repeats * lax.axis_size("fsdp")
    factor = 1.0 / math.sqrt(count_all)
    filter_grads = sum_over(sum_scatter(sums, "fsdp"), "ctx") * factor
    return (mixed, feature_grads, filter_grads)


def solution(mesh):
    return jax.shard_map(
        per_device,
        mesh=mesh,
        in_specs=(P(None, "ctx", "fsdp"), P("ctx", "fsdp"), P(None, None, "fsdp")),
        out_specs=(P("ctx", "fsdp"), P(None, "ctx", "fsdp"), P(None, None, "fsdp")),
        check_vma=False,
    )
```

```python
import functools
import math

import jax
import jax.numpy as jnp
from jax import lax
from jax.experimental import pallas as pl
from jax.experimental.pallas import tpu as pltpu
from jax.sharding import PartitionSpec as P

LANES = 128
CHUNK = 16
PAD = 16
PIECES = 4
VMEM_LIMIT = 12 * 1024 * 1024
F32 = jnp.float32
VMEM_SPEC = pl.BlockSpec(memory_space=pltpu.VMEM)
ANY_SPEC = pl.BlockSpec(memory_space=pl.ANY)


def shift_rows(value, axis, by):
    size = lax.axis_size(axis)
    pairs = [(i, i + by) for i in range(size) if 0 <= i + by < size]
    return lax.ppermute(value, axis, pairs)


def gather_filters(shard, axis):
    size = lax.axis_size(axis)
    if size != 2:
        return lax.all_gather(shard, axis, axis=2, tiled=True)
    other = lax.ppermute(shard, axis, [(0, 1), (1, 0)])
    first = lax.axis_index(axis) == 0
    return jnp.concatenate(
        [jnp.where(first, shard, other), jnp.where(first, other, shard)], axis=2
    )


def sum_over(value, axis, beside=None):
    size = lax.axis_size(axis)
    if size & (size - 1):
        return lax.psum(value, axis), 0
    rounds = size.bit_length() - 1
    for step in range(rounds):
        pairs = [(i, i ^ (1 << step)) for i in range(size)]
        received = lax.ppermute(value, axis, pairs)
        value = value + received
        if beside is not None:
            value = value + beside(step)
    return value, rounds


def sum_scatter(value, axis):
    size = lax.axis_size(axis)
    portion = value.shape[-1] // size
    if size != 2:
        total, _ = sum_over(value, axis)
        return lax.dynamic_slice_in_dim(
            total, lax.axis_index(axis) * portion, portion, value.ndim - 1
        )
    first = lax.axis_index(axis) == 0
    low, high = value[..., :portion], value[..., portion:]
    sent = lax.ppermute(jnp.where(first, high, low), axis, [(0, 1), (1, 0)])
    return jnp.where(first, low, high) + sent


def dot_taps(weights, pieces):
    total = weights[0] * pieces[0]
    for weight, piece in zip(weights[1:], pieces[1:]):
        total = total + weight * piece
    return total


def weight_rows(ref, bank, lanes):
    return [ref[lag, pl.ds(bank, 1), lanes] for lag in range(ref.shape[0])]


def lane_slice(index):
    return pl.ds(pl.multiple_of(index * LANES, LANES), LANES)


def part_slice(repeat, groups, column):
    return pl.ds(pl.multiple_of(repeat * groups + column * LANES, LANES), LANES)


class Tokens:
    def __init__(self, ref, repeats, origin=0, lead=()):
        self.ref, self.repeats, self.origin, self.lead = ref, repeats, origin, lead

    def rows(self, token, count=1):
        start = (self.origin + token) * self.repeats
        if not isinstance(start, int):
            start = pl.multiple_of(start, self.repeats)
        return pl.ds(start, count * self.repeats)

    def __getitem__(self, token):
        return self.ref[(*self.lead, self.rows(token), slice(None))]

    def __setitem__(self, token, value):
        self.ref[(*self.lead, self.rows(token), slice(None))] = value

    def strided(self, token, repeat, count):
        start = (self.origin + token) * self.repeats + repeat
        return pl.ds(start, count, stride=self.repeats)

    def put(self, token, repeat, value):
        rows = self.strided(token, repeat, value.shape[0])
        self.ref[(*self.lead, rows, slice(None))] = value

    def take(self, token, repeat, count):
        return self.ref[(*self.lead, self.strided(token, repeat, count), slice(None))]


class Window:
    def __init__(self, load):
        self.load, self.held = load, {}

    def __call__(self, token):
        if token not in self.held:
            self.held[token] = self.load(token)
        return self.held[token]

    def back(self, token, taps):
        return [self(token - lag) for lag in range(taps)]

    def ahead(self, token, taps):
        return [self(token + lag) for lag in range(taps)]


class Sums:
    def __init__(self, taps):
        self.taps = taps
        self.held = {}

    def add(self, bank, grad, pieces):
        for lag, piece in enumerate(pieces):
            term = grad * piece
            old = self.held.get((bank, lag))
            self.held[bank, lag] = term if old is None else old + term

    def store(self, ref, lanes):
        for (bank, lag), value in self.held.items():
            ref[bank, lag, :, lanes] += value


def pack_kernel(
    reach,
    features_hbm,
    cotangent_hbm,
    master_ref,
    before_ref,
    after_ref,
    rounded_ref,
    tail,
    head,
    upstream,
    b_s,
    a_s,
    sems,
):
    length = cotangent_hbm.shape[0]
    copies = [
        pltpu.make_async_copy(features_hbm.at[:, length - PAD :, :], tail, sems.at[0]),
        pltpu.make_async_copy(features_hbm.at[:, :PAD, :], head, sems.at[1]),
        pltpu.make_async_copy(cotangent_hbm.at[:PAD, :], upstream, sems.at[2]),
    ]
    for copy in copies:
        copy.start()
    rounded_ref[...] = master_ref[...].astype(rounded_ref.dtype)
    for copy in copies:
        copy.wait()

    def column(index, carry):
        lanes = lane_slice(index)

        def rows(ref, bank, start, stop):
            return ref[bank, :, lanes].astype(F32)[start:stop]

        b_s[0:reach, :] = rows(tail, 0, PAD - reach, PAD)
        b_s[reach : 3 * reach, :] = rows(tail, 1, PAD - 2 * reach, PAD)
        b_s[3 * reach : 5 * reach, :] = rows(tail, 2, PAD - 2 * reach, PAD)
        before_ref[:, lanes] = b_s[...].astype(before_ref.dtype)
        a_s[0 : 2 * reach, :] = rows(head, 0, 0, 2 * reach)
        a_s[2 * reach : 4 * reach, :] = upstream[:, lanes].astype(F32)[: 2 * reach]
        a_s[4 * reach : 5 * reach, :] = rows(head, 1, 0, reach)
        a_s[5 * reach : 6 * reach, :] = rows(head, 2, 0, reach)
        after_ref[:, lanes] = a_s[...].astype(after_ref.dtype)
        return carry

    lax.fori_loop(0, before_ref.shape[1] // LANES, column, 0)


def pack(features, cotangent, master):
    reach = master.shape[0] - 1
    banks, length, channels = features.shape
    kind = features.dtype
    return pl.pallas_call(
        functools.partial(pack_kernel, reach),
        out_shape=(
            jax.ShapeDtypeStruct((5 * reach, channels), kind),
            jax.ShapeDtypeStruct((6 * reach, channels), kind),
            jax.ShapeDtypeStruct(master.shape, jnp.bfloat16),
        ),
        in_specs=[
            pl.BlockSpec(memory_space=pltpu.HBM),
            pl.BlockSpec(memory_space=pltpu.HBM),
            VMEM_SPEC,
        ],
        out_specs=(VMEM_SPEC,) * 3,
        scratch_shapes=[
            pltpu.VMEM((banks, PAD, channels), kind),
            pltpu.VMEM((banks, PAD, channels), kind),
            pltpu.VMEM((PAD, channels), kind),
            pltpu.VMEM((5 * reach, LANES), F32),
            pltpu.VMEM((6 * reach, LANES), F32),
            pltpu.SemaphoreType.DMA((3,)),
        ],
        cost_estimate=pl.CostEstimate(flops=10**6, bytes_accessed=10**6, transcendentals=0),
        compiler_params=pltpu.CompilerParams(vmem_limit_bytes=8 * 1024 * 1024),
        name="pack_halos",
    )(
        pltpu.with_memory_space_constraint(features, pltpu.HBM),
        pltpu.with_memory_space_constraint(cotangent, pltpu.HBM),
        master,
    )


def interior_kernel(
    taps,
    repeats,
    features_ref,
    cotangent_ref,
    weights_ref,
    mixed_ref,
    gq_ref,
    gk_ref,
    gv_ref,
    q_s,
    k_s,
    v_s,
    c_s,
    kc_s,
    vc_s,
    p_s,
    gm_s,
    sums_ref,
    m_s,
):
    reach = taps - 1
    groups = weights_ref.shape[2]
    length = cotangent_ref.shape[0]
    count = length // CHUNK
    sums_ref[...] = jnp.zeros_like(sums_ref)
    m_t = Tokens(m_s, repeats)

    def column_step(column, carry):
        lanes = lane_slice(column)
        gq_t, gk_t, gv_t = (
            Tokens(ref, repeats, 0, (column,)) for ref in (gq_ref, gk_ref, gv_ref)
        )
        q_t, k_t, v_t, c_t, kc_t, vc_t, p_t, gm_t = (
            Tokens(ref, repeats, PAD, (column,))
            for ref in (q_s, k_s, v_s, c_s, kc_s, vc_s, p_s, gm_s)
        )
        zero = jnp.zeros((reach * repeats, LANES), F32)
        for ref in (q_s, k_s, v_s, p_s):
            ref[column, (PAD - reach) * repeats : PAD * repeats, :] = zero
        gm_s[column, gm_t.rows(length, reach), :] = zero
        wq, wk, wv, wm = (weight_rows(weights_ref, bank, lanes) for bank in range(4))

        def forward(step, carry):
            base = pl.multiple_of(step * CHUNK, CHUNK)
            rows = pl.ds(base, CHUNK)
            for repeat in range(repeats):
                part = part_slice(repeat, groups, column)
                for bank, view in enumerate((q_t, k_t, v_t)):
                    view.put(base, repeat, features_ref[bank, rows, part].astype(F32))
                c_t.put(base, repeat, cotangent_ref[rows, part].astype(F32))
            k_w, v_w = (Window(lambda t, view=view: view[base + t]) for view in (k_t, v_t))
            for token in range(CHUNK):
                kc = dot_taps(wk, k_w.back(token, taps))
                vc = dot_taps(wv, v_w.back(token, taps))
                kc_t[base + token] = kc
                vc_t[base + token] = vc
                p_t[base + token] = kc * vc
            sums = Sums(taps)
            q_w, p_w = (Window(lambda t, view=view: view[base + t]) for view in (q_t, p_t))
            for token in range(CHUNK):
                up = c_t[base + token]
                sources = q_w.back(token, taps)
                products = p_w.back(token, taps)
                qc = dot_taps(wq, sources)
                mixer = dot_taps(wm, products)
                gq = up * mixer
                gm = up * qc
                m_t[token] = qc * mixer
                gm_t[base + token] = gm
                gq_t[base + token] = gq
                if token < 2 * reach:
                    gq = jnp.where(step > 0, gq, 0.0)
                    gm = jnp.where(step > 0, gm, 0.0)
                sums.add(0, gq, sources)
                sums.add(3, gm, products)
            sums.store(sums_ref, lanes)
            for repeat in range(repeats):
                part = part_slice(repeat, groups, column)
                mixed_ref[rows, part] = m_t.take(0, repeat, CHUNK).astype(mixed_ref.dtype)
            return carry

        def backward(step, carry):
            base = pl.multiple_of(step * CHUNK, CHUNK)
            k_w, v_w, gm_w = (
                Window(lambda t, view=view: view[base + t]) for view in (k_t, v_t, gm_t)
            )
            sums = Sums(taps)
            for token in range(CHUNK):
                gp = dot_taps(wm, gm_w.ahead(token, taps))
                if token < reach:
                    gp = jnp.where(step > 0, gp, 0.0)
                if token >= CHUNK - reach:
                    gp = jnp.where(step < count - 1, gp, 0.0)
                gk = gp * vc_t[base + token]
                gv = gp * kc_t[base + token]
                gk_t[base + token] = gk
                gv_t[base + token] = gv
                sums.add(1, gk, k_w.back(token, taps))
                sums.add(2, gv, v_w.back(token, taps))
            sums.store(sums_ref, lanes)
            return carry

        lax.fori_loop(0, count, forward, 0)
        lax.fori_loop(0, count, backward, 0)
        return carry

    lax.fori_loop(0, groups // LANES, column_step, 0)


def interior(features, cotangent, weights):
    length, channels = cotangent.shape
    taps, banks, groups = weights.shape
    repeats = channels // groups
    columns = groups // LANES
    work = length * channels * taps * 2
    grad = jax.ShapeDtypeStruct((columns, length * repeats, LANES), F32)
    held = jax.ShapeDtypeStruct((columns, (length + 2 * PAD) * repeats, LANES), F32)
    mixed, gq, gk, gv, *arrays, sums = pl.pallas_call(
        functools.partial(interior_kernel, taps, repeats),
        out_shape=(
            jax.ShapeDtypeStruct(cotangent.shape, cotangent.dtype),
            *[grad] * 3,
            *[held] * 8,
            jax.ShapeDtypeStruct((banks, taps, repeats, groups), F32),
        ),
        in_specs=[VMEM_SPEC] * 3,
        out_specs=(VMEM_SPEC,) * 13,
        scratch_shapes=[pltpu.VMEM((CHUNK * repeats, LANES), F32)],
        cost_estimate=pl.CostEstimate(
            flops=9 * work, bytes_accessed=22 * length * channels, transcendentals=0
        ),
        compiler_params=pltpu.CompilerParams(vmem_limit_bytes=VMEM_LIMIT),
        name="interior",
    )(features, cotangent, weights)
    return mixed, (gq, gk, gv), arrays, sums


def stage_halo(halo_ref, n_s, view, repeats, groups, column, rows):
    for repeat in range(repeats):
        n_s[0:rows, :] = halo_ref[0:rows, part_slice(repeat, groups, column)].astype(F32)
        view.put(0, repeat, n_s[...])


def edge_kernel(
    taps,
    repeats,
    weights_ref,
    before_ref,
    after_ref,
    sums_in_ref,
    q_a,
    k_a,
    v_a,
    c_a,
    kc_a,
    vc_a,
    p_a,
    gm_a,
    mixed_ref,
    ghead_ref,
    gtail_ref,
    sums_ref,
    acc,
    n_s,
    h_s,
    kc_s,
    vc_s,
    p_s,
    gm_s,
    m_s,
):
    reach = taps - 1
    groups = weights_ref.shape[2]
    length = q_a.shape[1] // repeats - 2 * PAD
    acc[...] = sums_in_ref[...]
    h_t, m_t = Tokens(h_s, repeats), Tokens(m_s, repeats)
    kc_t, vc_t, p_t, gm_t = (Tokens(ref, repeats, PAD) for ref in (kc_s, vc_s, p_s, gm_s))

    def column_step(column, carry):
        lanes = lane_slice(column)
        wq, wk, wv, wm = (weight_rows(weights_ref, bank, lanes) for bank in range(4))
        q_t, k_t, v_t, c_t, kc_i, vc_i, p_i, gm_i = (
            Tokens(ref, repeats, PAD, (column,))
            for ref in (q_a, k_a, v_a, c_a, kc_a, vc_a, p_a, gm_a)
        )
        sums = Sums(taps)

        stage_halo(before_ref, n_s, h_t, repeats, groups, column, 5 * reach)
        q_w = Window(lambda t: q_t[t] if t >= 0 else h_t[reach + t])
        k_w = Window(lambda t: k_t[t] if t >= 0 else h_t[3 * reach + t])
        v_w = Window(lambda t: v_t[t] if t >= 0 else h_t[5 * reach + t])
        gq_o, gk_o, gv_o = (Tokens(ghead_ref, repeats, 0, (bank, column)) for bank in range(3))
        for token in range(-reach, reach):
            kc = dot_taps(wk, k_w.back(token, taps))
            vc = dot_taps(wv, v_w.back(token, taps))
            p_t[token] = kc * vc
            if token >= 0:
                kc_t[token] = kc
                vc_t[token] = vc
        p_w = Window(lambda t: p_t[t] if t < reach else p_i[t])
        for token in range(CHUNK):
            up = c_t[token]
            sources = q_w.back(token, taps)
            products = p_w.back(token, taps)
            qc = dot_taps(wq, sources)
            mixer = dot_taps(wm, products)
            m_t[token] = qc * mixer
            if token < 2 * reach:
                gq = up * mixer
                gm = up * qc
                gm_t[token] = gm
                gq_o[token] = gq
                sums.add(0, gq, sources)
                sums.add(3, gm, products)
        gm_w = Window(lambda t: gm_t[t])
        for token in range(reach):
            gp = dot_taps(wm, gm_w.ahead(token, taps))
            gk = gp * vc_t[token]
            gv = gp * kc_t[token]
            gk_o[token] = gk
            gv_o[token] = gv
            sums.add(1, gk, k_w.back(token, taps))
            sums.add(2, gv, v_w.back(token, taps))
        for repeat in range(repeats):
            part = part_slice(repeat, groups, column)
            mixed_ref[:, part] = m_t.take(0, repeat, CHUNK).astype(mixed_ref.dtype)

        stage_halo(after_ref, n_s, h_t, repeats, groups, column, 4 * reach)
        q_w = Window(lambda t: q_t[length + t] if t < 0 else h_t[t])
        gk_o, gv_o = (Tokens(gtail_ref, repeats, reach, (bank, column)) for bank in range(2))
        for token in range(reach):
            gm_t[token] = h_t[2 * reach + token] * dot_taps(wq, q_w.back(token, taps))
        gm_w = Window(lambda t: gm_i[length + t] if t < 0 else gm_t[t])
        k_w, v_w = (Window(lambda t, view=view: view[length + t]) for view in (k_t, v_t))
        for token in range(-reach, 0):
            gp = dot_taps(wm, gm_w.ahead(token, taps))
            gk = gp * vc_i[length + token]
            gv = gp * kc_i[length + token]
            gk_o[token] = gk
            gv_o[token] = gv
            sums.add(1, gk, k_w.back(token, taps))
            sums.add(2, gv, v_w.back(token, taps))
        sums.store(acc, lanes)
        return carry

    lax.fori_loop(0, groups // LANES, column_step, 0)
    for bank in range(sums_ref.shape[1]):
        sums_ref[:, bank, :] = jnp.sum(acc[bank], axis=1)


def edge(weights, before, after, sums, arrays):
    taps, banks, groups = weights.shape
    channels = before.shape[1]
    repeats = channels // groups
    columns = groups // LANES
    reach = taps - 1
    halo_rows = -(-5 * reach // 8) * 8
    return pl.pallas_call(
        functools.partial(edge_kernel, taps, repeats),
        out_shape=(
            jax.ShapeDtypeStruct((CHUNK, channels), before.dtype),
            jax.ShapeDtypeStruct((3, columns, 2 * reach * repeats, LANES), F32),
            jax.ShapeDtypeStruct((2, columns, reach * repeats, LANES), F32),
            jax.ShapeDtypeStruct((taps, banks, groups), F32),
        ),
        in_specs=[VMEM_SPEC] * 12,
        out_specs=(VMEM_SPEC,) * 4,
        scratch_shapes=[
            pltpu.VMEM(sums.shape, F32),
            pltpu.VMEM((halo_rows, LANES), F32),
            pltpu.VMEM((halo_rows * repeats, LANES), F32),
        ]
        + [pltpu.VMEM((2 * PAD * repeats, LANES), F32) for _ in range(4)]
        + [pltpu.VMEM((CHUNK * repeats, LANES), F32)],
        cost_estimate=pl.CostEstimate(
            flops=10**7, bytes_accessed=4 * 10**6, transcendentals=0
        ),
        compiler_params=pltpu.CompilerParams(vmem_limit_bytes=VMEM_LIMIT),
        name="edge",
    )(weights, before, after, sums, *arrays)


def grads_kernel(taps, repeats, first, steps, count, *refs):
    refs = list(refs)
    top, bottom = first == 0, first + steps == count

    def pop(number):
        taken, refs[:number] = refs[:number], []
        return taken

    weights_ref, gq, gk, gv, ghead, gtail = pop(6)
    if top:
        middle, head = pop(2)
    else:
        pop(1)
    if bottom:
        after_ref, *ahead_of = pop(5)
    out_hbm, zero_ref = pop(2)
    copies = []
    out_s, o_s, sems = refs[-3:]
    reach = taps - 1
    groups = weights_ref.shape[2]
    columns = groups // LANES
    length = gq.shape[1] // repeats
    zero_ref[...] = jnp.zeros_like(zero_ref)
    if top:
        (mixed_hbm,) = pop(1)
        copies = [
            pltpu.make_async_copy(head, mixed_hbm.at[:CHUNK, :], sems.at[steps]),
            pltpu.make_async_copy(
                middle.at[CHUNK:, :], mixed_hbm.at[CHUNK:, :], sems.at[steps + 1]
            ),
        ]
        for copy in copies:
            copy.start()

    def load(bank, column, token):
        if token >= length:
            return Tokens(refs[0], repeats, 0, (bank, column))[token - length]
        if token < (reach if bank else 2 * reach):
            return Tokens(ghead, repeats, 0, (bank, column))[token]
        if bank and token >= length - reach:
            return Tokens(gtail, repeats, reach - length, (bank - 1, column))[token]
        return Tokens((gq, gk, gv)[bank], repeats, 0, (column,))[token]

    def next_shard(column, carry):
        gnext, n_s, h_s, p_s, gm_s = refs[:5]
        lanes = lane_slice(column)
        wq, wk, wv, wm = (weight_rows(weights_ref, bank, lanes) for bank in range(4))
        h_t, p_t, gm_t = (Tokens(ref, repeats) for ref in (h_s, p_s, gm_s))
        q_t, k_t, v_t, p_i = (
            Tokens(ref, repeats, PAD + length, (column,)) for ref in ahead_of
        )
        stage_halo(after_ref, n_s, h_t, repeats, groups, column, 6 * reach)
        q_w = Window(lambda t: q_t[t] if t < 0 else h_t[t])
        k_w = Window(lambda t: k_t[t] if t < 0 else h_t[4 * reach + t])
        v_w = Window(lambda t: v_t[t] if t < 0 else h_t[5 * reach + t])
        p_w = Window(lambda t: p_i[t] if t < 0 else p_t[t])
        gm_w = Window(lambda t: gm_t[t])
        next_q, next_k, next_v = (
            Tokens(gnext, repeats, 0, (bank, column)) for bank in range(3)
        )
        for token in range(2 * reach):
            gm_t[token] = h_t[2 * reach + token] * dot_taps(wq, q_w.back(token, taps))
        for token in range(reach):
            kc = dot_taps(wk, k_w.back(token, taps))
            vc = dot_taps(wv, v_w.back(token, taps))
            p_t[token] = kc * vc
            gp = dot_taps(wm, gm_w.ahead(token, taps))
            next_k[token] = gp * vc
            next_v[token] = gp * kc
            next_q[token] = h_t[2 * reach + token] * dot_taps(wm, p_w.back(token, taps))
        return carry

    def out_copy(slot):
        rows = slice((first + slot) * CHUNK, (first + slot + 1) * CHUNK)
        return pltpu.make_async_copy(out_s.at[slot], out_hbm.at[:, rows, :], sems.at[slot])

    if bottom:
        lax.fori_loop(0, columns, next_shard, 0)
    for slot in range(steps):
        base = (first + slot) * CHUNK

        def column_step(column, carry):
            lanes = lane_slice(column)
            o_t = Tokens(o_s, repeats)
            for bank in range(3):
                weights = weight_rows(weights_ref, bank, lanes)
                window = Window(lambda t: load(bank, column, base + t))
                for token in range(CHUNK):
                    o_t[token] = dot_taps(weights, window.ahead(token, taps))
                for repeat in range(repeats):
                    part = part_slice(repeat, groups, column)
                    out_s[slot, bank, :, part] = o_t.take(0, repeat, CHUNK).astype(out_s.dtype)
            return carry

        lax.fori_loop(0, columns, column_step, 0)
        out_copy(slot).start()
    for slot in range(steps):
        out_copy(slot).wait()
    for copy in copies:
        copy.wait()


def feature_gradients(
    piece, pieces, features, weights, grads, ghead, gtail, mixed, after, arrays, earlier, zero
):
    banks, length, channels = features.shape
    taps, _, groups = weights.shape
    repeats = channels // groups
    columns = groups // LANES
    reach = taps - 1
    count = length // CHUNK
    steps = count // pieces
    first = piece * steps
    operands = [weights, *grads, ghead, gtail]
    in_specs = [VMEM_SPEC] * len(operands)
    out_shape = [jax.ShapeDtypeStruct(features.shape, features.dtype), zero]
    out_specs = [ANY_SPEC, VMEM_SPEC]
    aliases = {}
    scratch = []
    if piece == 0:
        operands += mixed
        in_specs += [VMEM_SPEC] * 2
        out_shape.append(jax.ShapeDtypeStruct(mixed[0].shape, mixed[0].dtype))
        out_specs.append(ANY_SPEC)
    else:
        aliases = {len(operands): 0}
        operands.append(earlier)
        in_specs.append(ANY_SPEC)
    if piece == pieces - 1:
        q_a, k_a, v_a, _, _, _, p_a, _ = arrays
        operands += [after, q_a, k_a, v_a, p_a]
        in_specs += [VMEM_SPEC] * 5
        halo_rows = -(-after.shape[0] // 8) * 8
        scratch = [
            pltpu.VMEM((3, columns, reach * repeats, LANES), F32),
            pltpu.VMEM((halo_rows, LANES), F32),
            pltpu.VMEM((halo_rows * repeats, LANES), F32),
            pltpu.VMEM((reach * repeats, LANES), F32),
            pltpu.VMEM((2 * reach * repeats, LANES), F32),
        ]
    work = length * channels * taps * 2 // pieces
    return pl.pallas_call(
        functools.partial(grads_kernel, taps, repeats, first, steps, count),
        out_shape=out_shape,
        in_specs=in_specs,
        out_specs=out_specs,
        scratch_shapes=scratch
        + [
            pltpu.VMEM((steps, banks, CHUNK, channels), features.dtype),
            pltpu.VMEM((CHUNK * repeats, LANES), F32),
            pltpu.SemaphoreType.DMA((steps + 2,)),
        ],
        input_output_aliases=aliases,
        cost_estimate=pl.CostEstimate(
            flops=4 * work,
            bytes_accessed=18 * length * channels // pieces,
            transcendentals=0,
        ),
        compiler_params=pltpu.CompilerParams(vmem_limit_bytes=VMEM_LIMIT),
        name="feature_gradients",
    )(*operands)


def per_device(features, cotangent, master_filters):
    length = features.shape[1]
    tail, head, rounded = pack(features, cotangent, jnp.transpose(master_filters, (1, 0, 2)))
    staged, upstream, tail, head = lax.optimization_barrier((features, cotangent, tail, head))
    weights = gather_filters(rounded, "fsdp").astype(F32)
    before = shift_rows(tail, "ctx", 1)
    after = shift_rows(head, "ctx", -1)
    middle, grads, arrays, sums = interior(staged, upstream, weights)
    top, ghead, gtail, sums = edge(weights, before, after, sums, arrays)
    repeats = features.shape[2] // weights.shape[2]
    pieces = PIECES if (length // CHUNK) % PIECES == 0 else 1
    owned = sum_scatter(sums, "fsdp")
    made = {"grads": None}

    def beside(piece):
        if piece >= pieces:
            return 0.0
        made["grads"], zero, *rest = feature_gradients(
            piece,
            pieces,
            features,
            weights,
            grads,
            ghead,
            gtail,
            (middle, top),
            after,
            arrays,
            made["grads"],
            jax.ShapeDtypeStruct(owned.shape, F32),
        )
        if rest:
            made["mixed"] = rest[0]
        return zero

    summed, done = sum_over(owned, "ctx", beside)
    for piece in range(done, pieces):
        beside(piece)
    count_all = length * lax.axis_size("ctx") * repeats * lax.axis_size("fsdp")
    filter_grads = jnp.transpose(summed * (1.0 / math.sqrt(count_all)), (1, 0, 2))
    return (made["mixed"], made["grads"], filter_grads)


def solution(mesh):
    return jax.shard_map(
        per_device,
        mesh=mesh,
        in_specs=(P(None, "ctx", "fsdp"), P("ctx", "fsdp"), P(None, None, "fsdp")),
        out_specs=(P("ctx", "fsdp"), P(None, "ctx", "fsdp"), P(None, None, "fsdp")),
        check_vma=False,
    )
```

```python
import functools
import math

import jax
import jax.numpy as jnp
from jax import lax
from jax.experimental import pallas as pl
from jax.experimental.pallas import tpu as pltpu
from jax.sharding import PartitionSpec as P

LANES = 128
CHUNK = 16
PAD = 16
PIECES = 4
VMEM_LIMIT = 12 * 1024 * 1024
PACK_LIMIT = 16 * 1024 * 1024
F32 = jnp.float32
VMEM_SPEC = pl.BlockSpec(memory_space=pltpu.VMEM)
ANY_SPEC = pl.BlockSpec(memory_space=pl.ANY)


def swap_pairs(near, far, axis):
    size = lax.axis_size(axis)
    inner = [(i, i ^ 1) for i in range(size) if i ^ 1 < size]
    outer = [(i, i - 1 if i % 2 == 0 else i + 1) for i in range(size)]
    outer = [(i, j) for i, j in outer if 0 <= j < size]
    far = lax.ppermute(far, axis, outer)
    near = lax.ppermute(near, axis, inner)
    return near, far


def is_even(axis):
    return lax.rem(lax.axis_index(axis), 2) == 0


def gather_filters(shard, axis):
    size = lax.axis_size(axis)
    if size != 2:
        return lax.all_gather(shard, axis, axis=2, tiled=True)
    other = lax.ppermute(shard, axis, [(0, 1), (1, 0)])
    first = lax.axis_index(axis) == 0
    return jnp.concatenate(
        [jnp.where(first, shard, other), jnp.where(first, other, shard)], axis=2
    )


def sum_over(value, axis, beside=None):
    size = lax.axis_size(axis)
    if size & (size - 1):
        return lax.psum(value, axis), 0
    rounds = size.bit_length() - 1
    for step in range(rounds):
        pairs = [(i, i ^ (1 << step)) for i in range(size)]
        received = lax.ppermute(value, axis, pairs)
        value = value + received
        if beside is not None:
            value = value + beside(step)
    return value, rounds


def sum_scatter(value, axis):
    size = lax.axis_size(axis)
    portion = value.shape[-1] // size
    if size != 2:
        total, _ = sum_over(value, axis)
        return lax.dynamic_slice_in_dim(
            total, lax.axis_index(axis) * portion, portion, value.ndim - 1
        )
    first = lax.axis_index(axis) == 0
    low, high = value[..., :portion], value[..., portion:]
    sent = lax.ppermute(jnp.where(first, high, low), axis, [(0, 1), (1, 0)])
    return jnp.where(first, low, high) + sent


def dot_taps(weights, pieces):
    total = weights[0] * pieces[0]
    for weight, piece in zip(weights[1:], pieces[1:]):
        total = total + weight * piece
    return total


def weight_rows(ref, bank, lanes):
    return [ref[lag, pl.ds(bank, 1), lanes] for lag in range(ref.shape[0])]


def lane_slice(index):
    return pl.ds(pl.multiple_of(index * LANES, LANES), LANES)


def part_slice(repeat, groups, column):
    return pl.ds(pl.multiple_of(repeat * groups + column * LANES, LANES), LANES)


class Tokens:
    def __init__(self, ref, repeats, origin=0, lead=()):
        self.ref, self.repeats, self.origin, self.lead = ref, repeats, origin, lead

    def rows(self, token, count=1):
        start = (self.origin + token) * self.repeats
        if not isinstance(start, int):
            start = pl.multiple_of(start, self.repeats)
        return pl.ds(start, count * self.repeats)

    def __getitem__(self, token):
        return self.ref[(*self.lead, self.rows(token), slice(None))]

    def __setitem__(self, token, value):
        self.ref[(*self.lead, self.rows(token), slice(None))] = value

    def strided(self, token, repeat, count):
        start = (self.origin + token) * self.repeats + repeat
        return pl.ds(start, count, stride=self.repeats)

    def put(self, token, repeat, value):
        rows = self.strided(token, repeat, value.shape[0])
        self.ref[(*self.lead, rows, slice(None))] = value

    def take(self, token, repeat, count):
        return self.ref[(*self.lead, self.strided(token, repeat, count), slice(None))]


class Window:
    def __init__(self, load):
        self.load, self.held = load, {}

    def __call__(self, token):
        if token not in self.held:
            self.held[token] = self.load(token)
        return self.held[token]

    def back(self, token, taps):
        return [self(token - lag) for lag in range(taps)]

    def ahead(self, token, taps):
        return [self(token + lag) for lag in range(taps)]


class Sums:
    def __init__(self, taps):
        self.taps = taps
        self.held = {}

    def add(self, bank, grad, pieces):
        for lag, piece in enumerate(pieces):
            term = grad * piece
            old = self.held.get((bank, lag))
            self.held[bank, lag] = term if old is None else old + term

    def store(self, ref, lanes):
        for (bank, lag), value in self.held.items():
            ref[bank, lag, :, lanes] += value


def pack_kernel(
    reach,
    features_hbm,
    cotangent_hbm,
    master_hbm,
    near_ref,
    far_ref,
    rounded_ref,
    tail,
    head,
    upstream,
    master,
    b_s,
    a_s,
    sems,
):
    length = cotangent_hbm.shape[0]
    copies = [
        pltpu.make_async_copy(master_hbm, master, sems.at[3]),
        pltpu.make_async_copy(features_hbm.at[:, length - PAD :, :], tail, sems.at[0]),
        pltpu.make_async_copy(features_hbm.at[:, :PAD, :], head, sems.at[1]),
        pltpu.make_async_copy(cotangent_hbm.at[:PAD, :], upstream, sems.at[2]),
    ]
    for copy in copies:
        copy.start()
    even = is_even("ctx")
    b_s[...] = jnp.zeros_like(b_s)
    for copy in copies:
        copy.wait()
    rounded_ref[...] = master[...].astype(rounded_ref.dtype)

    def column(index, carry):
        lanes = lane_slice(index)

        def rows(ref, bank, start, stop):
            return ref[bank, :, lanes].astype(F32)[start:stop]

        b_s[0:reach, :] = rows(tail, 0, PAD - reach, PAD)
        b_s[reach : 3 * reach, :] = rows(tail, 1, PAD - 2 * reach, PAD)
        b_s[3 * reach : 5 * reach, :] = rows(tail, 2, PAD - 2 * reach, PAD)
        a_s[0 : 2 * reach, :] = rows(head, 0, 0, 2 * reach)
        a_s[2 * reach : 4 * reach, :] = upstream[:, lanes].astype(F32)[: 2 * reach]
        a_s[4 * reach : 5 * reach, :] = rows(head, 1, 0, reach)
        a_s[5 * reach : 6 * reach, :] = rows(head, 2, 0, reach)
        last, first = b_s[...], a_s[...]
        near_ref[:, lanes] = jnp.where(even, last, first).astype(near_ref.dtype)
        far_ref[:, lanes] = jnp.where(even, first, last).astype(far_ref.dtype)
        return carry

    lax.fori_loop(0, near_ref.shape[1] // LANES, column, 0)


def pack(features, cotangent, master):
    reach = master.shape[0] - 1
    banks, length, channels = features.shape
    kind = features.dtype
    hbm = [
        pltpu.with_memory_space_constraint(value, pltpu.HBM)
        for value in (features, cotangent, master)
    ]
    message = jax.ShapeDtypeStruct((6 * reach, channels), kind)
    return pl.pallas_call(
        functools.partial(pack_kernel, reach),
        out_shape=(message, message, jax.ShapeDtypeStruct(master.shape, jnp.bfloat16)),
        in_specs=[pl.BlockSpec(memory_space=pltpu.HBM)] * 3,
        out_specs=(VMEM_SPEC,) * 3,
        scratch_shapes=[
            pltpu.VMEM((banks, PAD, channels), kind),
            pltpu.VMEM((banks, PAD, channels), kind),
            pltpu.VMEM((PAD, channels), kind),
            pltpu.VMEM(master.shape, F32),
            pltpu.VMEM((6 * reach, LANES), F32),
            pltpu.VMEM((6 * reach, LANES), F32),
            pltpu.SemaphoreType.DMA((4,)),
        ],
        cost_estimate=pl.CostEstimate(flops=10**6, bytes_accessed=10**6, transcendentals=0),
        compiler_params=pltpu.CompilerParams(vmem_limit_bytes=PACK_LIMIT),
        name="pack_halos",
    )(*hbm)


def interior_kernel(
    taps,
    repeats,
    features_ref,
    cotangent_ref,
    weights_ref,
    mixed_ref,
    gq_ref,
    gk_ref,
    gv_ref,
    q_s,
    k_s,
    v_s,
    c_s,
    kc_s,
    vc_s,
    p_s,
    gm_s,
    sums_ref,
    m_s,
):
    reach = taps - 1
    groups = weights_ref.shape[2]
    length = cotangent_ref.shape[0]
    count = length // CHUNK
    sums_ref[...] = jnp.zeros_like(sums_ref)
    m_t = Tokens(m_s, repeats)

    def column_step(column, carry):
        lanes = lane_slice(column)
        gq_t, gk_t, gv_t = (
            Tokens(ref, repeats, 0, (column,)) for ref in (gq_ref, gk_ref, gv_ref)
        )
        q_t, k_t, v_t, c_t, kc_t, vc_t, p_t, gm_t = (
            Tokens(ref, repeats, PAD, (column,))
            for ref in (q_s, k_s, v_s, c_s, kc_s, vc_s, p_s, gm_s)
        )
        zero = jnp.zeros((reach * repeats, LANES), F32)
        for ref in (q_s, k_s, v_s, p_s):
            ref[column, (PAD - reach) * repeats : PAD * repeats, :] = zero
        gm_s[column, gm_t.rows(length, reach), :] = zero
        wq, wk, wv, wm = (weight_rows(weights_ref, bank, lanes) for bank in range(4))

        def forward(step, carry):
            base = pl.multiple_of(step * CHUNK, CHUNK)
            rows = pl.ds(base, CHUNK)
            for repeat in range(repeats):
                part = part_slice(repeat, groups, column)
                for bank, view in enumerate((q_t, k_t, v_t)):
                    view.put(base, repeat, features_ref[bank, rows, part].astype(F32))
                c_t.put(base, repeat, cotangent_ref[rows, part].astype(F32))
            k_w, v_w = (Window(lambda t, view=view: view[base + t]) for view in (k_t, v_t))
            for token in range(CHUNK):
                kc = dot_taps(wk, k_w.back(token, taps))
                vc = dot_taps(wv, v_w.back(token, taps))
                kc_t[base + token] = kc
                vc_t[base + token] = vc
                p_t[base + token] = kc * vc
            sums = Sums(taps)
            q_w, p_w = (Window(lambda t, view=view: view[base + t]) for view in (q_t, p_t))
            for token in range(CHUNK):
                up = c_t[base + token]
                sources = q_w.back(token, taps)
                products = p_w.back(token, taps)
                qc = dot_taps(wq, sources)
                mixer = dot_taps(wm, products)
                gq = up * mixer
                gm = up * qc
                m_t[token] = qc * mixer
                gm_t[base + token] = gm
                gq_t[base + token] = gq
                if token < 2 * reach:
                    gq = jnp.where(step > 0, gq, 0.0)
                    gm = jnp.where(step > 0, gm, 0.0)
                sums.add(0, gq, sources)
                sums.add(3, gm, products)
            sums.store(sums_ref, lanes)
            for repeat in range(repeats):
                part = part_slice(repeat, groups, column)
                mixed_ref[rows, part] = m_t.take(0, repeat, CHUNK).astype(mixed_ref.dtype)
            return carry

        def backward(step, carry):
            base = pl.multiple_of(step * CHUNK, CHUNK)
            k_w, v_w, gm_w = (
                Window(lambda t, view=view: view[base + t]) for view in (k_t, v_t, gm_t)
            )
            sums = Sums(taps)
            for token in range(CHUNK):
                gp = dot_taps(wm, gm_w.ahead(token, taps))
                if token < reach:
                    gp = jnp.where(step > 0, gp, 0.0)
                if token >= CHUNK - reach:
                    gp = jnp.where(step < count - 1, gp, 0.0)
                gk = gp * vc_t[base + token]
                gv = gp * kc_t[base + token]
                gk_t[base + token] = gk
                gv_t[base + token] = gv
                sums.add(1, gk, k_w.back(token, taps))
                sums.add(2, gv, v_w.back(token, taps))
            sums.store(sums_ref, lanes)
            return carry

        lax.fori_loop(0, count, forward, 0)
        lax.fori_loop(0, count, backward, 0)
        return carry

    lax.fori_loop(0, groups // LANES, column_step, 0)


def interior(features, cotangent, weights):
    length, channels = cotangent.shape
    taps, banks, groups = weights.shape
    repeats = channels // groups
    columns = groups // LANES
    work = length * channels * taps * 2
    grad = jax.ShapeDtypeStruct((columns, length * repeats, LANES), F32)
    held = jax.ShapeDtypeStruct((columns, (length + 2 * PAD) * repeats, LANES), F32)
    mixed, gq, gk, gv, *arrays, sums = pl.pallas_call(
        functools.partial(interior_kernel, taps, repeats),
        out_shape=(
            jax.ShapeDtypeStruct(cotangent.shape, cotangent.dtype),
            *[grad] * 3,
            *[held] * 8,
            jax.ShapeDtypeStruct((banks, taps, repeats, groups), F32),
        ),
        in_specs=[VMEM_SPEC] * 3,
        out_specs=(VMEM_SPEC,) * 13,
        scratch_shapes=[pltpu.VMEM((CHUNK * repeats, LANES), F32)],
        cost_estimate=pl.CostEstimate(
            flops=9 * work, bytes_accessed=22 * length * channels, transcendentals=0
        ),
        compiler_params=pltpu.CompilerParams(vmem_limit_bytes=VMEM_LIMIT),
        name="interior",
    )(features, cotangent, weights)
    return mixed, (gq, gk, gv), arrays, sums


def stage_halo(load, n_s, view, repeats, groups, column, rows):
    for repeat in range(repeats):
        n_s[0:rows, :] = load(part_slice(repeat, groups, column)).astype(F32)
        view.put(0, repeat, n_s[...])


def edge_kernel(
    taps,
    repeats,
    weights_ref,
    near_ref,
    far_ref,
    sums_in_ref,
    q_a,
    k_a,
    v_a,
    c_a,
    kc_a,
    vc_a,
    p_a,
    gm_a,
    mixed_ref,
    ghead_ref,
    gtail_ref,
    after_ref,
    sums_ref,
    acc,
    n_s,
    h_s,
    kc_s,
    vc_s,
    p_s,
    gm_s,
    m_s,
):
    reach = taps - 1
    groups = weights_ref.shape[2]
    length = q_a.shape[1] // repeats - 2 * PAD
    acc[...] = sums_in_ref[...]
    even = is_even("ctx")
    h_t, m_t = Tokens(h_s, repeats), Tokens(m_s, repeats)
    kc_t, vc_t, p_t, gm_t = (Tokens(ref, repeats, PAD) for ref in (kc_s, vc_s, p_s, gm_s))

    def column_step(column, carry):
        lanes = lane_slice(column)
        wq, wk, wv, wm = (weight_rows(weights_ref, bank, lanes) for bank in range(4))
        q_t, k_t, v_t, c_t, kc_i, vc_i, p_i, gm_i = (
            Tokens(ref, repeats, PAD, (column,))
            for ref in (q_a, k_a, v_a, c_a, kc_a, vc_a, p_a, gm_a)
        )
        sums = Sums(taps)

        def before(part):
            rows = slice(0, 5 * reach)
            return jnp.where(
                even, far_ref[rows, part].astype(F32), near_ref[rows, part].astype(F32)
            )

        def after(part):
            value = jnp.where(even, near_ref[:, part].astype(F32), far_ref[:, part].astype(F32))
            after_ref[:, part] = value.astype(after_ref.dtype)
            return value

        stage_halo(before, n_s, h_t, repeats, groups, column, 5 * reach)
        q_w = Window(lambda t: q_t[t] if t >= 0 else h_t[reach + t])
        k_w = Window(lambda t: k_t[t] if t >= 0 else h_t[3 * reach + t])
        v_w = Window(lambda t: v_t[t] if t >= 0 else h_t[5 * reach + t])
        gq_o, gk_o, gv_o = (Tokens(ghead_ref, repeats, 0, (bank, column)) for bank in range(3))
        for token in range(-reach, reach):
            kc = dot_taps(wk, k_w.back(token, taps))
            vc = dot_taps(wv, v_w.back(token, taps))
            p_t[token] = kc * vc
            if token >= 0:
                kc_t[token] = kc
                vc_t[token] = vc
        p_w = Window(lambda t: p_t[t] if t < reach else p_i[t])
        for token in range(CHUNK):
            up = c_t[token]
            sources = q_w.back(token, taps)
            products = p_w.back(token, taps)
            qc = dot_taps(wq, sources)
            mixer = dot_taps(wm, products)
            m_t[token] = qc * mixer
            if token < 2 * reach:
                gq = up * mixer
                gm = up * qc
                gm_t[token] = gm
                gq_o[token] = gq
                sums.add(0, gq, sources)
                sums.add(3, gm, products)
        gm_w = Window(lambda t: gm_t[t])
        for token in range(reach):
            gp = dot_taps(wm, gm_w.ahead(token, taps))
            gk = gp * vc_t[token]
            gv = gp * kc_t[token]
            gk_o[token] = gk
            gv_o[token] = gv
            sums.add(1, gk, k_w.back(token, taps))
            sums.add(2, gv, v_w.back(token, taps))
        for repeat in range(repeats):
            part = part_slice(repeat, groups, column)
            mixed_ref[:, part] = m_t.take(0, repeat, CHUNK).astype(mixed_ref.dtype)

        stage_halo(after, n_s, h_t, repeats, groups, column, 6 * reach)
        q_w = Window(lambda t: q_t[length + t] if t < 0 else h_t[t])
        gk_o, gv_o = (Tokens(gtail_ref, repeats, reach, (bank, column)) for bank in range(2))
        for token in range(reach):
            gm_t[token] = h_t[2 * reach + token] * dot_taps(wq, q_w.back(token, taps))
        gm_w = Window(lambda t: gm_i[length + t] if t < 0 else gm_t[t])
        k_w, v_w = (Window(lambda t, view=view: view[length + t]) for view in (k_t, v_t))
        for token in range(-reach, 0):
            gp = dot_taps(wm, gm_w.ahead(token, taps))
            gk = gp * vc_i[length + token]
            gv = gp * kc_i[length + token]
            gk_o[token] = gk
            gv_o[token] = gv
            sums.add(1, gk, k_w.back(token, taps))
            sums.add(2, gv, v_w.back(token, taps))
        sums.store(acc, lanes)
        return carry

    lax.fori_loop(0, groups // LANES, column_step, 0)
    for bank in range(sums_ref.shape[1]):
        sums_ref[:, bank, :] = jnp.sum(acc[bank], axis=1)


def edge(weights, near, far, sums, arrays):
    taps, banks, groups = weights.shape
    channels = near.shape[1]
    repeats = channels // groups
    columns = groups // LANES
    reach = taps - 1
    halo_rows = -(-6 * reach // 8) * 8
    return pl.pallas_call(
        functools.partial(edge_kernel, taps, repeats),
        out_shape=(
            jax.ShapeDtypeStruct((CHUNK, channels), near.dtype),
            jax.ShapeDtypeStruct((3, columns, 2 * reach * repeats, LANES), F32),
            jax.ShapeDtypeStruct((2, columns, reach * repeats, LANES), F32),
            jax.ShapeDtypeStruct(near.shape, near.dtype),
            jax.ShapeDtypeStruct((taps, banks, groups), F32),
        ),
        in_specs=[VMEM_SPEC] * 12,
        out_specs=(VMEM_SPEC,) * 5,
        scratch_shapes=[
            pltpu.VMEM(sums.shape, F32),
            pltpu.VMEM((halo_rows, LANES), F32),
            pltpu.VMEM((halo_rows * repeats, LANES), F32),
        ]
        + [pltpu.VMEM((2 * PAD * repeats, LANES), F32) for _ in range(4)]
        + [pltpu.VMEM((CHUNK * repeats, LANES), F32)],
        cost_estimate=pl.CostEstimate(
            flops=10**7, bytes_accessed=4 * 10**6, transcendentals=0
        ),
        compiler_params=pltpu.CompilerParams(vmem_limit_bytes=VMEM_LIMIT),
        name="edge",
    )(weights, near, far, sums, *arrays)


def grads_kernel(taps, repeats, first, steps, count, *refs):
    refs = list(refs)
    top, bottom = first == 0, first + steps == count

    def pop(number):
        taken, refs[:number] = refs[:number], []
        return taken

    weights_ref, gq, gk, gv, ghead, gtail = pop(6)
    if top:
        middle, head = pop(2)
    else:
        pop(1)
    if bottom:
        after_ref, *ahead_of = pop(5)
    out_hbm, zero_ref = pop(2)
    copies = []
    out_s, o_s, sems = refs[-3:]
    reach = taps - 1
    groups = weights_ref.shape[2]
    columns = groups // LANES
    length = gq.shape[1] // repeats
    zero_ref[...] = jnp.zeros_like(zero_ref)
    if top:
        (mixed_hbm,) = pop(1)
        copies = [
            pltpu.make_async_copy(head, mixed_hbm.at[:CHUNK, :], sems.at[steps]),
            pltpu.make_async_copy(
                middle.at[CHUNK:, :], mixed_hbm.at[CHUNK:, :], sems.at[steps + 1]
            ),
        ]
        for copy in copies:
            copy.start()

    def load(bank, column, token):
        if token >= length:
            return Tokens(refs[0], repeats, 0, (bank, column))[token - length]
        if token < (reach if bank else 2 * reach):
            return Tokens(ghead, repeats, 0, (bank, column))[token]
        if bank and token >= length - reach:
            return Tokens(gtail, repeats, reach - length, (bank - 1, column))[token]
        return Tokens((gq, gk, gv)[bank], repeats, 0, (column,))[token]

    def next_shard(column, carry):
        gnext, n_s, h_s, p_s, gm_s = refs[:5]
        lanes = lane_slice(column)
        wq, wk, wv, wm = (weight_rows(weights_ref, bank, lanes) for bank in range(4))
        h_t, p_t, gm_t = (Tokens(ref, repeats) for ref in (h_s, p_s, gm_s))
        q_t, k_t, v_t, p_i = (
            Tokens(ref, repeats, PAD + length, (column,)) for ref in ahead_of
        )
        stage_halo(lambda part: after_ref[:, part], n_s, h_t, repeats, groups, column, 6 * reach)
        q_w = Window(lambda t: q_t[t] if t < 0 else h_t[t])
        k_w = Window(lambda t: k_t[t] if t < 0 else h_t[4 * reach + t])
        v_w = Window(lambda t: v_t[t] if t < 0 else h_t[5 * reach + t])
        p_w = Window(lambda t: p_i[t] if t < 0 else p_t[t])
        gm_w = Window(lambda t: gm_t[t])
        next_q, next_k, next_v = (
            Tokens(gnext, repeats, 0, (bank, column)) for bank in range(3)
        )
        for token in range(2 * reach):
            gm_t[token] = h_t[2 * reach + token] * dot_taps(wq, q_w.back(token, taps))
        for token in range(reach):
            kc = dot_taps(wk, k_w.back(token, taps))
            vc = dot_taps(wv, v_w.back(token, taps))
            p_t[token] = kc * vc
            gp = dot_taps(wm, gm_w.ahead(token, taps))
            next_k[token] = gp * vc
            next_v[token] = gp * kc
            next_q[token] = h_t[2 * reach + token] * dot_taps(wm, p_w.back(token, taps))
        return carry

    def out_copy(slot):
        rows = slice((first + slot) * CHUNK, (first + slot + 1) * CHUNK)
        return pltpu.make_async_copy(out_s.at[slot], out_hbm.at[:, rows, :], sems.at[slot])

    if bottom:
        lax.fori_loop(0, columns, next_shard, 0)
    for slot in range(steps):
        base = (first + slot) * CHUNK

        def column_step(column, carry):
            lanes = lane_slice(column)
            o_t = Tokens(o_s, repeats)
            for bank in range(3):
                weights = weight_rows(weights_ref, bank, lanes)
                window = Window(lambda t: load(bank, column, base + t))
                for token in range(CHUNK):
                    o_t[token] = dot_taps(weights, window.ahead(token, taps))
                for repeat in range(repeats):
                    part = part_slice(repeat, groups, column)
                    out_s[slot, bank, :, part] = o_t.take(0, repeat, CHUNK).astype(out_s.dtype)
            return carry

        lax.fori_loop(0, columns, column_step, 0)
        out_copy(slot).start()
    for slot in range(steps):
        out_copy(slot).wait()
    for copy in copies:
        copy.wait()


def feature_gradients(
    piece, pieces, features, weights, grads, ghead, gtail, mixed, after, arrays, earlier, zero
):
    banks, length, channels = features.shape
    taps, _, groups = weights.shape
    repeats = channels // groups
    columns = groups // LANES
    reach = taps - 1
    count = length // CHUNK
    steps = count // pieces
    first = piece * steps
    operands = [weights, *grads, ghead, gtail]
    in_specs = [VMEM_SPEC] * len(operands)
    out_shape = [jax.ShapeDtypeStruct(features.shape, features.dtype), zero]
    out_specs = [ANY_SPEC, VMEM_SPEC]
    aliases = {}
    scratch = []
    if piece == 0:
        operands += mixed
        in_specs += [VMEM_SPEC] * 2
        out_shape.append(jax.ShapeDtypeStruct(mixed[0].shape, mixed[0].dtype))
        out_specs.append(ANY_SPEC)
    else:
        aliases = {len(operands): 0}
        operands.append(earlier)
        in_specs.append(ANY_SPEC)
    if piece == pieces - 1:
        q_a, k_a, v_a, _, _, _, p_a, _ = arrays
        operands += [after, q_a, k_a, v_a, p_a]
        in_specs += [VMEM_SPEC] * 5
        halo_rows = -(-after.shape[0] // 8) * 8
        scratch = [
            pltpu.VMEM((3, columns, reach * repeats, LANES), F32),
            pltpu.VMEM((halo_rows, LANES), F32),
            pltpu.VMEM((halo_rows * repeats, LANES), F32),
            pltpu.VMEM((reach * repeats, LANES), F32),
            pltpu.VMEM((2 * reach * repeats, LANES), F32),
        ]
    work = length * channels * taps * 2 // pieces
    return pl.pallas_call(
        functools.partial(grads_kernel, taps, repeats, first, steps, count),
        out_shape=out_shape,
        in_specs=in_specs,
        out_specs=out_specs,
        scratch_shapes=scratch
        + [
            pltpu.VMEM((steps, banks, CHUNK, channels), features.dtype),
            pltpu.VMEM((CHUNK * repeats, LANES), F32),
            pltpu.SemaphoreType.DMA((steps + 2,)),
        ],
        input_output_aliases=aliases,
        cost_estimate=pl.CostEstimate(
            flops=4 * work,
            bytes_accessed=18 * length * channels // pieces,
            transcendentals=0,
        ),
        compiler_params=pltpu.CompilerParams(vmem_limit_bytes=VMEM_LIMIT),
        name="feature_gradients",
    )(*operands)


def per_device(features, cotangent, master_filters):
    length = features.shape[1]
    near, far, rounded = pack(features, cotangent, jnp.transpose(master_filters, (1, 0, 2)))
    weights = gather_filters(rounded, "fsdp").astype(F32)
    halos = swap_pairs(near, far, "ctx")
    middle, grads, arrays, sums = interior(features, cotangent, weights)
    top, ghead, gtail, after, sums = edge(weights, *halos, sums, arrays)
    repeats = features.shape[2] // weights.shape[2]
    pieces = PIECES if (length // CHUNK) % PIECES == 0 else 1
    owned = sum_scatter(sums, "fsdp")
    made = {"grads": None}

    def beside(piece):
        if piece >= pieces:
            return 0.0
        made["grads"], zero, *rest = feature_gradients(
            piece,
            pieces,
            features,
            weights,
            grads,
            ghead,
            gtail,
            (middle, top),
            after,
            arrays,
            made["grads"],
            jax.ShapeDtypeStruct(owned.shape, F32),
        )
        if rest:
            made["mixed"] = rest[0]
        return zero

    summed, done = sum_over(owned, "ctx", beside)
    for piece in range(done, pieces):
        beside(piece)
    count_all = length * lax.axis_size("ctx") * repeats * lax.axis_size("fsdp")
    filter_grads = jnp.transpose(summed * (1.0 / math.sqrt(count_all)), (1, 0, 2))
    return (made["mixed"], made["grads"], filter_grads)


def solution(mesh):
    return jax.shard_map(
        per_device,
        mesh=mesh,
        in_specs=(P(None, "ctx", "fsdp"), P("ctx", "fsdp"), P(None, None, "fsdp")),
        out_specs=(P("ctx", "fsdp"), P(None, "ctx", "fsdp"), P(None, None, "fsdp")),
        check_vma=False,
    )
```

```python
import functools
import math

import jax
import jax.numpy as jnp
from jax import lax
from jax.experimental import pallas as pl
from jax.experimental.pallas import tpu as pltpu
from jax.sharding import PartitionSpec as P

LANES = 128
CHUNK = 16
PAD = 16
PIECES = 4
VMEM_LIMIT = 12 * 1024 * 1024
PACK_LIMIT = 16 * 1024 * 1024
F32 = jnp.float32
VMEM_SPEC = pl.BlockSpec(memory_space=pltpu.VMEM)
ANY_SPEC = pl.BlockSpec(memory_space=pl.ANY)


def swap_pairs(near, far, axis):
    size = lax.axis_size(axis)
    inner = [(i, i ^ 1) for i in range(size) if i ^ 1 < size]
    outer = [(i, i - 1 if i % 2 == 0 else i + 1) for i in range(size)]
    outer = [(i, j) for i, j in outer if 0 <= j < size]
    far = lax.ppermute(far, axis, outer)
    near = lax.ppermute(near, axis, inner)
    return near, far


def is_even(axis):
    return lax.rem(lax.axis_index(axis), 2) == 0


def gather_filters(shard, axis):
    size = lax.axis_size(axis)
    if size != 2:
        return lax.all_gather(shard, axis, axis=2, tiled=True)
    other = lax.ppermute(shard, axis, [(0, 1), (1, 0)])
    first = lax.axis_index(axis) == 0
    return jnp.concatenate(
        [jnp.where(first, shard, other), jnp.where(first, other, shard)], axis=2
    )


def sum_over(value, axis, beside=None):
    size = lax.axis_size(axis)
    if size & (size - 1):
        return lax.psum(value, axis), 0
    rounds = size.bit_length() - 1
    for step in range(rounds):
        pairs = [(i, i ^ (1 << step)) for i in range(size)]
        received = lax.ppermute(value, axis, pairs)
        value = value + received
        if beside is not None:
            value = value + beside(step)
    return value, rounds


def sum_scatter(value, axis):
    size = lax.axis_size(axis)
    portion = value.shape[-1] // size
    if size != 2:
        total, _ = sum_over(value, axis)
        return lax.dynamic_slice_in_dim(
            total, lax.axis_index(axis) * portion, portion, value.ndim - 1
        )
    first = lax.axis_index(axis) == 0
    low, high = value[..., :portion], value[..., portion:]
    sent = lax.ppermute(jnp.where(first, high, low), axis, [(0, 1), (1, 0)])
    return jnp.where(first, low, high) + sent


def dot_taps(weights, pieces):
    total = weights[0] * pieces[0]
    for weight, piece in zip(weights[1:], pieces[1:]):
        total = total + weight * piece
    return total


def weight_rows(ref, bank, lanes):
    return [ref[lag, pl.ds(bank, 1), lanes] for lag in range(ref.shape[0])]


def lane_slice(index):
    return pl.ds(pl.multiple_of(index * LANES, LANES), LANES)


def part_slice(repeat, groups, column):
    return pl.ds(pl.multiple_of(repeat * groups + column * LANES, LANES), LANES)


class Tokens:
    def __init__(self, ref, repeats, origin=0, lead=()):
        self.ref, self.repeats, self.origin, self.lead = ref, repeats, origin, lead

    def rows(self, token, count=1):
        start = (self.origin + token) * self.repeats
        if not isinstance(start, int):
            start = pl.multiple_of(start, self.repeats)
        return pl.ds(start, count * self.repeats)

    def __getitem__(self, token):
        return self.ref[(*self.lead, self.rows(token), slice(None))]

    def __setitem__(self, token, value):
        self.ref[(*self.lead, self.rows(token), slice(None))] = value

    def strided(self, token, repeat, count):
        start = (self.origin + token) * self.repeats + repeat
        return pl.ds(start, count, stride=self.repeats)

    def put(self, token, repeat, value):
        rows = self.strided(token, repeat, value.shape[0])
        self.ref[(*self.lead, rows, slice(None))] = value

    def take(self, token, repeat, count):
        return self.ref[(*self.lead, self.strided(token, repeat, count), slice(None))]


def held_tokens(reach):
    wide = 2 * reach
    return (
        (0, CHUNK, reach),
        (0, reach, wide),
        (0, reach, wide),
        (0, CHUNK, 0),
        (0, 0, reach),
        (0, 0, reach),
        (reach, CHUNK, reach),
        (0, 0, reach),
    )


class Held:
    def __init__(self, ref, repeats, column, span):
        self.first, self.last, self.tail = span
        self.view = Tokens(ref, repeats, 0, (column,))

    def __getitem__(self, token):
        if token < 0:
            return self.view[self.last - self.first + self.tail + token]
        return self.view[token - self.first]


class Window:
    def __init__(self, load):
        self.load, self.held = load, {}

    def __call__(self, token):
        if token not in self.held:
            self.held[token] = self.load(token)
        return self.held[token]

    def back(self, token, taps):
        return [self(token - lag) for lag in range(taps)]

    def ahead(self, token, taps):
        return [self(token + lag) for lag in range(taps)]


class Sums:
    def __init__(self, taps):
        self.taps = taps
        self.held = {}

    def add(self, bank, grad, pieces):
        for lag, piece in enumerate(pieces):
            term = grad * piece
            old = self.held.get((bank, lag))
            self.held[bank, lag] = term if old is None else old + term

    def store(self, ref, lanes):
        for (bank, lag), value in self.held.items():
            ref[bank, lag, :, lanes] += value


def pack_kernel(
    reach,
    features_hbm,
    cotangent_hbm,
    master_hbm,
    near_ref,
    far_ref,
    rounded_ref,
    tail,
    head,
    upstream,
    master,
    b_s,
    a_s,
    sems,
):
    length = cotangent_hbm.shape[0]
    copies = [
        pltpu.make_async_copy(master_hbm, master, sems.at[3]),
        pltpu.make_async_copy(features_hbm.at[:, length - PAD :, :], tail, sems.at[0]),
        pltpu.make_async_copy(features_hbm.at[:, :PAD, :], head, sems.at[1]),
        pltpu.make_async_copy(cotangent_hbm.at[:PAD, :], upstream, sems.at[2]),
    ]
    for copy in copies:
        copy.start()
    even = is_even("ctx")
    b_s[...] = jnp.zeros_like(b_s)
    for copy in copies:
        copy.wait()
    rounded_ref[...] = master[...].astype(rounded_ref.dtype)

    def column(index, carry):
        lanes = lane_slice(index)

        def rows(ref, bank, start, stop):
            return ref[bank, :, lanes].astype(F32)[start:stop]

        b_s[0:reach, :] = rows(tail, 0, PAD - reach, PAD)
        b_s[reach : 3 * reach, :] = rows(tail, 1, PAD - 2 * reach, PAD)
        b_s[3 * reach : 5 * reach, :] = rows(tail, 2, PAD - 2 * reach, PAD)
        a_s[0 : 2 * reach, :] = rows(head, 0, 0, 2 * reach)
        a_s[2 * reach : 4 * reach, :] = upstream[:, lanes].astype(F32)[: 2 * reach]
        a_s[4 * reach : 5 * reach, :] = rows(head, 1, 0, reach)
        a_s[5 * reach : 6 * reach, :] = rows(head, 2, 0, reach)
        last, first = b_s[...], a_s[...]
        near_ref[:, lanes] = jnp.where(even, last, first).astype(near_ref.dtype)
        far_ref[:, lanes] = jnp.where(even, first, last).astype(far_ref.dtype)
        return carry

    lax.fori_loop(0, near_ref.shape[1] // LANES, column, 0)


def pack(features, cotangent, master):
    reach = master.shape[0] - 1
    banks, length, channels = features.shape
    kind = features.dtype
    hbm = [
        pltpu.with_memory_space_constraint(value, pltpu.HBM)
        for value in (features, cotangent, master)
    ]
    message = jax.ShapeDtypeStruct((6 * reach, channels), kind)
    return pl.pallas_call(
        functools.partial(pack_kernel, reach),
        out_shape=(message, message, jax.ShapeDtypeStruct(master.shape, jnp.bfloat16)),
        in_specs=[pl.BlockSpec(memory_space=pltpu.HBM)] * 3,
        out_specs=(VMEM_SPEC,) * 3,
        scratch_shapes=[
            pltpu.VMEM((banks, PAD, channels), kind),
            pltpu.VMEM((banks, PAD, channels), kind),
            pltpu.VMEM((PAD, channels), kind),
            pltpu.VMEM(master.shape, F32),
            pltpu.VMEM((6 * reach, LANES), F32),
            pltpu.VMEM((6 * reach, LANES), F32),
            pltpu.SemaphoreType.DMA((4,)),
        ],
        cost_estimate=pl.CostEstimate(flops=10**6, bytes_accessed=10**6, transcendentals=0),
        compiler_params=pltpu.CompilerParams(vmem_limit_bytes=PACK_LIMIT),
        name="pack_halos",
    )(*hbm)


def interior_kernel(
    taps,
    repeats,
    features_ref,
    cotangent_hbm,
    weights_ref,
    mixed_ref,
    gq_ref,
    gk_ref,
    gv_ref,
    *refs,
):
    *held_refs, sums_ref = refs[:9]
    *work_refs, m_s, cotangent_ref, sem = refs[9:]
    q_s, k_s, v_s, c_s, kc_s, vc_s, p_s, gm_s = work_refs
    reach = taps - 1
    groups = weights_ref.shape[2]
    length = cotangent_ref.shape[0]
    count = length // CHUNK
    fetch = pltpu.make_async_copy(cotangent_hbm, cotangent_ref, sem)
    fetch.start()
    sums_ref[...] = jnp.zeros_like(sums_ref)
    m_t = Tokens(m_s, repeats)

    def column_step(column, carry):
        lanes = lane_slice(column)
        gq_t, gk_t, gv_t = (
            Tokens(ref, repeats, 0, (column,)) for ref in (gq_ref, gk_ref, gv_ref)
        )
        q_t, k_t, v_t, c_t, kc_t, vc_t, p_t, gm_t = (
            Tokens(ref, repeats, PAD) for ref in work_refs
        )
        zero = jnp.zeros((reach * repeats, LANES), F32)
        for ref in (q_s, k_s, v_s, p_s):
            ref[(PAD - reach) * repeats : PAD * repeats, :] = zero
        gm_s[gm_t.rows(length, reach), :] = zero
        wq, wk, wv, wm = (weight_rows(weights_ref, bank, lanes) for bank in range(4))

        def products(step, carry):
            base = pl.multiple_of(step * CHUNK, CHUNK)
            rows = pl.ds(base, CHUNK)
            for repeat in range(repeats):
                part = part_slice(repeat, groups, column)
                k_t.put(base, repeat, features_ref[1, rows, part].astype(F32))
                v_t.put(base, repeat, features_ref[2, rows, part].astype(F32))
            k_w, v_w = (Window(lambda t, view=view: view[base + t]) for view in (k_t, v_t))
            for token in range(CHUNK):
                kc = dot_taps(wk, k_w.back(token, taps))
                vc = dot_taps(wv, v_w.back(token, taps))
                kc_t[base + token] = kc
                vc_t[base + token] = vc
                p_t[base + token] = kc * vc
            return carry

        def forward(step, carry):
            base = pl.multiple_of(step * CHUNK, CHUNK)
            rows = pl.ds(base, CHUNK)
            for repeat in range(repeats):
                part = part_slice(repeat, groups, column)
                q_t.put(base, repeat, features_ref[0, rows, part].astype(F32))
                c_t.put(base, repeat, cotangent_ref[rows, part].astype(F32))
            sums = Sums(taps)
            q_w, p_w = (Window(lambda t, view=view: view[base + t]) for view in (q_t, p_t))
            for token in range(CHUNK):
                up = c_t[base + token]
                sources = q_w.back(token, taps)
                inner = p_w.back(token, taps)
                qc = dot_taps(wq, sources)
                mixer = dot_taps(wm, inner)
                gq = up * mixer
                gm = up * qc
                m_t[token] = qc * mixer
                gm_t[base + token] = gm
                gq_t[base + token] = gq
                if token < 2 * reach:
                    gq = jnp.where(step > 0, gq, 0.0)
                    gm = jnp.where(step > 0, gm, 0.0)
                sums.add(0, gq, sources)
                sums.add(3, gm, inner)
            sums.store(sums_ref, lanes)
            for repeat in range(repeats):
                part = part_slice(repeat, groups, column)
                mixed_ref[rows, part] = m_t.take(0, repeat, CHUNK).astype(mixed_ref.dtype)
            return carry

        def backward(step, carry):
            base = pl.multiple_of(step * CHUNK, CHUNK)
            k_w, v_w, gm_w = (
                Window(lambda t, view=view: view[base + t]) for view in (k_t, v_t, gm_t)
            )
            sums = Sums(taps)
            for token in range(CHUNK):
                gp = dot_taps(wm, gm_w.ahead(token, taps))
                if token < reach:
                    gp = jnp.where(step > 0, gp, 0.0)
                if token >= CHUNK - reach:
                    gp = jnp.where(step < count - 1, gp, 0.0)
                gk = gp * vc_t[base + token]
                gv = gp * kc_t[base + token]
                gk_t[base + token] = gk
                gv_t[base + token] = gv
                sums.add(1, gk, k_w.back(token, taps))
                sums.add(2, gv, v_w.back(token, taps))
            sums.store(sums_ref, lanes)
            return carry

        lax.fori_loop(0, count, products, 0)

        @pl.when(column == 0)
        def _():
            fetch.wait()

        lax.fori_loop(0, count, forward, 0)
        lax.fori_loop(0, count, backward, 0)
        for ref, work, (first, last, tail) in zip(held_refs, work_refs, held_tokens(reach)):
            for token in (*range(first, last), *range(length - tail, length)):
                row = token - first if token < last else token - length + last - first + tail
                target = Tokens(ref, repeats, 0, (column,))
                target[row] = Tokens(work, repeats, PAD)[token]
        return carry

    lax.fori_loop(0, groups // LANES, column_step, 0)


def interior(features, cotangent, weights):
    length, channels = cotangent.shape
    taps, banks, groups = weights.shape
    repeats = channels // groups
    columns = groups // LANES
    work = length * channels * taps * 2
    grad = jax.ShapeDtypeStruct((columns, length * repeats, LANES), F32)
    held = [
        jax.ShapeDtypeStruct((columns, (last - first + tail) * repeats, LANES), F32)
        for first, last, tail in held_tokens(taps - 1)
    ]
    work_shape = ((length + 2 * PAD) * repeats, LANES)
    mixed, gq, gk, gv, *arrays, sums = pl.pallas_call(
        functools.partial(interior_kernel, taps, repeats),
        out_shape=(
            jax.ShapeDtypeStruct(cotangent.shape, cotangent.dtype),
            *[grad] * 3,
            *held,
            jax.ShapeDtypeStruct((banks, taps, repeats, groups), F32),
        ),
        in_specs=[VMEM_SPEC, pl.BlockSpec(memory_space=pltpu.HBM), VMEM_SPEC],
        out_specs=(VMEM_SPEC,) * 13,
        scratch_shapes=[pltpu.VMEM(work_shape, F32) for _ in range(8)]
        + [
            pltpu.VMEM((CHUNK * repeats, LANES), F32),
            pltpu.VMEM(cotangent.shape, cotangent.dtype),
            pltpu.SemaphoreType.DMA,
        ],
        cost_estimate=pl.CostEstimate(
            flops=9 * work, bytes_accessed=22 * length * channels, transcendentals=0
        ),
        compiler_params=pltpu.CompilerParams(vmem_limit_bytes=VMEM_LIMIT),
        name="interior",
    )(features, pltpu.with_memory_space_constraint(cotangent, pltpu.HBM), weights)
    return mixed, (gq, gk, gv), arrays, sums


def stage_halo(load, n_s, view, repeats, groups, column, rows):
    for repeat in range(repeats):
        n_s[0:rows, :] = load(part_slice(repeat, groups, column)).astype(F32)
        view.put(0, repeat, n_s[...])


def edge_kernel(
    taps,
    repeats,
    weights_ref,
    near_ref,
    far_ref,
    sums_in_ref,
    q_a,
    k_a,
    v_a,
    c_a,
    kc_a,
    vc_a,
    p_a,
    gm_a,
    mixed_ref,
    ghead_ref,
    gtail_ref,
    after_ref,
    sums_ref,
    acc,
    n_s,
    h_s,
    kc_s,
    vc_s,
    p_s,
    gm_s,
    m_s,
):
    reach = taps - 1
    groups = weights_ref.shape[2]
    acc[...] = sums_in_ref[...]
    even = is_even("ctx")
    h_t, m_t = Tokens(h_s, repeats), Tokens(m_s, repeats)
    kc_t, vc_t, p_t, gm_t = (Tokens(ref, repeats, PAD) for ref in (kc_s, vc_s, p_s, gm_s))

    def column_step(column, carry):
        lanes = lane_slice(column)
        wq, wk, wv, wm = (weight_rows(weights_ref, bank, lanes) for bank in range(4))
        q_t, k_t, v_t, c_t, kc_i, vc_i, p_i, gm_i = (
            Held(ref, repeats, column, span)
            for ref, span in zip(
                (q_a, k_a, v_a, c_a, kc_a, vc_a, p_a, gm_a), held_tokens(reach)
            )
        )
        sums = Sums(taps)

        def before(part):
            rows = slice(0, 5 * reach)
            return jnp.where(
                even, far_ref[rows, part].astype(F32), near_ref[rows, part].astype(F32)
            )

        def after(part):
            value = jnp.where(even, near_ref[:, part].astype(F32), far_ref[:, part].astype(F32))
            after_ref[:, part] = value.astype(after_ref.dtype)
            return value

        stage_halo(before, n_s, h_t, repeats, groups, column, 5 * reach)
        q_w = Window(lambda t: q_t[t] if t >= 0 else h_t[reach + t])
        k_w = Window(lambda t: k_t[t] if t >= 0 else h_t[3 * reach + t])
        v_w = Window(lambda t: v_t[t] if t >= 0 else h_t[5 * reach + t])
        gq_o, gk_o, gv_o = (Tokens(ghead_ref, repeats, 0, (bank, column)) for bank in range(3))
        for token in range(-reach, reach):
            kc = dot_taps(wk, k_w.back(token, taps))
            vc = dot_taps(wv, v_w.back(token, taps))
            p_t[token] = kc * vc
            if token >= 0:
                kc_t[token] = kc
                vc_t[token] = vc
        p_w = Window(lambda t: p_t[t] if t < reach else p_i[t])
        for token in range(CHUNK):
            up = c_t[token]
            sources = q_w.back(token, taps)
            products = p_w.back(token, taps)
            qc = dot_taps(wq, sources)
            mixer = dot_taps(wm, products)
            m_t[token] = qc * mixer
            if token < 2 * reach:
                gq = up * mixer
                gm = up * qc
                gm_t[token] = gm
                gq_o[token] = gq
                sums.add(0, gq, sources)
                sums.add(3, gm, products)
        gm_w = Window(lambda t: gm_t[t])
        for token in range(reach):
            gp = dot_taps(wm, gm_w.ahead(token, taps))
            gk = gp * vc_t[token]
            gv = gp * kc_t[token]
            gk_o[token] = gk
            gv_o[token] = gv
            sums.add(1, gk, k_w.back(token, taps))
            sums.add(2, gv, v_w.back(token, taps))
        for repeat in range(repeats):
            part = part_slice(repeat, groups, column)
            mixed_ref[:, part] = m_t.take(0, repeat, CHUNK).astype(mixed_ref.dtype)

        stage_halo(after, n_s, h_t, repeats, groups, column, 6 * reach)
        q_w = Window(lambda t: q_t[t] if t < 0 else h_t[t])
        gk_o, gv_o = (Tokens(gtail_ref, repeats, reach, (bank, column)) for bank in range(2))
        for token in range(reach):
            gm_t[token] = h_t[2 * reach + token] * dot_taps(wq, q_w.back(token, taps))
        gm_w = Window(lambda t: gm_i[t] if t < 0 else gm_t[t])
        k_w, v_w = (Window(lambda t, view=view: view[t]) for view in (k_t, v_t))
        for token in range(-reach, 0):
            gp = dot_taps(wm, gm_w.ahead(token, taps))
            gk = gp * vc_i[token]
            gv = gp * kc_i[token]
            gk_o[token] = gk
            gv_o[token] = gv
            sums.add(1, gk, k_w.back(token, taps))
            sums.add(2, gv, v_w.back(token, taps))
        sums.store(acc, lanes)
        return carry

    lax.fori_loop(0, groups // LANES, column_step, 0)
    for bank in range(sums_ref.shape[1]):
        sums_ref[:, bank, :] = jnp.sum(acc[bank], axis=1)


def edge(weights, near, far, sums, arrays):
    taps, banks, groups = weights.shape
    channels = near.shape[1]
    repeats = channels // groups
    columns = groups // LANES
    reach = taps - 1
    halo_rows = -(-6 * reach // 8) * 8
    return pl.pallas_call(
        functools.partial(edge_kernel, taps, repeats),
        out_shape=(
            jax.ShapeDtypeStruct((CHUNK, channels), near.dtype),
            jax.ShapeDtypeStruct((3, columns, 2 * reach * repeats, LANES), F32),
            jax.ShapeDtypeStruct((2, columns, reach * repeats, LANES), F32),
            jax.ShapeDtypeStruct(near.shape, near.dtype),
            jax.ShapeDtypeStruct((taps, banks, groups), F32),
        ),
        in_specs=[VMEM_SPEC] * 12,
        out_specs=(VMEM_SPEC,) * 5,
        scratch_shapes=[
            pltpu.VMEM(sums.shape, F32),
            pltpu.VMEM((halo_rows, LANES), F32),
            pltpu.VMEM((halo_rows * repeats, LANES), F32),
        ]
        + [pltpu.VMEM((2 * PAD * repeats, LANES), F32) for _ in range(4)]
        + [pltpu.VMEM((CHUNK * repeats, LANES), F32)],
        cost_estimate=pl.CostEstimate(
            flops=10**7, bytes_accessed=4 * 10**6, transcendentals=0
        ),
        compiler_params=pltpu.CompilerParams(vmem_limit_bytes=VMEM_LIMIT),
        name="edge",
    )(weights, near, far, sums, *arrays)


def grads_kernel(taps, repeats, first, steps, count, *refs):
    refs = list(refs)
    top, bottom = first == 0, first + steps == count

    def pop(number):
        taken, refs[:number] = refs[:number], []
        return taken

    weights_ref, gq, gk, gv, ghead, gtail = pop(6)
    if top:
        middle, head = pop(2)
    else:
        pop(1)
    if bottom:
        after_ref, *ahead_of = pop(5)
    out_hbm, zero_ref = pop(2)
    copies = []
    out_s, o_s, sems = refs[-3:]
    reach = taps - 1
    groups = weights_ref.shape[2]
    columns = groups // LANES
    length = gq.shape[1] // repeats
    zero_ref[...] = jnp.zeros_like(zero_ref)
    if top:
        (mixed_hbm,) = pop(1)
        copies = [
            pltpu.make_async_copy(head, mixed_hbm.at[:CHUNK, :], sems.at[steps]),
            pltpu.make_async_copy(
                middle.at[CHUNK:, :], mixed_hbm.at[CHUNK:, :], sems.at[steps + 1]
            ),
        ]
        for copy in copies:
            copy.start()

    def load(bank, column, token):
        if token >= length:
            return Tokens(refs[0], repeats, 0, (bank, column))[token - length]
        if token < (reach if bank else 2 * reach):
            return Tokens(ghead, repeats, 0, (bank, column))[token]
        if bank and token >= length - reach:
            return Tokens(gtail, repeats, reach - length, (bank - 1, column))[token]
        return Tokens((gq, gk, gv)[bank], repeats, 0, (column,))[token]

    def next_shard(column, carry):
        gnext, n_s, h_s, p_s, gm_s = refs[:5]
        lanes = lane_slice(column)
        wq, wk, wv, wm = (weight_rows(weights_ref, bank, lanes) for bank in range(4))
        h_t, p_t, gm_t = (Tokens(ref, repeats) for ref in (h_s, p_s, gm_s))
        q_t, k_t, v_t, p_i = (
            Held(ref, repeats, column, held_tokens(reach)[which])
            for ref, which in zip(ahead_of, (0, 1, 2, 6))
        )
        stage_halo(lambda part: after_ref[:, part], n_s, h_t, repeats, groups, column, 6 * reach)
        q_w = Window(lambda t: q_t[t] if t < 0 else h_t[t])
        k_w = Window(lambda t: k_t[t] if t < 0 else h_t[4 * reach + t])
        v_w = Window(lambda t: v_t[t] if t < 0 else h_t[5 * reach + t])
        p_w = Window(lambda t: p_i[t] if t < 0 else p_t[t])
        gm_w = Window(lambda t: gm_t[t])
        next_q, next_k, next_v = (
            Tokens(gnext, repeats, 0, (bank, column)) for bank in range(3)
        )
        for token in range(2 * reach):
            gm_t[token] = h_t[2 * reach + token] * dot_taps(wq, q_w.back(token, taps))
        for token in range(reach):
            kc = dot_taps(wk, k_w.back(token, taps))
            vc = dot_taps(wv, v_w.back(token, taps))
            p_t[token] = kc * vc
            gp = dot_taps(wm, gm_w.ahead(token, taps))
            next_k[token] = gp * vc
            next_v[token] = gp * kc
            next_q[token] = h_t[2 * reach + token] * dot_taps(wm, p_w.back(token, taps))
        return carry

    def out_copy(slot):
        rows = slice((first + slot) * CHUNK, (first + slot + 1) * CHUNK)
        return pltpu.make_async_copy(out_s.at[slot], out_hbm.at[:, rows, :], sems.at[slot])

    if bottom:
        lax.fori_loop(0, columns, next_shard, 0)
    for slot in range(steps):
        base = (first + slot) * CHUNK

        def column_step(column, carry):
            lanes = lane_slice(column)
            o_t = Tokens(o_s, repeats)
            for bank in range(3):
                weights = weight_rows(weights_ref, bank, lanes)
                window = Window(lambda t: load(bank, column, base + t))
                for token in range(CHUNK):
                    o_t[token] = dot_taps(weights, window.ahead(token, taps))
                for repeat in range(repeats):
                    part = part_slice(repeat, groups, column)
                    out_s[slot, bank, :, part] = o_t.take(0, repeat, CHUNK).astype(out_s.dtype)
            return carry

        lax.fori_loop(0, columns, column_step, 0)
        out_copy(slot).start()
    for slot in range(steps):
        out_copy(slot).wait()
    for copy in copies:
        copy.wait()


def feature_gradients(
    piece, pieces, features, weights, grads, ghead, gtail, mixed, after, arrays, earlier, zero
):
    banks, length, channels = features.shape
    taps, _, groups = weights.shape
    repeats = channels // groups
    columns = groups // LANES
    reach = taps - 1
    count = length // CHUNK
    steps = count // pieces
    first = piece * steps
    operands = [weights, *grads, ghead, gtail]
    in_specs = [VMEM_SPEC] * len(operands)
    out_shape = [jax.ShapeDtypeStruct(features.shape, features.dtype), zero]
    out_specs = [ANY_SPEC, VMEM_SPEC]
    aliases = {}
    scratch = []
    if piece == 0:
        operands += mixed
        in_specs += [VMEM_SPEC] * 2
        out_shape.append(jax.ShapeDtypeStruct(mixed[0].shape, mixed[0].dtype))
        out_specs.append(ANY_SPEC)
    else:
        aliases = {len(operands): 0}
        operands.append(earlier)
        in_specs.append(ANY_SPEC)
    if piece == pieces - 1:
        q_a, k_a, v_a, _, _, _, p_a, _ = arrays
        operands += [after, q_a, k_a, v_a, p_a]
        in_specs += [VMEM_SPEC] * 5
        halo_rows = -(-after.shape[0] // 8) * 8
        scratch = [
            pltpu.VMEM((3, columns, reach * repeats, LANES), F32),
            pltpu.VMEM((halo_rows, LANES), F32),
            pltpu.VMEM((halo_rows * repeats, LANES), F32),
            pltpu.VMEM((reach * repeats, LANES), F32),
            pltpu.VMEM((2 * reach * repeats, LANES), F32),
        ]
    work = length * channels * taps * 2 // pieces
    return pl.pallas_call(
        functools.partial(grads_kernel, taps, repeats, first, steps, count),
        out_shape=out_shape,
        in_specs=in_specs,
        out_specs=out_specs,
        scratch_shapes=scratch
        + [
            pltpu.VMEM((steps, banks, CHUNK, channels), features.dtype),
            pltpu.VMEM((CHUNK * repeats, LANES), F32),
            pltpu.SemaphoreType.DMA((steps + 2,)),
        ],
        input_output_aliases=aliases,
        cost_estimate=pl.CostEstimate(
            flops=4 * work,
            bytes_accessed=18 * length * channels // pieces,
            transcendentals=0,
        ),
        compiler_params=pltpu.CompilerParams(vmem_limit_bytes=VMEM_LIMIT),
        name="feature_gradients",
    )(*operands)


def per_device(features, cotangent, master_filters):
    length = features.shape[1]
    near, far, rounded = pack(features, cotangent, jnp.transpose(master_filters, (1, 0, 2)))
    weights = gather_filters(rounded, "fsdp").astype(F32)
    halos = swap_pairs(near, far, "ctx")
    middle, grads, arrays, sums = interior(features, cotangent, weights)
    top, ghead, gtail, after, sums = edge(weights, *halos, sums, arrays)
    repeats = features.shape[2] // weights.shape[2]
    pieces = PIECES if (length // CHUNK) % PIECES == 0 else 1
    owned = sum_scatter(sums, "fsdp")
    made = {"grads": None}

    def beside(piece):
        if piece >= pieces:
            return 0.0
        made["grads"], zero, *rest = feature_gradients(
            piece,
            pieces,
            features,
            weights,
            grads,
            ghead,
            gtail,
            (middle, top),
            after,
            arrays,
            made["grads"],
            jax.ShapeDtypeStruct(owned.shape, F32),
        )
        if rest:
            made["mixed"] = rest[0]
        return zero

    summed, done = sum_over(owned, "ctx", beside)
    for piece in range(done, pieces):
        beside(piece)
    count_all = length * lax.axis_size("ctx") * repeats * lax.axis_size("fsdp")
    filter_grads = jnp.transpose(summed * (1.0 / math.sqrt(count_all)), (1, 0, 2))
    return (made["mixed"], made["grads"], filter_grads)


def solution(mesh):
    return jax.shard_map(
        per_device,
        mesh=mesh,
        in_specs=(P(None, "ctx", "fsdp"), P("ctx", "fsdp"), P(None, None, "fsdp")),
        out_specs=(P("ctx", "fsdp"), P(None, "ctx", "fsdp"), P(None, None, "fsdp")),
        check_vma=False,
    )
```

```python
import functools
import math

import jax
import jax.numpy as jnp
from jax import lax
from jax.experimental import pallas as pl
from jax.experimental.pallas import tpu as pltpu
from jax.sharding import PartitionSpec as P

LANES = 128
CHUNK = 16
PAD = 16
PIECES = 4
VMEM_LIMIT = 12 * 1024 * 1024
PACK_LIMIT = 16 * 1024 * 1024
F32 = jnp.float32
VMEM_SPEC = pl.BlockSpec(memory_space=pltpu.VMEM)
ANY_SPEC = pl.BlockSpec(memory_space=pl.ANY)


def swap_pairs(near, far, axis):
    size = lax.axis_size(axis)
    inner = [(i, i ^ 1) for i in range(size) if i ^ 1 < size]
    outer = [(i, i - 1 if i % 2 == 0 else i + 1) for i in range(size)]
    outer = [(i, j) for i, j in outer if 0 <= j < size]
    far = lax.ppermute(far, axis, outer)
    near = lax.ppermute(near, axis, inner)
    return near, far


def is_even(axis):
    return lax.rem(lax.axis_index(axis), 2) == 0


def gather_filters(shard, axis):
    size = lax.axis_size(axis)
    if size != 2:
        return lax.all_gather(shard, axis, axis=2, tiled=True)
    other = lax.ppermute(shard, axis, [(0, 1), (1, 0)])
    first = lax.axis_index(axis) == 0
    return jnp.concatenate(
        [jnp.where(first, shard, other), jnp.where(first, other, shard)], axis=2
    )


def sum_over(value, axis, beside=None):
    size = lax.axis_size(axis)
    if size & (size - 1):
        return lax.psum(value, axis), 0
    rounds = size.bit_length() - 1
    for step in range(rounds):
        pairs = [(i, i ^ (1 << step)) for i in range(size)]
        received = lax.ppermute(value, axis, pairs)
        value = value + received
        if beside is not None:
            value = value + beside(step)
    return value, rounds


def sum_scatter(value, axis):
    size = lax.axis_size(axis)
    portion = value.shape[-1] // size
    if size != 2:
        total, _ = sum_over(value, axis)
        return lax.dynamic_slice_in_dim(
            total, lax.axis_index(axis) * portion, portion, value.ndim - 1
        )
    first = lax.axis_index(axis) == 0
    low, high = value[..., :portion], value[..., portion:]
    sent = lax.ppermute(jnp.where(first, high, low), axis, [(0, 1), (1, 0)])
    return jnp.where(first, low, high) + sent


def dot_taps(weights, pieces):
    total = weights[0] * pieces[0]
    for weight, piece in zip(weights[1:], pieces[1:]):
        total = total + weight * piece
    return total


def weight_rows(ref, bank, lanes):
    return [ref[lag, pl.ds(bank, 1), lanes] for lag in range(ref.shape[0])]


def lane_slice(index):
    return pl.ds(pl.multiple_of(index * LANES, LANES), LANES)


def part_slice(repeat, groups, column):
    return pl.ds(pl.multiple_of(repeat * groups + column * LANES, LANES), LANES)


class Tokens:
    def __init__(self, ref, repeats, origin=0, lead=()):
        self.ref, self.repeats, self.origin, self.lead = ref, repeats, origin, lead

    def rows(self, token, count=1):
        start = (self.origin + token) * self.repeats
        if not isinstance(start, int):
            start = pl.multiple_of(start, self.repeats)
        return pl.ds(start, count * self.repeats)

    def __getitem__(self, token):
        return self.ref[(*self.lead, self.rows(token), slice(None))]

    def __setitem__(self, token, value):
        self.ref[(*self.lead, self.rows(token), slice(None))] = value

    def strided(self, token, repeat, count):
        start = (self.origin + token) * self.repeats + repeat
        return pl.ds(start, count, stride=self.repeats)

    def put(self, token, repeat, value):
        rows = self.strided(token, repeat, value.shape[0])
        self.ref[(*self.lead, rows, slice(None))] = value

    def take(self, token, repeat, count):
        return self.ref[(*self.lead, self.strided(token, repeat, count), slice(None))]


class Halo:
    def __init__(self, ref, repeats, columns):
        self.ref, self.repeats, self.columns = ref, repeats, columns

    def put(self, token, column, repeat, value):
        start = (token * self.columns + column) * self.repeats + repeat
        rows = pl.ds(start, value.shape[0], stride=self.columns * self.repeats)
        self.ref[rows, :] = value

    def tokens(self, column):
        class View:
            def __getitem__(_, token):
                start = (token * self.columns + column) * self.repeats
                if not isinstance(start, int):
                    start = pl.multiple_of(start, self.repeats)
                return self.ref[pl.ds(start, self.repeats), :]

        return View()


def held_tokens(reach):
    wide = 2 * reach
    return (
        (0, CHUNK, reach),
        (0, reach, wide),
        (0, reach, wide),
        (0, CHUNK, 0),
        (0, 0, reach),
        (0, 0, reach),
        (reach, CHUNK, reach),
        (0, 0, reach),
    )


class Held:
    def __init__(self, ref, repeats, column, span):
        self.first, self.last, self.tail = span
        self.view = Tokens(ref, repeats, 0, (column,))

    def __getitem__(self, token):
        if token < 0:
            return self.view[self.last - self.first + self.tail + token]
        return self.view[token - self.first]


class Window:
    def __init__(self, load):
        self.load, self.held = load, {}

    def __call__(self, token):
        if token not in self.held:
            self.held[token] = self.load(token)
        return self.held[token]

    def back(self, token, taps):
        return [self(token - lag) for lag in range(taps)]

    def ahead(self, token, taps):
        return [self(token + lag) for lag in range(taps)]


class Sums:
    def __init__(self, taps):
        self.taps = taps
        self.held = {}

    def add(self, bank, grad, pieces):
        for lag, piece in enumerate(pieces):
            term = grad * piece
            old = self.held.get((bank, lag))
            self.held[bank, lag] = term if old is None else old + term

    def store(self, ref, lanes):
        for (bank, lag), value in self.held.items():
            ref[bank, lag, :, lanes] += value


def pack_kernel(
    reach,
    columns,
    features_hbm,
    cotangent_hbm,
    master_hbm,
    near_ref,
    far_ref,
    rounded_ref,
    tail,
    head,
    upstream,
    master,
    b_s,
    a_s,
    sems,
):
    length = cotangent_hbm.shape[0]
    copies = [
        pltpu.make_async_copy(master_hbm, master, sems.at[3]),
        pltpu.make_async_copy(features_hbm.at[:, length - PAD :, :], tail, sems.at[0]),
        pltpu.make_async_copy(features_hbm.at[:, :PAD, :], head, sems.at[1]),
        pltpu.make_async_copy(cotangent_hbm.at[:PAD, :], upstream, sems.at[2]),
    ]
    for copy in copies:
        copy.start()
    even = is_even("ctx")
    repeats = upstream.shape[1] // (columns * LANES)
    block = reach * columns * repeats
    b_s[-block:, :] = jnp.zeros((block, LANES), F32)
    last, first = Halo(b_s, repeats, columns), Halo(a_s, repeats, columns)
    for copy in copies:
        copy.wait()
    rounded_ref[...] = master[...].astype(rounded_ref.dtype)
    wide = 2 * reach

    def repeat_step(repeat, carry):
        for column in range(columns):
            lanes = lane_slice(repeat * columns + column)

            def put(message, token, ref, start, stop):
                value = ref[:, lanes].astype(F32)[start:stop]
                message.put(token, column, repeat, value)

            put(last, 0, tail.at[0], PAD - reach, PAD)
            put(last, reach, tail.at[1], PAD - wide, PAD)
            put(last, 3 * reach, tail.at[2], PAD - wide, PAD)
            put(first, 0, head.at[0], 0, wide)
            put(first, wide, upstream, 0, wide)
            put(first, 2 * wide, head.at[1], 0, reach)
            put(first, 5 * reach, head.at[2], 0, reach)
        return carry

    lax.fori_loop(0, repeats, repeat_step, 0)
    ending, opening = b_s[...], a_s[...]
    near_ref[...] = jnp.where(even, ending, opening).astype(near_ref.dtype)
    far_ref[...] = jnp.where(even, opening, ending).astype(far_ref.dtype)


def pack(features, cotangent, master, groups):
    reach = master.shape[0] - 1
    banks, length, channels = features.shape
    kind = features.dtype
    hbm = [
        pltpu.with_memory_space_constraint(value, pltpu.HBM)
        for value in (features, cotangent, master)
    ]
    message = jax.ShapeDtypeStruct((6 * reach * channels // LANES, LANES), kind)
    return pl.pallas_call(
        functools.partial(pack_kernel, reach, groups // LANES),
        out_shape=(message, message, jax.ShapeDtypeStruct(master.shape, jnp.bfloat16)),
        in_specs=[pl.BlockSpec(memory_space=pltpu.HBM)] * 3,
        out_specs=(VMEM_SPEC,) * 3,
        scratch_shapes=[
            pltpu.VMEM((banks, PAD, channels), kind),
            pltpu.VMEM((banks, PAD, channels), kind),
            pltpu.VMEM((PAD, channels), kind),
            pltpu.VMEM(master.shape, F32),
            pltpu.VMEM(message.shape, F32),
            pltpu.VMEM(message.shape, F32),
            pltpu.SemaphoreType.DMA((4,)),
        ],
        cost_estimate=pl.CostEstimate(flops=10**6, bytes_accessed=10**6, transcendentals=0),
        compiler_params=pltpu.CompilerParams(vmem_limit_bytes=PACK_LIMIT),
        name="pack_halos",
    )(*hbm)


def interior_kernel(
    taps,
    repeats,
    features_ref,
    cotangent_hbm,
    weights_ref,
    mixed_ref,
    gq_ref,
    gk_ref,
    gv_ref,
    *refs,
):
    *held_refs, sums_ref = refs[:9]
    *work_refs, m_s, cotangent_ref, sem = refs[9:]
    *work_refs, k_other, v_other = work_refs
    q_s, k_s, v_s, c_s, kc_s, vc_s, p_s, gm_s = work_refs
    pairs = ((k_s, v_s), (k_other, v_other))
    reach = taps - 1
    groups = weights_ref.shape[2]
    length = cotangent_ref.shape[0]
    count = length // CHUNK
    fetch = pltpu.make_async_copy(cotangent_hbm, cotangent_ref, sem)
    fetch.start()
    sums_ref[...] = jnp.zeros_like(sums_ref)
    m_t = Tokens(m_s, repeats)

    def part_of(repeat, column):
        first = repeat * groups + column * LANES
        return slice(first, first + LANES)

    zero = jnp.zeros((reach * repeats, LANES), F32)
    for ref in (q_s, p_s, k_s, v_s, k_other, v_other):
        ref[(PAD - reach) * repeats : PAD * repeats, :] = zero
    gm_s[(PAD + length) * repeats : (PAD + length + reach) * repeats, :] = zero
    q_t, c_t, kc_t, vc_t, p_t, gm_t = (
        Tokens(ref, repeats, PAD) for ref in (q_s, c_s, kc_s, vc_s, p_s, gm_s)
    )
    columns = groups // LANES

    def put_pair(column, base, rows):
        for bank, ref in enumerate(pairs[column % 2]):
            view = Tokens(ref, repeats, PAD)
            for repeat in range(repeats):
                part = part_of(repeat, column)
                view.put(base, repeat, features_ref[1 + bank, rows, part].astype(F32))

    def chunks(body):
        def step_body(step, carry):
            base = pl.multiple_of(step * CHUNK, CHUNK)
            body(step, base, pl.ds(base, CHUNK))
            return carry

        lax.fori_loop(0, count, step_body, 0)

    chunks(lambda step, base, rows: put_pair(0, base, rows))
    for column in range(columns):
        lanes = slice(column * LANES, (column + 1) * LANES)
        gq_t, gk_t, gv_t = (
            Tokens(ref, repeats, 0, (column,)) for ref in (gq_ref, gk_ref, gv_ref)
        )
        k_t, v_t = (Tokens(ref, repeats, PAD) for ref in pairs[column % 2])
        wq, wk, wv, wm = (weight_rows(weights_ref, bank, lanes) for bank in range(4))

        def products(step, base, rows):
            for repeat in range(repeats):
                part = part_of(repeat, column)
                q_t.put(base, repeat, features_ref[0, rows, part].astype(F32))
            k_w, v_w = (Window(lambda t, view=view: view[base + t]) for view in (k_t, v_t))
            for token in range(CHUNK):
                kc = dot_taps(wk, k_w.back(token, taps))
                vc = dot_taps(wv, v_w.back(token, taps))
                kc_t[base + token] = kc
                vc_t[base + token] = vc
                p_t[base + token] = kc * vc

        def forward(step, base, rows):
            for repeat in range(repeats):
                part = part_of(repeat, column)
                c_t.put(base, repeat, cotangent_ref[rows, part].astype(F32))
            if column + 1 < columns:
                put_pair(column + 1, base, rows)
            sums = Sums(taps)
            q_w, p_w = (Window(lambda t, view=view: view[base + t]) for view in (q_t, p_t))
            for token in range(CHUNK):
                up = c_t[base + token]
                sources = q_w.back(token, taps)
                inner = p_w.back(token, taps)
                qc = dot_taps(wq, sources)
                mixer = dot_taps(wm, inner)
                gq = up * mixer
                gm = up * qc
                m_t[token] = qc * mixer
                gm_t[base + token] = gm
                gq_t[base + token] = gq
                if token < 2 * reach:
                    gq = jnp.where(step > 0, gq, 0.0)
                    gm = jnp.where(step > 0, gm, 0.0)
                sums.add(0, gq, sources)
                sums.add(3, gm, inner)
            sums.store(sums_ref, lanes)
            for repeat in range(repeats):
                part = part_of(repeat, column)
                mixed_ref[rows, part] = m_t.take(0, repeat, CHUNK).astype(mixed_ref.dtype)

        def backward(step, base, rows):
            k_w, v_w, gm_w = (
                Window(lambda t, view=view: view[base + t]) for view in (k_t, v_t, gm_t)
            )
            sums = Sums(taps)
            for token in range(CHUNK):
                gp = dot_taps(wm, gm_w.ahead(token, taps))
                if token < reach:
                    gp = jnp.where(step > 0, gp, 0.0)
                if token >= CHUNK - reach:
                    gp = jnp.where(step < count - 1, gp, 0.0)
                gk = gp * vc_t[base + token]
                gv = gp * kc_t[base + token]
                gk_t[base + token] = gk
                gv_t[base + token] = gv
                sums.add(1, gk, k_w.back(token, taps))
                sums.add(2, gv, v_w.back(token, taps))
            sums.store(sums_ref, lanes)

        chunks(products)
        if column == 0:
            fetch.wait()
        chunks(forward)
        chunks(backward)
        sources = (q_s, *pairs[column % 2], c_s, kc_s, vc_s, p_s, gm_s)
        for ref, work, (first, last, tail) in zip(held_refs, sources, held_tokens(reach)):
            target, source = Tokens(ref, repeats, 0, (column,)), Tokens(work, repeats, PAD)
            for token in (*range(first, last), *range(length - tail, length)):
                row = token - first if token < last else token - length + last - first + tail
                target[row] = source[token]


def interior(features, cotangent, weights):
    length, channels = cotangent.shape
    taps, banks, groups = weights.shape
    repeats = channels // groups
    columns = groups // LANES
    work = length * channels * taps * 2
    grad = jax.ShapeDtypeStruct((columns, length * repeats, LANES), F32)
    held = [
        jax.ShapeDtypeStruct((columns, (last - first + tail) * repeats, LANES), F32)
        for first, last, tail in held_tokens(taps - 1)
    ]
    work_shape = ((length + 2 * PAD) * repeats, LANES)
    mixed, gq, gk, gv, *arrays, sums = pl.pallas_call(
        functools.partial(interior_kernel, taps, repeats),
        out_shape=(
            jax.ShapeDtypeStruct(cotangent.shape, cotangent.dtype),
            *[grad] * 3,
            *held,
            jax.ShapeDtypeStruct((banks, taps, repeats, groups), F32),
        ),
        in_specs=[VMEM_SPEC, pl.BlockSpec(memory_space=pltpu.HBM), VMEM_SPEC],
        out_specs=(VMEM_SPEC,) * 13,
        scratch_shapes=[pltpu.VMEM(work_shape, F32) for _ in range(10)]
        + [
            pltpu.VMEM((CHUNK * repeats, LANES), F32),
            pltpu.VMEM(cotangent.shape, cotangent.dtype),
            pltpu.SemaphoreType.DMA,
        ],
        cost_estimate=pl.CostEstimate(
            flops=9 * work, bytes_accessed=22 * length * channels, transcendentals=0
        ),
        compiler_params=pltpu.CompilerParams(vmem_limit_bytes=VMEM_LIMIT),
        name="interior",
    )(features, pltpu.with_memory_space_constraint(cotangent, pltpu.HBM), weights)
    return mixed, (gq, gk, gv), arrays, sums


def edge_kernel(
    taps,
    repeats,
    weights_ref,
    near_ref,
    far_ref,
    sums_in_ref,
    q_a,
    k_a,
    v_a,
    c_a,
    kc_a,
    vc_a,
    p_a,
    gm_a,
    mixed_ref,
    ghead_ref,
    gtail_ref,
    after_ref,
    sums_ref,
    acc,
    before_s,
    kc_s,
    vc_s,
    p_s,
    gm_s,
    m_s,
):
    reach = taps - 1
    groups = weights_ref.shape[2]
    acc[...] = sums_in_ref[...]
    even = is_even("ctx")
    columns = groups // LANES
    near, far = near_ref[...].astype(F32), far_ref[...].astype(F32)
    before_s[...] = jnp.where(even, far, near)
    after_ref[...] = jnp.where(even, near, far)
    m_t = Tokens(m_s, repeats)
    kc_t, vc_t, p_t, gm_t = (Tokens(ref, repeats, PAD) for ref in (kc_s, vc_s, p_s, gm_s))

    def column_step(column, carry):
        lanes = lane_slice(column)
        wq, wk, wv, wm = (weight_rows(weights_ref, bank, lanes) for bank in range(4))
        q_t, k_t, v_t, c_t, kc_i, vc_i, p_i, gm_i = (
            Held(ref, repeats, column, span)
            for ref, span in zip(
                (q_a, k_a, v_a, c_a, kc_a, vc_a, p_a, gm_a), held_tokens(reach)
            )
        )
        sums = Sums(taps)

        h_t = Halo(before_s, repeats, columns).tokens(column)
        q_w = Window(lambda t: q_t[t] if t >= 0 else h_t[reach + t])
        k_w = Window(lambda t: k_t[t] if t >= 0 else h_t[3 * reach + t])
        v_w = Window(lambda t: v_t[t] if t >= 0 else h_t[5 * reach + t])
        gq_o, gk_o, gv_o = (Tokens(ghead_ref, repeats, 0, (bank, column)) for bank in range(3))
        for token in range(-reach, reach):
            kc = dot_taps(wk, k_w.back(token, taps))
            vc = dot_taps(wv, v_w.back(token, taps))
            p_t[token] = kc * vc
            if token >= 0:
                kc_t[token] = kc
                vc_t[token] = vc
        p_w = Window(lambda t: p_t[t] if t < reach else p_i[t])
        for token in range(CHUNK):
            up = c_t[token]
            sources = q_w.back(token, taps)
            products = p_w.back(token, taps)
            qc = dot_taps(wq, sources)
            mixer = dot_taps(wm, products)
            m_t[token] = qc * mixer
            if token < 2 * reach:
                gq = up * mixer
                gm = up * qc
                gm_t[token] = gm
                gq_o[token] = gq
                sums.add(0, gq, sources)
                sums.add(3, gm, products)
        gm_w = Window(lambda t: gm_t[t])
        for token in range(reach):
            gp = dot_taps(wm, gm_w.ahead(token, taps))
            gk = gp * vc_t[token]
            gv = gp * kc_t[token]
            gk_o[token] = gk
            gv_o[token] = gv
            sums.add(1, gk, k_w.back(token, taps))
            sums.add(2, gv, v_w.back(token, taps))
        for repeat in range(repeats):
            part = part_slice(repeat, groups, column)
            mixed_ref[:, part] = m_t.take(0, repeat, CHUNK).astype(mixed_ref.dtype)

        n_t = Halo(after_ref, repeats, columns).tokens(column)
        q_w = Window(lambda t: q_t[t] if t < 0 else n_t[t])
        gk_o, gv_o = (Tokens(gtail_ref, repeats, reach, (bank, column)) for bank in range(2))
        for token in range(reach):
            gm_t[token] = n_t[2 * reach + token] * dot_taps(wq, q_w.back(token, taps))
        gm_w = Window(lambda t: gm_i[t] if t < 0 else gm_t[t])
        k_w, v_w = (Window(lambda t, view=view: view[t]) for view in (k_t, v_t))
        for token in range(-reach, 0):
            gp = dot_taps(wm, gm_w.ahead(token, taps))
            gk = gp * vc_i[token]
            gv = gp * kc_i[token]
            gk_o[token] = gk
            gv_o[token] = gv
            sums.add(1, gk, k_w.back(token, taps))
            sums.add(2, gv, v_w.back(token, taps))
        sums.store(acc, lanes)
        return carry

    lax.fori_loop(0, groups // LANES, column_step, 0)
    for bank in range(sums_ref.shape[1]):
        sums_ref[:, bank, :] = jnp.sum(acc[bank], axis=1)


def edge(weights, near, far, sums, arrays):
    taps, banks, groups = weights.shape
    columns = groups // LANES
    reach = taps - 1
    repeats = near.shape[0] // (6 * reach * columns)
    channels = repeats * groups
    return pl.pallas_call(
        functools.partial(edge_kernel, taps, repeats),
        out_shape=(
            jax.ShapeDtypeStruct((CHUNK, channels), near.dtype),
            jax.ShapeDtypeStruct((3, columns, 2 * reach * repeats, LANES), F32),
            jax.ShapeDtypeStruct((2, columns, reach * repeats, LANES), F32),
            jax.ShapeDtypeStruct(near.shape, F32),
            jax.ShapeDtypeStruct((taps, banks, groups), F32),
        ),
        in_specs=[VMEM_SPEC] * 12,
        out_specs=(VMEM_SPEC,) * 5,
        scratch_shapes=[
            pltpu.VMEM(sums.shape, F32),
            pltpu.VMEM(near.shape, F32),
        ]
        + [pltpu.VMEM((2 * PAD * repeats, LANES), F32) for _ in range(4)]
        + [pltpu.VMEM((CHUNK * repeats, LANES), F32)],
        cost_estimate=pl.CostEstimate(
            flops=10**7, bytes_accessed=4 * 10**6, transcendentals=0
        ),
        compiler_params=pltpu.CompilerParams(vmem_limit_bytes=VMEM_LIMIT),
        name="edge",
    )(weights, near, far, sums, *arrays)


def grads_kernel(taps, repeats, first, steps, count, *refs):
    refs = list(refs)
    top, bottom = first == 0, first + steps == count

    def pop(number):
        taken, refs[:number] = refs[:number], []
        return taken

    weights_ref, gq, gk, gv, ghead, gtail = pop(6)
    if top:
        middle, head = pop(2)
    else:
        pop(1)
    if bottom:
        after_ref, *ahead_of = pop(5)
    out_hbm, zero_ref = pop(2)
    copies = []
    out_s, o_s, sems = refs[-3:]
    reach = taps - 1
    groups = weights_ref.shape[2]
    columns = groups // LANES
    length = gq.shape[1] // repeats
    zero_ref[...] = jnp.zeros_like(zero_ref)
    if top:
        (mixed_hbm,) = pop(1)
        copies = [
            pltpu.make_async_copy(head, mixed_hbm.at[:CHUNK, :], sems.at[steps]),
            pltpu.make_async_copy(
                middle.at[CHUNK:, :], mixed_hbm.at[CHUNK:, :], sems.at[steps + 1]
            ),
        ]
        for copy in copies:
            copy.start()

    def load(bank, column, token):
        if token >= length:
            return Tokens(refs[0], repeats, 0, (bank, column))[token - length]
        if token < (reach if bank else 2 * reach):
            return Tokens(ghead, repeats, 0, (bank, column))[token]
        if bank and token >= length - reach:
            return Tokens(gtail, repeats, reach - length, (bank - 1, column))[token]
        return Tokens((gq, gk, gv)[bank], repeats, 0, (column,))[token]

    def next_shard(column, carry):
        gnext, p_s, gm_s = refs[:3]
        lanes = lane_slice(column)
        wq, wk, wv, wm = (weight_rows(weights_ref, bank, lanes) for bank in range(4))
        p_t, gm_t = (Tokens(ref, repeats) for ref in (p_s, gm_s))
        h_t = Halo(after_ref, repeats, columns).tokens(column)
        q_t, k_t, v_t, p_i = (
            Held(ref, repeats, column, held_tokens(reach)[which])
            for ref, which in zip(ahead_of, (0, 1, 2, 6))
        )
        q_w = Window(lambda t: q_t[t] if t < 0 else h_t[t])
        k_w = Window(lambda t: k_t[t] if t < 0 else h_t[4 * reach + t])
        v_w = Window(lambda t: v_t[t] if t < 0 else h_t[5 * reach + t])
        p_w = Window(lambda t: p_i[t] if t < 0 else p_t[t])
        gm_w = Window(lambda t: gm_t[t])
        next_q, next_k, next_v = (
            Tokens(gnext, repeats, 0, (bank, column)) for bank in range(3)
        )
        for token in range(2 * reach):
            gm_t[token] = h_t[2 * reach + token] * dot_taps(wq, q_w.back(token, taps))
        for token in range(reach):
            kc = dot_taps(wk, k_w.back(token, taps))
            vc = dot_taps(wv, v_w.back(token, taps))
            p_t[token] = kc * vc
            gp = dot_taps(wm, gm_w.ahead(token, taps))
            next_k[token] = gp * vc
            next_v[token] = gp * kc
            next_q[token] = h_t[2 * reach + token] * dot_taps(wm, p_w.back(token, taps))
        return carry

    def out_copy(slot):
        rows = slice((first + slot) * CHUNK, (first + slot + 1) * CHUNK)
        return pltpu.make_async_copy(out_s.at[slot], out_hbm.at[:, rows, :], sems.at[slot])

    if bottom:
        lax.fori_loop(0, columns, next_shard, 0)
    for slot in range(steps):
        base = (first + slot) * CHUNK

        def column_step(column, carry):
            lanes = lane_slice(column)
            o_t = Tokens(o_s, repeats)
            for bank in range(3):
                weights = weight_rows(weights_ref, bank, lanes)
                window = Window(lambda t: load(bank, column, base + t))
                for token in range(CHUNK):
                    o_t[token] = dot_taps(weights, window.ahead(token, taps))
                for repeat in range(repeats):
                    part = part_slice(repeat, groups, column)
                    out_s[slot, bank, :, part] = o_t.take(0, repeat, CHUNK).astype(out_s.dtype)
            return carry

        lax.fori_loop(0, columns, column_step, 0)
        out_copy(slot).start()
    for slot in range(steps):
        out_copy(slot).wait()
    for copy in copies:
        copy.wait()


def feature_gradients(
    piece, pieces, features, weights, grads, ghead, gtail, mixed, after, arrays, earlier, zero
):
    banks, length, channels = features.shape
    taps, _, groups = weights.shape
    repeats = channels // groups
    columns = groups // LANES
    reach = taps - 1
    count = length // CHUNK
    steps = count // pieces
    first = piece * steps
    operands = [weights, *grads, ghead, gtail]
    in_specs = [VMEM_SPEC] * len(operands)
    out_shape = [jax.ShapeDtypeStruct(features.shape, features.dtype), zero]
    out_specs = [ANY_SPEC, VMEM_SPEC]
    aliases = {}
    scratch = []
    if piece == 0:
        operands += mixed
        in_specs += [VMEM_SPEC] * 2
        out_shape.append(jax.ShapeDtypeStruct(mixed[0].shape, mixed[0].dtype))
        out_specs.append(ANY_SPEC)
    else:
        aliases = {len(operands): 0}
        operands.append(earlier)
        in_specs.append(ANY_SPEC)
    if piece == pieces - 1:
        q_a, k_a, v_a, _, _, _, p_a, _ = arrays
        operands += [after, q_a, k_a, v_a, p_a]
        in_specs += [VMEM_SPEC] * 5
        scratch = [
            pltpu.VMEM((3, columns, reach * repeats, LANES), F32),
            pltpu.VMEM((reach * repeats, LANES), F32),
            pltpu.VMEM((2 * reach * repeats, LANES), F32),
        ]
    work = length * channels * taps * 2 // pieces
    return pl.pallas_call(
        functools.partial(grads_kernel, taps, repeats, first, steps, count),
        out_shape=out_shape,
        in_specs=in_specs,
        out_specs=out_specs,
        scratch_shapes=scratch
        + [
            pltpu.VMEM((steps, banks, CHUNK, channels), features.dtype),
            pltpu.VMEM((CHUNK * repeats, LANES), F32),
            pltpu.SemaphoreType.DMA((steps + 2,)),
        ],
        input_output_aliases=aliases,
        cost_estimate=pl.CostEstimate(
            flops=4 * work,
            bytes_accessed=18 * length * channels // pieces,
            transcendentals=0,
        ),
        compiler_params=pltpu.CompilerParams(vmem_limit_bytes=VMEM_LIMIT),
        name="feature_gradients",
    )(*operands)


def per_device(features, cotangent, master_filters):
    length = features.shape[1]
    near, far, rounded = pack(
        features,
        cotangent,
        jnp.transpose(master_filters, (1, 0, 2)),
        master_filters.shape[2] * lax.axis_size("fsdp"),
    )
    weights = gather_filters(rounded, "fsdp").astype(F32)
    halos = swap_pairs(near, far, "ctx")
    middle, grads, arrays, sums = interior(features, cotangent, weights)
    top, ghead, gtail, after, sums = edge(weights, *halos, sums, arrays)
    repeats = features.shape[2] // weights.shape[2]
    pieces = PIECES if (length // CHUNK) % PIECES == 0 else 1
    owned = sum_scatter(sums, "fsdp")
    made = {"grads": None}

    def beside(piece):
        if piece >= pieces:
            return 0.0
        made["grads"], zero, *rest = feature_gradients(
            piece,
            pieces,
            features,
            weights,
            grads,
            ghead,
            gtail,
            (middle, top),
            after,
            arrays,
            made["grads"],
            jax.ShapeDtypeStruct(owned.shape, F32),
        )
        if rest:
            made["mixed"] = rest[0]
        return zero

    summed, done = sum_over(owned, "ctx", beside)
    for piece in range(done, pieces):
        beside(piece)
    count_all = length * lax.axis_size("ctx") * repeats * lax.axis_size("fsdp")
    filter_grads = jnp.transpose(summed * (1.0 / math.sqrt(count_all)), (1, 0, 2))
    return (made["mixed"], made["grads"], filter_grads)


def solution(mesh):
    return jax.shard_map(
        per_device,
        mesh=mesh,
        in_specs=(P(None, "ctx", "fsdp"), P("ctx", "fsdp"), P(None, None, "fsdp")),
        out_specs=(P("ctx", "fsdp"), P(None, "ctx", "fsdp"), P(None, None, "fsdp")),
        check_vma=False,
    )
```

```python
import functools
import math

import jax
import jax.numpy as jnp
from jax import lax
from jax.experimental import pallas as pl
from jax.experimental.pallas import tpu as pltpu
from jax.sharding import PartitionSpec as P

LANES = 128
CHUNK = 16
PAD = 16
PIECES = 4
VMEM_LIMIT = 28 * 1024 * 1024
PACK_LIMIT = 16 * 1024 * 1024
F32 = jnp.float32
VMEM_SPEC = pl.BlockSpec(memory_space=pltpu.VMEM)
ANY_SPEC = pl.BlockSpec(memory_space=pl.ANY)


def swap_pairs(near, far, axis):
    size = lax.axis_size(axis)
    inner = [(i, i ^ 1) for i in range(size) if i ^ 1 < size]
    outer = [(i, i - 1 if i % 2 == 0 else i + 1) for i in range(size)]
    outer = [(i, j) for i, j in outer if 0 <= j < size]
    far = lax.ppermute(far, axis, outer)
    near = lax.ppermute(near, axis, inner)
    return near, far


def is_even(axis):
    return lax.rem(lax.axis_index(axis), 2) == 0


def gather_filters(shard, axis):
    size = lax.axis_size(axis)
    if size != 2:
        return lax.all_gather(shard, axis, axis=2, tiled=True)
    other = lax.ppermute(shard, axis, [(0, 1), (1, 0)])
    first = lax.axis_index(axis) == 0
    return jnp.concatenate(
        [jnp.where(first, shard, other), jnp.where(first, other, shard)], axis=2
    )


def sum_over(value, axis, beside=None):
    size = lax.axis_size(axis)
    if size & (size - 1):
        return lax.psum(value, axis), 0
    rounds = size.bit_length() - 1
    for step in range(rounds):
        pairs = [(i, i ^ (1 << step)) for i in range(size)]
        received = lax.ppermute(value, axis, pairs)
        value = value + received
        if beside is not None:
            value = value + beside(step)
    return value, rounds


def sum_scatter(value, axis):
    size = lax.axis_size(axis)
    portion = value.shape[-1] // size
    if size != 2:
        total, _ = sum_over(value, axis)
        return lax.dynamic_slice_in_dim(
            total, lax.axis_index(axis) * portion, portion, value.ndim - 1
        )
    first = lax.axis_index(axis) == 0
    low, high = value[..., :portion], value[..., portion:]
    sent = lax.ppermute(jnp.where(first, high, low), axis, [(0, 1), (1, 0)])
    return jnp.where(first, low, high) + sent


def dot_taps(weights, pieces):
    total = weights[0] * pieces[0]
    for weight, piece in zip(weights[1:], pieces[1:]):
        total = total + weight * piece
    return total


def weight_rows(ref, bank, lanes):
    return [ref[lag, pl.ds(bank, 1), lanes] for lag in range(ref.shape[0])]


def lane_slice(index):
    return pl.ds(pl.multiple_of(index * LANES, LANES), LANES)


def part_slice(repeat, groups, column):
    return pl.ds(pl.multiple_of(repeat * groups + column * LANES, LANES), LANES)


class Tokens:
    def __init__(self, ref, repeats, origin=0, lead=()):
        self.ref, self.repeats, self.origin, self.lead = ref, repeats, origin, lead

    def rows(self, token, count=1):
        start = (self.origin + token) * self.repeats
        if not isinstance(start, int):
            start = pl.multiple_of(start, self.repeats)
        return pl.ds(start, count * self.repeats)

    def __getitem__(self, token):
        return self.ref[(*self.lead, self.rows(token), slice(None))]

    def __setitem__(self, token, value):
        self.ref[(*self.lead, self.rows(token), slice(None))] = value

    def strided(self, token, repeat, count):
        start = (self.origin + token) * self.repeats + repeat
        return pl.ds(start, count, stride=self.repeats)

    def put(self, token, repeat, value):
        rows = self.strided(token, repeat, value.shape[0])
        self.ref[(*self.lead, rows, slice(None))] = value

    def take(self, token, repeat, count):
        return self.ref[(*self.lead, self.strided(token, repeat, count), slice(None))]


class Halo:
    def __init__(self, ref, repeats, columns):
        self.ref, self.repeats, self.columns = ref, repeats, columns

    def put(self, token, column, repeat, value):
        start = (token * self.columns + column) * self.repeats + repeat
        rows = pl.ds(start, value.shape[0], stride=self.columns * self.repeats)
        self.ref[rows, :] = value

    def tokens(self, column):
        class View:
            def __getitem__(_, token):
                start = (token * self.columns + column) * self.repeats
                if not isinstance(start, int):
                    start = pl.multiple_of(start, self.repeats)
                return self.ref[pl.ds(start, self.repeats), :]

        return View()


def held_tokens(reach):
    wide = 2 * reach
    return (
        (0, wide, reach),
        (0, reach, wide),
        (0, reach, wide),
        (0, wide, 0),
        (0, 0, reach),
        (0, 0, reach),
        (reach, wide, reach),
        (0, 0, reach),
    )


class Held:
    def __init__(self, ref, repeats, column, span):
        self.first, self.last, self.tail = span
        self.view = Tokens(ref, repeats, 0, (column,))

    def __getitem__(self, token):
        if token < 0:
            return self.view[self.last - self.first + self.tail + token]
        return self.view[token - self.first]


class Window:
    def __init__(self, load):
        self.load, self.held = load, {}

    def __call__(self, token):
        if token not in self.held:
            self.held[token] = self.load(token)
        return self.held[token]

    def back(self, token, taps):
        return [self(token - lag) for lag in range(taps)]

    def ahead(self, token, taps):
        return [self(token + lag) for lag in range(taps)]


class Sums:
    def __init__(self, taps):
        self.taps = taps
        self.held = {}

    def add(self, bank, grad, pieces):
        for lag, piece in enumerate(pieces):
            term = grad * piece
            old = self.held.get((bank, lag))
            self.held[bank, lag] = term if old is None else old + term

    def store(self, ref, lanes):
        for (bank, lag), value in self.held.items():
            ref[bank, lag, :, lanes] += value


def pack_kernel(
    reach,
    columns,
    features_hbm,
    cotangent_hbm,
    master_hbm,
    near_ref,
    far_ref,
    rounded_ref,
    tail,
    head,
    upstream,
    master,
    b_s,
    a_s,
    sems,
):
    length = cotangent_hbm.shape[0]
    copies = [
        pltpu.make_async_copy(features_hbm.at[:, length - PAD :, :], tail, sems.at[0]),
        pltpu.make_async_copy(features_hbm.at[:, :PAD, :], head, sems.at[1]),
        pltpu.make_async_copy(cotangent_hbm.at[:PAD, :], upstream, sems.at[2]),
        pltpu.make_async_copy(master_hbm, master, sems.at[3]),
    ]
    for copy in copies:
        copy.start()
    even = is_even("ctx")
    repeats = upstream.shape[1] // (columns * LANES)
    block = reach * columns * repeats
    b_s[5 * block : 6 * block, :] = jnp.zeros((block, LANES), F32)
    last, first = Halo(b_s, repeats, columns), Halo(a_s, repeats, columns)
    wide = 2 * reach

    def place(message, parts):
        def repeat_step(repeat, carry):
            for column in range(columns):
                lanes = lane_slice(repeat * columns + column)
                for token, ref, start, stop in parts:
                    value = ref[:, lanes].astype(F32)[start:stop]
                    message.put(token, column, repeat, value)
            return carry

        lax.fori_loop(0, repeats, repeat_step, 0)

    copies[0].wait()
    place(
        last,
        (
            (0, tail.at[0], PAD - reach, PAD),
            (reach, tail.at[1], PAD - wide, PAD),
            (3 * reach, tail.at[2], PAD - wide, PAD),
        ),
    )
    for copy in copies[1:]:
        copy.wait()
    rounded_ref[...] = master[...].astype(rounded_ref.dtype)
    place(
        first,
        (
            (0, head.at[0], 0, wide),
            (wide, upstream, 0, wide),
            (2 * wide, head.at[1], 0, reach),
            (5 * reach, head.at[2], 0, reach),
        ),
    )
    ending, opening = b_s[: 6 * block, :], a_s[: 6 * block, :]
    near_ref[...] = jnp.where(even, ending, opening).astype(near_ref.dtype)
    far_ref[...] = jnp.where(even, opening, ending).astype(far_ref.dtype)


def pack(features, cotangent, master, groups):
    reach = master.shape[0] - 1
    banks, length, channels = features.shape
    kind = features.dtype
    hbm = [
        pltpu.with_memory_space_constraint(value, pltpu.HBM)
        for value in (features, cotangent, master)
    ]
    message = jax.ShapeDtypeStruct((6 * reach * channels // LANES, LANES), kind)
    room = ((6 * reach + 8) * channels // LANES, LANES)
    return pl.pallas_call(
        functools.partial(pack_kernel, reach, groups // LANES),
        out_shape=(message, message, jax.ShapeDtypeStruct(master.shape, jnp.bfloat16)),
        in_specs=[pl.BlockSpec(memory_space=pltpu.HBM)] * 3,
        out_specs=(VMEM_SPEC,) * 3,
        scratch_shapes=[
            pltpu.VMEM((banks, PAD, channels), kind),
            pltpu.VMEM((banks, PAD, channels), kind),
            pltpu.VMEM((PAD, channels), kind),
            pltpu.VMEM(master.shape, F32),
            pltpu.VMEM(room, F32),
            pltpu.VMEM(room, F32),
            pltpu.SemaphoreType.DMA((4,)),
        ],
        cost_estimate=pl.CostEstimate(flops=10**6, bytes_accessed=10**6, transcendentals=0),
        compiler_params=pltpu.CompilerParams(vmem_limit_bytes=PACK_LIMIT),
        name="pack_halos",
    )(*hbm)


def interior_kernel(
    taps,
    repeats,
    features_ref,
    cotangent_hbm,
    weights_ref,
    mixed_ref,
    gq_ref,
    gk_ref,
    gv_ref,
    *refs,
):
    *held_refs, sums_ref = refs[:9]
    *work_refs, cotangent_ref, sem = refs[9:]
    *work_refs, k_other, v_other = work_refs
    q_s, k_s, v_s, c_s, kc_s, vc_s, p_s, gm_s = work_refs
    pairs = ((k_s, v_s), (k_other, v_other))
    reach = taps - 1
    groups = weights_ref.shape[2]
    length = cotangent_ref.shape[0]
    count = length // CHUNK
    fetch = pltpu.make_async_copy(cotangent_hbm, cotangent_ref, sem)
    fetch.start()
    sums_ref[...] = jnp.zeros_like(sums_ref)

    def part_of(repeat, column):
        first = repeat * groups + column * LANES
        return slice(first, first + LANES)

    zero = jnp.zeros((reach * repeats, LANES), F32)
    for ref in (q_s, p_s, k_s, v_s, k_other, v_other):
        ref[(PAD - reach) * repeats : PAD * repeats, :] = zero
    gm_s[(PAD + length) * repeats : (PAD + length + reach) * repeats, :] = zero
    q_t, c_t, kc_t, vc_t, p_t, gm_t = (
        Tokens(ref, repeats, PAD) for ref in (q_s, c_s, kc_s, vc_s, p_s, gm_s)
    )
    columns = groups // LANES

    def put_pair(column, base, rows):
        for bank, ref in enumerate(pairs[column % 2]):
            view = Tokens(ref, repeats, PAD)
            for repeat in range(repeats):
                part = part_of(repeat, column)
                view.put(base, repeat, features_ref[1 + bank, rows, part].astype(F32))

    def chunks(body):
        def step_body(step, carry):
            base = pl.multiple_of(step * CHUNK, CHUNK)
            body(step, base, pl.ds(base, CHUNK))
            return carry

        lax.fori_loop(0, count, step_body, 0)

    chunks(lambda step, base, rows: put_pair(0, base, rows))
    for column in range(columns):
        lanes = slice(column * LANES, (column + 1) * LANES)
        m_t, gq_t, gk_t, gv_t = (
            Tokens(ref, repeats, 0, (column,)) for ref in (mixed_ref, gq_ref, gk_ref, gv_ref)
        )
        k_t, v_t = (Tokens(ref, repeats, PAD) for ref in pairs[column % 2])
        wq, wk, wv, wm = (weight_rows(weights_ref, bank, lanes) for bank in range(4))

        def products(step, base, rows):
            for repeat in range(repeats):
                part = part_of(repeat, column)
                q_t.put(base, repeat, features_ref[0, rows, part].astype(F32))
            k_w, v_w = (Window(lambda t, view=view: view[base + t]) for view in (k_t, v_t))
            for token in range(CHUNK):
                kc = dot_taps(wk, k_w.back(token, taps))
                vc = dot_taps(wv, v_w.back(token, taps))
                kc_t[base + token] = kc
                vc_t[base + token] = vc
                p_t[base + token] = kc * vc

        def forward(step, base, rows):
            for repeat in range(repeats):
                part = part_of(repeat, column)
                c_t.put(base, repeat, cotangent_ref[rows, part].astype(F32))
            if column + 1 < columns:
                put_pair(column + 1, base, rows)
            sums = Sums(taps)
            q_w, p_w = (Window(lambda t, view=view: view[base + t]) for view in (q_t, p_t))
            for token in range(CHUNK):
                up = c_t[base + token]
                sources = q_w.back(token, taps)
                inner = p_w.back(token, taps)
                qc = dot_taps(wq, sources)
                mixer = dot_taps(wm, inner)
                gq = up * mixer
                gm = up * qc
                m_t[base + token] = qc * mixer
                gm_t[base + token] = gm
                gq_t[base + token] = gq
                if token < 2 * reach:
                    gq = jnp.where(step > 0, gq, 0.0)
                    gm = jnp.where(step > 0, gm, 0.0)
                sums.add(0, gq, sources)
                sums.add(3, gm, inner)
            sums.store(sums_ref, lanes)

        def backward(step, base, rows):
            k_w, v_w, gm_w = (
                Window(lambda t, view=view: view[base + t]) for view in (k_t, v_t, gm_t)
            )
            sums = Sums(taps)
            for token in range(CHUNK):
                gp = dot_taps(wm, gm_w.ahead(token, taps))
                if token < reach:
                    gp = jnp.where(step > 0, gp, 0.0)
                if token >= CHUNK - reach:
                    gp = jnp.where(step < count - 1, gp, 0.0)
                gk = gp * vc_t[base + token]
                gv = gp * kc_t[base + token]
                gk_t[base + token] = gk
                gv_t[base + token] = gv
                sums.add(1, gk, k_w.back(token, taps))
                sums.add(2, gv, v_w.back(token, taps))
            sums.store(sums_ref, lanes)

        chunks(products)
        if column == 0:
            fetch.wait()
        chunks(forward)
        chunks(backward)
        sources = (q_s, *pairs[column % 2], c_s, kc_s, vc_s, p_s, gm_s)
        for ref, work, (first, last, tail) in zip(held_refs, sources, held_tokens(reach)):
            target, source = Tokens(ref, repeats, 0, (column,)), Tokens(work, repeats, PAD)
            for token in (*range(first, last), *range(length - tail, length)):
                row = token - first if token < last else token - length + last - first + tail
                target[row] = source[token]


def interior(features, cotangent, weights):
    length, channels = cotangent.shape
    taps, banks, groups = weights.shape
    repeats = channels // groups
    columns = groups // LANES
    work = length * channels * taps * 2
    grad = jax.ShapeDtypeStruct((columns, length * repeats, LANES), F32)
    held = [
        jax.ShapeDtypeStruct((columns, (last - first + tail) * repeats, LANES), F32)
        for first, last, tail in held_tokens(taps - 1)
    ]
    work_shape = ((length + 2 * PAD) * repeats, LANES)
    mixed, gq, gk, gv, *arrays, sums = pl.pallas_call(
        functools.partial(interior_kernel, taps, repeats),
        out_shape=(
            *[grad] * 4,
            *held,
            jax.ShapeDtypeStruct((banks, taps, repeats, groups), F32),
        ),
        in_specs=[VMEM_SPEC, pl.BlockSpec(memory_space=pltpu.HBM), VMEM_SPEC],
        out_specs=(VMEM_SPEC,) * 13,
        scratch_shapes=[pltpu.VMEM(work_shape, F32) for _ in range(10)]
        + [
            pltpu.VMEM(cotangent.shape, cotangent.dtype),
            pltpu.SemaphoreType.DMA,
        ],
        cost_estimate=pl.CostEstimate(
            flops=9 * work, bytes_accessed=22 * length * channels, transcendentals=0
        ),
        compiler_params=pltpu.CompilerParams(vmem_limit_bytes=VMEM_LIMIT),
        name="interior",
    )(features, pltpu.with_memory_space_constraint(cotangent, pltpu.HBM), weights)
    return mixed, (gq, gk, gv), arrays, sums


def edge_kernel(
    taps,
    repeats,
    weights_ref,
    near_ref,
    far_ref,
    sums_in_ref,
    q_a,
    k_a,
    v_a,
    c_a,
    kc_a,
    vc_a,
    p_a,
    gm_a,
    mixed_ref,
    ghead_ref,
    gtail_ref,
    after_ref,
    sums_ref,
    acc,
    before_s,
    kc_s,
    vc_s,
    p_s,
    gm_s,
):
    reach = taps - 1
    groups = weights_ref.shape[2]
    acc[...] = sums_in_ref[...]
    even = is_even("ctx")
    columns = groups // LANES
    near, far = near_ref[...].astype(F32), far_ref[...].astype(F32)
    before_s[...] = jnp.where(even, far, near)
    after_ref[...] = jnp.where(even, near, far)
    kc_t, vc_t, p_t, gm_t = (Tokens(ref, repeats, PAD) for ref in (kc_s, vc_s, p_s, gm_s))

    def column_step(column, carry):
        lanes = lane_slice(column)
        wq, wk, wv, wm = (weight_rows(weights_ref, bank, lanes) for bank in range(4))
        q_t, k_t, v_t, c_t, kc_i, vc_i, p_i, gm_i = (
            Held(ref, repeats, column, span)
            for ref, span in zip(
                (q_a, k_a, v_a, c_a, kc_a, vc_a, p_a, gm_a), held_tokens(reach)
            )
        )
        sums = Sums(taps)

        h_t = Halo(before_s, repeats, columns).tokens(column)
        q_w = Window(lambda t: q_t[t] if t >= 0 else h_t[reach + t])
        k_w = Window(lambda t: k_t[t] if t >= 0 else h_t[3 * reach + t])
        v_w = Window(lambda t: v_t[t] if t >= 0 else h_t[5 * reach + t])
        gq_o, gk_o, gv_o = (Tokens(ghead_ref, repeats, 0, (bank, column)) for bank in range(3))
        m_o = Tokens(mixed_ref, repeats, 0, (column,))
        for token in range(-reach, reach):
            kc = dot_taps(wk, k_w.back(token, taps))
            vc = dot_taps(wv, v_w.back(token, taps))
            p_t[token] = kc * vc
            if token >= 0:
                kc_t[token] = kc
                vc_t[token] = vc
        p_w = Window(lambda t: p_t[t] if t < reach else p_i[t])
        for token in range(2 * reach):
            up = c_t[token]
            sources = q_w.back(token, taps)
            products = p_w.back(token, taps)
            qc = dot_taps(wq, sources)
            mixer = dot_taps(wm, products)
            gq = up * mixer
            gm = up * qc
            m_o[token] = qc * mixer
            gm_t[token] = gm
            gq_o[token] = gq
            sums.add(0, gq, sources)
            sums.add(3, gm, products)
        gm_w = Window(lambda t: gm_t[t])
        for token in range(reach):
            gp = dot_taps(wm, gm_w.ahead(token, taps))
            gk = gp * vc_t[token]
            gv = gp * kc_t[token]
            gk_o[token] = gk
            gv_o[token] = gv
            sums.add(1, gk, k_w.back(token, taps))
            sums.add(2, gv, v_w.back(token, taps))

        n_t = Halo(after_ref, repeats, columns).tokens(column)
        q_w = Window(lambda t: q_t[t] if t < 0 else n_t[t])
        gk_o, gv_o = (Tokens(gtail_ref, repeats, reach, (bank, column)) for bank in range(2))
        for token in range(reach):
            gm_t[token] = n_t[2 * reach + token] * dot_taps(wq, q_w.back(token, taps))
        gm_w = Window(lambda t: gm_i[t] if t < 0 else gm_t[t])
        k_w, v_w = (Window(lambda t, view=view: view[t]) for view in (k_t, v_t))
        for token in range(-reach, 0):
            gp = dot_taps(wm, gm_w.ahead(token, taps))
            gk = gp * vc_i[token]
            gv = gp * kc_i[token]
            gk_o[token] = gk
            gv_o[token] = gv
            sums.add(1, gk, k_w.back(token, taps))
            sums.add(2, gv, v_w.back(token, taps))
        sums.store(acc, lanes)
        return carry

    lax.fori_loop(0, groups // LANES, column_step, 0)
    for bank in range(sums_ref.shape[1]):
        sums_ref[:, bank, :] = jnp.sum(acc[bank], axis=1)


def edge(weights, near, far, sums, arrays):
    taps, banks, groups = weights.shape
    columns = groups // LANES
    reach = taps - 1
    repeats = near.shape[0] // (6 * reach * columns)
    return pl.pallas_call(
        functools.partial(edge_kernel, taps, repeats),
        out_shape=(
            jax.ShapeDtypeStruct((columns, 2 * reach * repeats, LANES), F32),
            jax.ShapeDtypeStruct((3, columns, 2 * reach * repeats, LANES), F32),
            jax.ShapeDtypeStruct((2, columns, reach * repeats, LANES), F32),
            jax.ShapeDtypeStruct(near.shape, F32),
            jax.ShapeDtypeStruct((taps, banks, groups), F32),
        ),
        in_specs=[VMEM_SPEC] * 12,
        out_specs=(VMEM_SPEC,) * 5,
        scratch_shapes=[
            pltpu.VMEM(sums.shape, F32),
            pltpu.VMEM(near.shape, F32),
        ]
        + [pltpu.VMEM((2 * PAD * repeats, LANES), F32) for _ in range(4)],
        cost_estimate=pl.CostEstimate(
            flops=10**7, bytes_accessed=4 * 10**6, transcendentals=0
        ),
        compiler_params=pltpu.CompilerParams(vmem_limit_bytes=VMEM_LIMIT),
        name="edge",
    )(weights, near, far, sums, *arrays)


def mixed_kernel(repeats, middle, top, out_ref, zero_ref, o_s):
    columns, rows, _ = middle.shape
    groups = columns * LANES
    ready = top.shape[1] // repeats
    zero_ref[...] = jnp.zeros_like(zero_ref)

    def column_step(column, carry):
        m_t, t_t = (Tokens(ref, repeats, 0, (column,)) for ref in (middle, top))
        o_t = Tokens(o_s, repeats)
        for token in range(CHUNK):
            o_t[token] = t_t[token] if token < ready else m_t[token]
        for repeat in range(repeats):
            part = part_slice(repeat, groups, column)
            out_ref[:CHUNK, part] = o_t.take(0, repeat, CHUNK).astype(out_ref.dtype)

        def chunk_step(chunk, carry):
            base = pl.multiple_of(chunk * CHUNK, CHUNK)
            for repeat in range(repeats):
                part = part_slice(repeat, groups, column)
                value = m_t.take(base, repeat, CHUNK)
                out_ref[pl.ds(base, CHUNK), part] = value.astype(out_ref.dtype)
            return carry

        return lax.fori_loop(1, rows // repeats // CHUNK, chunk_step, carry)

    lax.fori_loop(0, columns, column_step, 0)


def round_mixed(middle, top, cotangent, zero):
    columns, rows, _ = middle.shape
    length, channels = cotangent.shape
    repeats = rows // length
    return pl.pallas_call(
        functools.partial(mixed_kernel, repeats),
        out_shape=(jax.ShapeDtypeStruct(cotangent.shape, cotangent.dtype), zero),
        in_specs=[VMEM_SPEC] * 2,
        out_specs=(VMEM_SPEC,) * 2,
        scratch_shapes=[pltpu.VMEM((CHUNK * repeats, LANES), F32)],
        cost_estimate=pl.CostEstimate(
            flops=length * channels, bytes_accessed=6 * length * channels, transcendentals=0
        ),
        compiler_params=pltpu.CompilerParams(vmem_limit_bytes=VMEM_LIMIT),
        name="round_mixed",
    )(middle, top)


def grads_kernel(taps, repeats, first, steps, count, *refs):
    refs = list(refs)
    top, bottom = first == 0, first + steps == count

    def pop(number):
        taken, refs[:number] = refs[:number], []
        return taken

    weights_ref, gq, gk, gv, ghead, gtail = pop(6)
    if top:
        (whole,) = pop(1)
    else:
        pop(1)
    if bottom:
        after_ref, *ahead_of = pop(5)
    out_hbm, zero_ref = pop(2)
    copies = []
    out_s, o_s, sems = refs[-3:]
    reach = taps - 1
    groups = weights_ref.shape[2]
    columns = groups // LANES
    length = gq.shape[1] // repeats
    zero_ref[...] = jnp.zeros_like(zero_ref)
    if top:
        (mixed_hbm,) = pop(1)
        copies = [pltpu.make_async_copy(whole, mixed_hbm, sems.at[steps])]
        for copy in copies:
            copy.start()

    def load(bank, column, token):
        if token >= length:
            return Tokens(refs[0], repeats, 0, (bank, column))[token - length]
        if token < (reach if bank else 2 * reach):
            return Tokens(ghead, repeats, 0, (bank, column))[token]
        if bank and token >= length - reach:
            return Tokens(gtail, repeats, reach - length, (bank - 1, column))[token]
        return Tokens((gq, gk, gv)[bank], repeats, 0, (column,))[token]

    def next_shard(column, carry):
        gnext, p_s, gm_s = refs[:3]
        lanes = lane_slice(column)
        wq, wk, wv, wm = (weight_rows(weights_ref, bank, lanes) for bank in range(4))
        p_t, gm_t = (Tokens(ref, repeats) for ref in (p_s, gm_s))
        h_t = Halo(after_ref, repeats, columns).tokens(column)
        q_t, k_t, v_t, p_i = (
            Held(ref, repeats, column, held_tokens(reach)[which])
            for ref, which in zip(ahead_of, (0, 1, 2, 6))
        )
        q_w = Window(lambda t: q_t[t] if t < 0 else h_t[t])
        k_w = Window(lambda t: k_t[t] if t < 0 else h_t[4 * reach + t])
        v_w = Window(lambda t: v_t[t] if t < 0 else h_t[5 * reach + t])
        p_w = Window(lambda t: p_i[t] if t < 0 else p_t[t])
        gm_w = Window(lambda t: gm_t[t])
        next_q, next_k, next_v = (
            Tokens(gnext, repeats, 0, (bank, column)) for bank in range(3)
        )
        for token in range(2 * reach):
            gm_t[token] = h_t[2 * reach + token] * dot_taps(wq, q_w.back(token, taps))
        for token in range(reach):
            kc = dot_taps(wk, k_w.back(token, taps))
            vc = dot_taps(wv, v_w.back(token, taps))
            p_t[token] = kc * vc
            gp = dot_taps(wm, gm_w.ahead(token, taps))
            next_k[token] = gp * vc
            next_v[token] = gp * kc
            next_q[token] = h_t[2 * reach + token] * dot_taps(wm, p_w.back(token, taps))
        return carry

    def out_copy(slot):
        rows = slice((first + slot) * CHUNK, (first + slot + 1) * CHUNK)
        return pltpu.make_async_copy(out_s.at[slot], out_hbm.at[:, rows, :], sems.at[slot])

    if bottom:
        lax.fori_loop(0, columns, next_shard, 0)
    for slot in range(steps):
        base = (first + slot) * CHUNK

        def column_step(column, carry):
            lanes = lane_slice(column)
            o_t = Tokens(o_s, repeats)
            for bank in range(3):
                weights = weight_rows(weights_ref, bank, lanes)
                window = Window(lambda t: load(bank, column, base + t))
                for token in range(CHUNK):
                    o_t[token] = dot_taps(weights, window.ahead(token, taps))
                for repeat in range(repeats):
                    part = part_slice(repeat, groups, column)
                    out_s[slot, bank, :, part] = o_t.take(0, repeat, CHUNK).astype(out_s.dtype)
            return carry

        lax.fori_loop(0, columns, column_step, 0)
        out_copy(slot).start()
    for slot in range(steps):
        out_copy(slot).wait()
    for copy in copies:
        copy.wait()


def feature_gradients(
    piece, pieces, features, weights, grads, ghead, gtail, mixed, after, arrays, earlier, zero
):
    banks, length, channels = features.shape
    taps, _, groups = weights.shape
    repeats = channels // groups
    columns = groups // LANES
    reach = taps - 1
    count = length // CHUNK
    steps = count // pieces
    first = piece * steps
    operands = [weights, *grads, ghead, gtail]
    in_specs = [VMEM_SPEC] * len(operands)
    out_shape = [jax.ShapeDtypeStruct(features.shape, features.dtype), zero]
    out_specs = [ANY_SPEC, VMEM_SPEC]
    aliases = {}
    scratch = []
    if piece == 0:
        operands.append(mixed)
        in_specs.append(VMEM_SPEC)
        out_shape.append(jax.ShapeDtypeStruct(mixed.shape, mixed.dtype))
        out_specs.append(ANY_SPEC)
    else:
        aliases = {len(operands): 0}
        operands.append(earlier)
        in_specs.append(ANY_SPEC)
    if piece == pieces - 1:
        q_a, k_a, v_a, _, _, _, p_a, _ = arrays
        operands += [after, q_a, k_a, v_a, p_a]
        in_specs += [VMEM_SPEC] * 5
        scratch = [
            pltpu.VMEM((3, columns, reach * repeats, LANES), F32),
            pltpu.VMEM((reach * repeats, LANES), F32),
            pltpu.VMEM((2 * reach * repeats, LANES), F32),
        ]
    work = length * channels * taps * 2 // pieces
    return pl.pallas_call(
        functools.partial(grads_kernel, taps, repeats, first, steps, count),
        out_shape=out_shape,
        in_specs=in_specs,
        out_specs=out_specs,
        scratch_shapes=scratch
        + [
            pltpu.VMEM((steps, banks, CHUNK, channels), features.dtype),
            pltpu.VMEM((CHUNK * repeats, LANES), F32),
            pltpu.SemaphoreType.DMA((steps + 1,)),
        ],
        input_output_aliases=aliases,
        cost_estimate=pl.CostEstimate(
            flops=4 * work,
            bytes_accessed=18 * length * channels // pieces,
            transcendentals=0,
        ),
        compiler_params=pltpu.CompilerParams(vmem_limit_bytes=VMEM_LIMIT),
        name="feature_gradients",
    )(*operands)


def per_device(features, cotangent, master_filters):
    length = features.shape[1]
    near, far, rounded = pack(
        features,
        cotangent,
        jnp.transpose(master_filters, (1, 0, 2)),
        master_filters.shape[2] * lax.axis_size("fsdp"),
    )
    weights = gather_filters(rounded, "fsdp").astype(F32)
    halos = swap_pairs(near, far, "ctx")
    middle, grads, arrays, sums = interior(features, cotangent, weights)
    top, ghead, gtail, after, sums = edge(weights, *halos, sums, arrays)
    repeats = features.shape[2] // weights.shape[2]
    pieces = PIECES if (length // CHUNK) % PIECES == 0 else 1
    portion = sums.shape[2] // lax.axis_size("fsdp")
    zero = jax.ShapeDtypeStruct((*sums.shape[:2], portion), F32)
    whole, nothing = round_mixed(middle, top, cotangent, zero)
    owned = sum_scatter(sums, "fsdp") + nothing
    made = {"grads": None}

    def beside(piece):
        if piece >= pieces:
            return 0.0
        made["grads"], nothing, *rest = feature_gradients(
            piece,
            pieces,
            features,
            weights,
            grads,
            ghead,
            gtail,
            whole,
            after,
            arrays,
            made["grads"],
            zero,
        )
        if rest:
            made["mixed"] = rest[0]
        return nothing

    summed, done = sum_over(owned, "ctx", beside)
    for piece in range(done, pieces):
        beside(piece)
    count_all = length * lax.axis_size("ctx") * repeats * lax.axis_size("fsdp")
    filter_grads = jnp.transpose(summed * (1.0 / math.sqrt(count_all)), (1, 0, 2))
    return (made["mixed"], made["grads"], filter_grads)


def solution(mesh):
    return jax.shard_map(
        per_device,
        mesh=mesh,
        in_specs=(P(None, "ctx", "fsdp"), P("ctx", "fsdp"), P(None, None, "fsdp")),
        out_specs=(P("ctx", "fsdp"), P(None, "ctx", "fsdp"), P(None, None, "fsdp")),
        check_vma=False,
    )
```

```python
import functools
import math

import jax
import jax.numpy as jnp
from jax import lax
from jax.experimental import pallas as pl
from jax.experimental.pallas import tpu as pltpu
from jax.sharding import PartitionSpec as P

LANES = 128
CHUNK = 16
PAD = 16
PIECES = 4
VMEM_LIMIT = 28 * 1024 * 1024
PACK_LIMIT = 16 * 1024 * 1024
F32 = jnp.float32
VMEM_SPEC = pl.BlockSpec(memory_space=pltpu.VMEM)
ANY_SPEC = pl.BlockSpec(memory_space=pl.ANY)


def swap_pairs(near, far, axis):
    size = lax.axis_size(axis)
    inner = [(i, i ^ 1) for i in range(size) if i ^ 1 < size]
    outer = [(i, i - 1 if i % 2 == 0 else i + 1) for i in range(size)]
    outer = [(i, j) for i, j in outer if 0 <= j < size]
    far = lax.ppermute(far, axis, outer)
    near = lax.ppermute(near, axis, inner)
    return near, far


def is_even(axis):
    return lax.rem(lax.axis_index(axis), 2) == 0


def gather_filters(shard, axis):
    size = lax.axis_size(axis)
    if size != 2:
        return lax.all_gather(shard, axis, axis=2, tiled=True)
    other = lax.ppermute(shard, axis, [(0, 1), (1, 0)])
    first = lax.axis_index(axis) == 0
    return jnp.concatenate(
        [jnp.where(first, shard, other), jnp.where(first, other, shard)], axis=2
    )


def sum_over(value, axis, beside=None):
    size = lax.axis_size(axis)
    if size & (size - 1):
        return lax.psum(value, axis), 0
    rounds = size.bit_length() - 1
    for step in range(rounds):
        pairs = [(i, i ^ (1 << step)) for i in range(size)]
        received = lax.ppermute(value, axis, pairs)
        value = value + received
        if beside is not None:
            value = value + beside(step)
    return value, rounds


def sum_scatter(value, axis):
    size = lax.axis_size(axis)
    portion = value.shape[-1] // size
    if size != 2:
        total, _ = sum_over(value, axis)
        return lax.dynamic_slice_in_dim(
            total, lax.axis_index(axis) * portion, portion, value.ndim - 1
        )
    first = lax.axis_index(axis) == 0
    low, high = value[..., :portion], value[..., portion:]
    sent = lax.ppermute(jnp.where(first, high, low), axis, [(0, 1), (1, 0)])
    return jnp.where(first, low, high) + sent


def dot_taps(weights, pieces):
    total = weights[0] * pieces[0]
    for weight, piece in zip(weights[1:], pieces[1:]):
        total = total + weight * piece
    return total


def weight_rows(ref, bank, lanes):
    return [ref[lag, pl.ds(bank, 1), lanes] for lag in range(ref.shape[0])]


def lane_slice(index):
    return pl.ds(pl.multiple_of(index * LANES, LANES), LANES)


def part_slice(repeat, groups, column):
    return pl.ds(pl.multiple_of(repeat * groups + column * LANES, LANES), LANES)


class Tokens:
    def __init__(self, ref, repeats, origin=0, lead=()):
        self.ref, self.repeats, self.origin, self.lead = ref, repeats, origin, lead

    def rows(self, token, count=1):
        start = (self.origin + token) * self.repeats
        if not isinstance(start, int):
            start = pl.multiple_of(start, self.repeats)
        return pl.ds(start, count * self.repeats)

    def __getitem__(self, token):
        return self.ref[(*self.lead, self.rows(token), slice(None))]

    def __setitem__(self, token, value):
        self.ref[(*self.lead, self.rows(token), slice(None))] = value

    def strided(self, token, repeat, count):
        start = (self.origin + token) * self.repeats + repeat
        return pl.ds(start, count, stride=self.repeats)

    def put(self, token, repeat, value):
        rows = self.strided(token, repeat, value.shape[0])
        self.ref[(*self.lead, rows, slice(None))] = value

    def take(self, token, repeat, count):
        return self.ref[(*self.lead, self.strided(token, repeat, count), slice(None))]


class Halo:
    def __init__(self, ref, repeats, columns):
        self.ref, self.repeats, self.columns = ref, repeats, columns

    def put(self, token, column, repeat, value):
        start = (token * self.columns + column) * self.repeats + repeat
        rows = pl.ds(start, value.shape[0], stride=self.columns * self.repeats)
        self.ref[rows, :] = value

    def tokens(self, column):
        class View:
            def __getitem__(_, token):
                start = (token * self.columns + column) * self.repeats
                if not isinstance(start, int):
                    start = pl.multiple_of(start, self.repeats)
                return self.ref[pl.ds(start, self.repeats), :]

        return View()


def held_tokens(reach):
    wide = 2 * reach
    return (
        (0, wide, reach),
        (0, reach, wide),
        (0, reach, wide),
        (0, wide, 0),
        (0, 0, reach),
        (0, 0, reach),
        (reach, wide, reach),
        (0, 0, reach),
    )


class Held:
    def __init__(self, ref, repeats, column, span):
        self.first, self.last, self.tail = span
        self.view = Tokens(ref, repeats, 0, (column,))

    def __getitem__(self, token):
        if token < 0:
            return self.view[self.last - self.first + self.tail + token]
        return self.view[token - self.first]


class Window:
    def __init__(self, load):
        self.load, self.held = load, {}

    def __call__(self, token):
        if token not in self.held:
            self.held[token] = self.load(token)
        return self.held[token]

    def back(self, token, taps):
        return [self(token - lag) for lag in range(taps)]

    def ahead(self, token, taps):
        return [self(token + lag) for lag in range(taps)]


class Sums:
    def __init__(self, taps):
        self.taps = taps
        self.held = {}

    def add(self, bank, grad, pieces):
        for lag, piece in enumerate(pieces):
            term = grad * piece
            old = self.held.get((bank, lag))
            self.held[bank, lag] = term if old is None else old + term

    def store(self, ref, lanes):
        for (bank, lag), value in self.held.items():
            ref[bank, lag, :, lanes] += value


def pack_kernel(
    reach,
    columns,
    features_hbm,
    cotangent_hbm,
    master_hbm,
    near_ref,
    far_ref,
    rounded_ref,
    tail,
    head,
    upstream,
    master,
    b_s,
    a_s,
    sems,
):
    length = cotangent_hbm.shape[0]
    copies = [
        pltpu.make_async_copy(features_hbm.at[:, length - PAD :, :], tail, sems.at[0]),
        pltpu.make_async_copy(features_hbm.at[:, :PAD, :], head, sems.at[1]),
        pltpu.make_async_copy(cotangent_hbm.at[:PAD, :], upstream, sems.at[2]),
        pltpu.make_async_copy(master_hbm, master, sems.at[3]),
    ]
    for copy in copies:
        copy.start()
    even = is_even("ctx")
    repeats = upstream.shape[1] // (columns * LANES)
    block = reach * columns * repeats
    b_s[5 * block : 6 * block, :] = jnp.zeros((block, LANES), F32)
    last, first = Halo(b_s, repeats, columns), Halo(a_s, repeats, columns)
    wide = 2 * reach

    def place(message, parts):
        def repeat_step(repeat, carry):
            for column in range(columns):
                lanes = lane_slice(repeat * columns + column)
                for token, ref, start, stop in parts:
                    value = ref[:, lanes].astype(F32)[start:stop]
                    message.put(token, column, repeat, value)
            return carry

        lax.fori_loop(0, repeats, repeat_step, 0)

    copies[0].wait()
    place(
        last,
        (
            (0, tail.at[0], PAD - reach, PAD),
            (reach, tail.at[1], PAD - wide, PAD),
            (3 * reach, tail.at[2], PAD - wide, PAD),
        ),
    )
    for copy in copies[1:]:
        copy.wait()
    rounded_ref[...] = master[...].astype(rounded_ref.dtype)
    place(
        first,
        (
            (0, head.at[0], 0, wide),
            (wide, upstream, 0, wide),
            (2 * wide, head.at[1], 0, reach),
            (5 * reach, head.at[2], 0, reach),
        ),
    )
    ending, opening = b_s[: 6 * block, :], a_s[: 6 * block, :]
    near_ref[...] = jnp.where(even, ending, opening).astype(near_ref.dtype)
    far_ref[...] = jnp.where(even, opening, ending).astype(far_ref.dtype)


def pack(features, cotangent, master, groups):
    reach = master.shape[0] - 1
    banks, length, channels = features.shape
    kind = features.dtype
    hbm = [
        pltpu.with_memory_space_constraint(value, pltpu.HBM)
        for value in (features, cotangent, master)
    ]
    message = jax.ShapeDtypeStruct((6 * reach * channels // LANES, LANES), kind)
    room = ((6 * reach + 8) * channels // LANES, LANES)
    return pl.pallas_call(
        functools.partial(pack_kernel, reach, groups // LANES),
        out_shape=(message, message, jax.ShapeDtypeStruct(master.shape, jnp.bfloat16)),
        in_specs=[pl.BlockSpec(memory_space=pltpu.HBM)] * 3,
        out_specs=(VMEM_SPEC,) * 3,
        scratch_shapes=[
            pltpu.VMEM((banks, PAD, channels), kind),
            pltpu.VMEM((banks, PAD, channels), kind),
            pltpu.VMEM((PAD, channels), kind),
            pltpu.VMEM(master.shape, F32),
            pltpu.VMEM(room, F32),
            pltpu.VMEM(room, F32),
            pltpu.SemaphoreType.DMA((4,)),
        ],
        cost_estimate=pl.CostEstimate(flops=10**6, bytes_accessed=10**6, transcendentals=0),
        compiler_params=pltpu.CompilerParams(vmem_limit_bytes=PACK_LIMIT),
        name="pack_halos",
    )(*hbm)


def interior_kernel(
    taps,
    repeats,
    features_ref,
    cotangent_hbm,
    weights_ref,
    mixed_ref,
    gq_ref,
    gk_ref,
    gv_ref,
    *refs,
):
    *held_refs, sums_ref = refs[:9]
    *work_refs, cotangent_ref, sem = refs[9:]
    *work_refs, k_other, v_other = work_refs
    q_s, k_s, v_s, c_s, kc_s, vc_s, p_s, gm_s = work_refs
    pairs = ((k_s, v_s), (k_other, v_other))
    reach = taps - 1
    groups = weights_ref.shape[2]
    length = cotangent_ref.shape[0]
    count = length // CHUNK
    fetch = pltpu.make_async_copy(cotangent_hbm, cotangent_ref, sem)
    fetch.start()
    sums_ref[...] = jnp.zeros_like(sums_ref)

    def part_of(repeat, column):
        first = repeat * groups + column * LANES
        return slice(first, first + LANES)

    zero = jnp.zeros((reach * repeats, LANES), F32)
    for ref in (q_s, p_s, k_s, v_s, k_other, v_other):
        ref[(PAD - reach) * repeats : PAD * repeats, :] = zero
    gm_s[(PAD + length) * repeats : (PAD + length + reach) * repeats, :] = zero
    q_t, c_t, kc_t, vc_t, p_t, gm_t = (
        Tokens(ref, repeats, PAD) for ref in (q_s, c_s, kc_s, vc_s, p_s, gm_s)
    )
    columns = groups // LANES

    def put_pair(column, base, rows):
        for bank, ref in enumerate(pairs[column % 2]):
            view = Tokens(ref, repeats, PAD)
            for repeat in range(repeats):
                part = part_of(repeat, column)
                view.put(base, repeat, features_ref[1 + bank, rows, part].astype(F32))

    def chunks(body):
        def step_body(step, carry):
            base = pl.multiple_of(step * CHUNK, CHUNK)
            body(step, base, pl.ds(base, CHUNK))
            return carry

        lax.fori_loop(0, count, step_body, 0)

    chunks(lambda step, base, rows: put_pair(0, base, rows))
    for column in range(columns):
        lanes = slice(column * LANES, (column + 1) * LANES)
        m_t, gq_t, gk_t, gv_t = (
            Tokens(ref, repeats, 0, (column,)) for ref in (mixed_ref, gq_ref, gk_ref, gv_ref)
        )
        k_t, v_t = (Tokens(ref, repeats, PAD) for ref in pairs[column % 2])
        wq, wk, wv, wm = (weight_rows(weights_ref, bank, lanes) for bank in range(4))

        def products(step, base, rows):
            for repeat in range(repeats):
                part = part_of(repeat, column)
                q_t.put(base, repeat, features_ref[0, rows, part].astype(F32))
            k_w, v_w = (Window(lambda t, view=view: view[base + t]) for view in (k_t, v_t))
            for token in range(CHUNK):
                kc = dot_taps(wk, k_w.back(token, taps))
                vc = dot_taps(wv, v_w.back(token, taps))
                kc_t[base + token] = kc
                vc_t[base + token] = vc
                p_t[base + token] = kc * vc

        def forward(step, base, rows):
            for repeat in range(repeats):
                part = part_of(repeat, column)
                c_t.put(base, repeat, cotangent_ref[rows, part].astype(F32))
            if column + 1 < columns:
                put_pair(column + 1, base, rows)
            sums = Sums(taps)
            q_w, p_w = (Window(lambda t, view=view: view[base + t]) for view in (q_t, p_t))
            for token in range(CHUNK):
                up = c_t[base + token]
                sources = q_w.back(token, taps)
                inner = p_w.back(token, taps)
                qc = dot_taps(wq, sources)
                mixer = dot_taps(wm, inner)
                gq = up * mixer
                gm = up * qc
                m_t[base + token] = qc * mixer
                gm_t[base + token] = gm
                gq_t[base + token] = gq
                if token < 2 * reach:
                    gq = jnp.where(step > 0, gq, 0.0)
                    gm = jnp.where(step > 0, gm, 0.0)
                sums.add(0, gq, sources)
                sums.add(3, gm, inner)
            sums.store(sums_ref, lanes)

        def backward(step, base, rows):
            k_w, v_w, gm_w = (
                Window(lambda t, view=view: view[base + t]) for view in (k_t, v_t, gm_t)
            )
            sums = Sums(taps)
            for token in range(CHUNK):
                gp = dot_taps(wm, gm_w.ahead(token, taps))
                if token < reach:
                    gp = jnp.where(step > 0, gp, 0.0)
                if token >= CHUNK - reach:
                    gp = jnp.where(step < count - 1, gp, 0.0)
                gk = gp * vc_t[base + token]
                gv = gp * kc_t[base + token]
                gk_t[base + token] = gk
                gv_t[base + token] = gv
                sums.add(1, gk, k_w.back(token, taps))
                sums.add(2, gv, v_w.back(token, taps))
            sums.store(sums_ref, lanes)

        chunks(products)
        if column == 0:
            fetch.wait()
        chunks(forward)
        chunks(backward)
        sources = (q_s, *pairs[column % 2], c_s, kc_s, vc_s, p_s, gm_s)
        for ref, work, (first, last, tail) in zip(held_refs, sources, held_tokens(reach)):
            target, source = Tokens(ref, repeats, 0, (column,)), Tokens(work, repeats, PAD)
            for token in (*range(first, last), *range(length - tail, length)):
                row = token - first if token < last else token - length + last - first + tail
                target[row] = source[token]


def interior(features, cotangent, weights):
    length, channels = cotangent.shape
    taps, banks, groups = weights.shape
    repeats = channels // groups
    columns = groups // LANES
    work = length * channels * taps * 2
    grad = jax.ShapeDtypeStruct((columns, length * repeats, LANES), F32)
    held = [
        jax.ShapeDtypeStruct((columns, (last - first + tail) * repeats, LANES), F32)
        for first, last, tail in held_tokens(taps - 1)
    ]
    work_shape = ((length + 2 * PAD) * repeats, LANES)
    mixed, gq, gk, gv, *arrays, sums = pl.pallas_call(
        functools.partial(interior_kernel, taps, repeats),
        out_shape=(
            *[grad] * 4,
            *held,
            jax.ShapeDtypeStruct((banks, taps, repeats, groups), F32),
        ),
        in_specs=[VMEM_SPEC, pl.BlockSpec(memory_space=pltpu.HBM), VMEM_SPEC],
        out_specs=(VMEM_SPEC,) * 13,
        scratch_shapes=[pltpu.VMEM(work_shape, F32) for _ in range(10)]
        + [
            pltpu.VMEM(cotangent.shape, cotangent.dtype),
            pltpu.SemaphoreType.DMA,
        ],
        cost_estimate=pl.CostEstimate(
            flops=9 * work, bytes_accessed=22 * length * channels, transcendentals=0
        ),
        compiler_params=pltpu.CompilerParams(vmem_limit_bytes=VMEM_LIMIT),
        name="interior",
    )(features, pltpu.with_memory_space_constraint(cotangent, pltpu.HBM), weights)
    return mixed, (gq, gk, gv), arrays, sums


def edge_kernel(
    taps,
    repeats,
    weights_ref,
    near_ref,
    far_ref,
    sums_in_ref,
    q_a,
    k_a,
    v_a,
    c_a,
    kc_a,
    vc_a,
    p_a,
    gm_a,
    mixed_ref,
    ghead_ref,
    gtail_ref,
    after_ref,
    sums_ref,
    before_s,
    kc_s,
    vc_s,
    p_s,
    gm_s,
):
    reach = taps - 1
    groups = weights_ref.shape[2]
    even = is_even("ctx")
    columns = groups // LANES
    near, far = near_ref[...].astype(F32), far_ref[...].astype(F32)
    before_s[...] = jnp.where(even, far, near)
    after_ref[...] = jnp.where(even, near, far)

    for column in range(columns):
        lanes = slice(column * LANES, (column + 1) * LANES)
        kc_t, vc_t, p_t, gm_t = (
            Tokens(ref, repeats, reach, (column,)) for ref in (kc_s, vc_s, p_s, gm_s)
        )
        wq, wk, wv, wm = (weight_rows(weights_ref, bank, lanes) for bank in range(4))
        q_t, k_t, v_t, c_t, kc_i, vc_i, p_i, gm_i = (
            Held(ref, repeats, column, span)
            for ref, span in zip(
                (q_a, k_a, v_a, c_a, kc_a, vc_a, p_a, gm_a), held_tokens(reach)
            )
        )
        sums = Sums(taps)

        h_t = Halo(before_s, repeats, columns).tokens(column)
        q_w = Window(lambda t: q_t[t] if t >= 0 else h_t[reach + t])
        k_w = Window(lambda t: k_t[t] if t >= 0 else h_t[3 * reach + t])
        v_w = Window(lambda t: v_t[t] if t >= 0 else h_t[5 * reach + t])
        gq_o, gk_o, gv_o = (Tokens(ghead_ref, repeats, 0, (bank, column)) for bank in range(3))
        m_o = Tokens(mixed_ref, repeats, 0, (column,))
        for token in range(-reach, reach):
            kc = dot_taps(wk, k_w.back(token, taps))
            vc = dot_taps(wv, v_w.back(token, taps))
            p_t[token] = kc * vc
            if token >= 0:
                kc_t[token] = kc
                vc_t[token] = vc
        p_w = Window(lambda t: p_t[t] if t < reach else p_i[t])
        for token in range(2 * reach):
            up = c_t[token]
            sources = q_w.back(token, taps)
            products = p_w.back(token, taps)
            qc = dot_taps(wq, sources)
            mixer = dot_taps(wm, products)
            gq = up * mixer
            gm = up * qc
            m_o[token] = qc * mixer
            gm_t[token] = gm
            gq_o[token] = gq
            sums.add(0, gq, sources)
            sums.add(3, gm, products)
        gm_w = Window(lambda t: gm_t[t])
        for token in range(reach):
            gp = dot_taps(wm, gm_w.ahead(token, taps))
            gk = gp * vc_t[token]
            gv = gp * kc_t[token]
            gk_o[token] = gk
            gv_o[token] = gv
            sums.add(1, gk, k_w.back(token, taps))
            sums.add(2, gv, v_w.back(token, taps))

        n_t = Halo(after_ref, repeats, columns).tokens(column)
        q_w = Window(lambda t: q_t[t] if t < 0 else n_t[t])
        gk_o, gv_o = (Tokens(gtail_ref, repeats, reach, (bank, column)) for bank in range(2))
        for token in range(reach):
            gm_t[token] = n_t[2 * reach + token] * dot_taps(wq, q_w.back(token, taps))
        gm_w = Window(lambda t: gm_i[t] if t < 0 else gm_t[t])
        k_w, v_w = (Window(lambda t, view=view: view[t]) for view in (k_t, v_t))
        for token in range(-reach, 0):
            gp = dot_taps(wm, gm_w.ahead(token, taps))
            gk = gp * vc_i[token]
            gv = gp * kc_i[token]
            gk_o[token] = gk
            gv_o[token] = gv
            sums.add(1, gk, k_w.back(token, taps))
            sums.add(2, gv, v_w.back(token, taps))
        for (bank, lag), value in sums.held.items():
            total = sums_in_ref[bank, lag, :, lanes] + value
            sums_ref[lag, bank : bank + 1, lanes] = jnp.sum(total, axis=0, keepdims=True)


def edge(weights, near, far, sums, arrays):
    taps, banks, groups = weights.shape
    columns = groups // LANES
    reach = taps - 1
    repeats = near.shape[0] // (6 * reach * columns)
    return pl.pallas_call(
        functools.partial(edge_kernel, taps, repeats),
        out_shape=(
            jax.ShapeDtypeStruct((columns, 2 * reach * repeats, LANES), F32),
            jax.ShapeDtypeStruct((3, columns, 2 * reach * repeats, LANES), F32),
            jax.ShapeDtypeStruct((2, columns, reach * repeats, LANES), F32),
            jax.ShapeDtypeStruct(near.shape, F32),
            jax.ShapeDtypeStruct((taps, banks, groups), F32),
        ),
        in_specs=[VMEM_SPEC] * 12,
        out_specs=(VMEM_SPEC,) * 5,
        scratch_shapes=[
            pltpu.VMEM(near.shape, F32),
        ]
        + [pltpu.VMEM((columns, 3 * reach * repeats, LANES), F32) for _ in range(4)],
        cost_estimate=pl.CostEstimate(
            flops=10**7, bytes_accessed=4 * 10**6, transcendentals=0
        ),
        compiler_params=pltpu.CompilerParams(vmem_limit_bytes=VMEM_LIMIT),
        name="edge",
    )(weights, near, far, sums, *arrays)


def mixed_kernel(repeats, middle, top, out_ref, zero_ref, o_s):
    columns, rows, _ = middle.shape
    groups = columns * LANES
    ready = top.shape[1] // repeats
    zero_ref[...] = jnp.zeros_like(zero_ref)

    def column_step(column, carry):
        m_t, t_t = (Tokens(ref, repeats, 0, (column,)) for ref in (middle, top))
        o_t = Tokens(o_s, repeats)
        for token in range(CHUNK):
            o_t[token] = t_t[token] if token < ready else m_t[token]
        for repeat in range(repeats):
            part = part_slice(repeat, groups, column)
            out_ref[:CHUNK, part] = o_t.take(0, repeat, CHUNK).astype(out_ref.dtype)

        def chunk_step(chunk, carry):
            base = pl.multiple_of(chunk * CHUNK, CHUNK)
            for repeat in range(repeats):
                part = part_slice(repeat, groups, column)
                value = m_t.take(base, repeat, CHUNK)
                out_ref[pl.ds(base, CHUNK), part] = value.astype(out_ref.dtype)
            return carry

        return lax.fori_loop(1, rows // repeats // CHUNK, chunk_step, carry)

    lax.fori_loop(0, columns, column_step, 0)


def round_mixed(middle, top, cotangent, zero):
    columns, rows, _ = middle.shape
    length, channels = cotangent.shape
    repeats = rows // length
    return pl.pallas_call(
        functools.partial(mixed_kernel, repeats),
        out_shape=(jax.ShapeDtypeStruct(cotangent.shape, cotangent.dtype), zero),
        in_specs=[VMEM_SPEC] * 2,
        out_specs=(VMEM_SPEC,) * 2,
        scratch_shapes=[pltpu.VMEM((CHUNK * repeats, LANES), F32)],
        cost_estimate=pl.CostEstimate(
            flops=length * channels, bytes_accessed=6 * length * channels, transcendentals=0
        ),
        compiler_params=pltpu.CompilerParams(vmem_limit_bytes=VMEM_LIMIT),
        name="round_mixed",
    )(middle, top)


def grads_kernel(taps, repeats, first, steps, count, *refs):
    refs = list(refs)
    top, bottom = first == 0, first + steps == count

    def pop(number):
        taken, refs[:number] = refs[:number], []
        return taken

    weights_ref, gq, gk, gv, ghead, gtail = pop(6)
    if top:
        (whole,) = pop(1)
    else:
        pop(1)
    if bottom:
        after_ref, *ahead_of = pop(5)
    out_hbm, zero_ref = pop(2)
    copies = []
    out_s, o_s, sems = refs[-3:]
    reach = taps - 1
    groups = weights_ref.shape[2]
    columns = groups // LANES
    length = gq.shape[1] // repeats
    zero_ref[...] = jnp.zeros_like(zero_ref)
    if top:
        (mixed_hbm,) = pop(1)
        copies = [pltpu.make_async_copy(whole, mixed_hbm, sems.at[steps])]
        for copy in copies:
            copy.start()

    def load(bank, column, token):
        if token >= length:
            return Tokens(refs[0], repeats, 0, (bank, column))[token - length]
        if token < (reach if bank else 2 * reach):
            return Tokens(ghead, repeats, 0, (bank, column))[token]
        if bank and token >= length - reach:
            return Tokens(gtail, repeats, reach - length, (bank - 1, column))[token]
        return Tokens((gq, gk, gv)[bank], repeats, 0, (column,))[token]

    def next_shard(column, carry):
        gnext, p_s, gm_s = refs[:3]
        lanes = lane_slice(column)
        wq, wk, wv, wm = (weight_rows(weights_ref, bank, lanes) for bank in range(4))
        p_t, gm_t = (Tokens(ref, repeats) for ref in (p_s, gm_s))
        h_t = Halo(after_ref, repeats, columns).tokens(column)
        q_t, k_t, v_t, p_i = (
            Held(ref, repeats, column, held_tokens(reach)[which])
            for ref, which in zip(ahead_of, (0, 1, 2, 6))
        )
        q_w = Window(lambda t: q_t[t] if t < 0 else h_t[t])
        k_w = Window(lambda t: k_t[t] if t < 0 else h_t[4 * reach + t])
        v_w = Window(lambda t: v_t[t] if t < 0 else h_t[5 * reach + t])
        p_w = Window(lambda t: p_i[t] if t < 0 else p_t[t])
        gm_w = Window(lambda t: gm_t[t])
        next_q, next_k, next_v = (
            Tokens(gnext, repeats, 0, (bank, column)) for bank in range(3)
        )
        for token in range(2 * reach):
            gm_t[token] = h_t[2 * reach + token] * dot_taps(wq, q_w.back(token, taps))
        for token in range(reach):
            kc = dot_taps(wk, k_w.back(token, taps))
            vc = dot_taps(wv, v_w.back(token, taps))
            p_t[token] = kc * vc
            gp = dot_taps(wm, gm_w.ahead(token, taps))
            next_k[token] = gp * vc
            next_v[token] = gp * kc
            next_q[token] = h_t[2 * reach + token] * dot_taps(wm, p_w.back(token, taps))
        return carry

    def out_copy(slot):
        rows = slice((first + slot) * CHUNK, (first + slot + 1) * CHUNK)
        return pltpu.make_async_copy(out_s.at[slot], out_hbm.at[:, rows, :], sems.at[slot])

    if bottom:
        lax.fori_loop(0, columns, next_shard, 0)
    for slot in range(steps):
        base = (first + slot) * CHUNK

        def column_step(column, carry):
            lanes = lane_slice(column)
            o_t = Tokens(o_s, repeats)
            for bank in range(3):
                weights = weight_rows(weights_ref, bank, lanes)
                window = Window(lambda t: load(bank, column, base + t))
                for token in range(CHUNK):
                    o_t[token] = dot_taps(weights, window.ahead(token, taps))
                for repeat in range(repeats):
                    part = part_slice(repeat, groups, column)
                    out_s[slot, bank, :, part] = o_t.take(0, repeat, CHUNK).astype(out_s.dtype)
            return carry

        lax.fori_loop(0, columns, column_step, 0)
        out_copy(slot).start()
    for slot in range(steps):
        out_copy(slot).wait()
    for copy in copies:
        copy.wait()


def feature_gradients(
    piece, pieces, features, weights, grads, ghead, gtail, mixed, after, arrays, earlier, zero
):
    banks, length, channels = features.shape
    taps, _, groups = weights.shape
    repeats = channels // groups
    columns = groups // LANES
    reach = taps - 1
    count = length // CHUNK
    steps = count // pieces
    first = piece * steps
    operands = [weights, *grads, ghead, gtail]
    in_specs = [VMEM_SPEC] * len(operands)
    out_shape = [jax.ShapeDtypeStruct(features.shape, features.dtype), zero]
    out_specs = [ANY_SPEC, VMEM_SPEC]
    aliases = {}
    scratch = []
    if piece == 0:
        operands.append(mixed)
        in_specs.append(VMEM_SPEC)
        out_shape.append(jax.ShapeDtypeStruct(mixed.shape, mixed.dtype))
        out_specs.append(ANY_SPEC)
    else:
        aliases = {len(operands): 0}
        operands.append(earlier)
        in_specs.append(ANY_SPEC)
    if piece == pieces - 1:
        q_a, k_a, v_a, _, _, _, p_a, _ = arrays
        operands += [after, q_a, k_a, v_a, p_a]
        in_specs += [VMEM_SPEC] * 5
        scratch = [
            pltpu.VMEM((3, columns, reach * repeats, LANES), F32),
            pltpu.VMEM((reach * repeats, LANES), F32),
            pltpu.VMEM((2 * reach * repeats, LANES), F32),
        ]
    work = length * channels * taps * 2 // pieces
    return pl.pallas_call(
        functools.partial(grads_kernel, taps, repeats, first, steps, count),
        out_shape=out_shape,
        in_specs=in_specs,
        out_specs=out_specs,
        scratch_shapes=scratch
        + [
            pltpu.VMEM((steps, banks, CHUNK, channels), features.dtype),
            pltpu.VMEM((CHUNK * repeats, LANES), F32),
            pltpu.SemaphoreType.DMA((steps + 1,)),
        ],
        input_output_aliases=aliases,
        cost_estimate=pl.CostEstimate(
            flops=4 * work,
            bytes_accessed=18 * length * channels // pieces,
            transcendentals=0,
        ),
        compiler_params=pltpu.CompilerParams(vmem_limit_bytes=VMEM_LIMIT),
        name="feature_gradients",
    )(*operands)


def per_device(features, cotangent, master_filters):
    length = features.shape[1]
    near, far, rounded = pack(
        features,
        cotangent,
        jnp.transpose(master_filters, (1, 0, 2)),
        master_filters.shape[2] * lax.axis_size("fsdp"),
    )
    weights = gather_filters(rounded, "fsdp").astype(F32)
    halos = swap_pairs(near, far, "ctx")
    middle, grads, arrays, sums = interior(features, cotangent, weights)
    top, ghead, gtail, after, sums = edge(weights, *halos, sums, arrays)
    repeats = features.shape[2] // weights.shape[2]
    pieces = PIECES if (length // CHUNK) % PIECES == 0 else 1
    portion = sums.shape[2] // lax.axis_size("fsdp")
    zero = jax.ShapeDtypeStruct((*sums.shape[:2], portion), F32)
    whole, nothing = round_mixed(middle, top, cotangent, zero)
    owned = sum_scatter(sums, "fsdp") + nothing
    made = {"grads": None}

    def beside(piece):
        if piece >= pieces:
            return 0.0
        made["grads"], nothing, *rest = feature_gradients(
            piece,
            pieces,
            features,
            weights,
            grads,
            ghead,
            gtail,
            whole,
            after,
            arrays,
            made["grads"],
            zero,
        )
        if rest:
            made["mixed"] = rest[0]
        return nothing

    summed, done = sum_over(owned, "ctx", beside)
    for piece in range(done, pieces):
        beside(piece)
    count_all = length * lax.axis_size("ctx") * repeats * lax.axis_size("fsdp")
    filter_grads = jnp.transpose(summed * (1.0 / math.sqrt(count_all)), (1, 0, 2))
    return (made["mixed"], made["grads"], filter_grads)


def solution(mesh):
    return jax.shard_map(
        per_device,
        mesh=mesh,
        in_specs=(P(None, "ctx", "fsdp"), P("ctx", "fsdp"), P(None, None, "fsdp")),
        out_specs=(P("ctx", "fsdp"), P(None, "ctx", "fsdp"), P(None, None, "fsdp")),
        check_vma=False,
    )
```

```python
import functools
import math

import jax
import jax.numpy as jnp
from jax import lax
from jax.experimental import pallas as pl
from jax.experimental.pallas import tpu as pltpu
from jax.sharding import PartitionSpec as P

LANES = 128
CHUNK = 16
PAD = 16
PIECES = 4
VMEM_LIMIT = 28 * 1024 * 1024
PACK_LIMIT = 16 * 1024 * 1024
F32 = jnp.float32
VMEM_SPEC = pl.BlockSpec(memory_space=pltpu.VMEM)
ANY_SPEC = pl.BlockSpec(memory_space=pl.ANY)


def swap_pairs(near, far, axis):
    size = lax.axis_size(axis)
    inner = [(i, i ^ 1) for i in range(size) if i ^ 1 < size]
    outer = [(i, i - 1 if i % 2 == 0 else i + 1) for i in range(size)]
    outer = [(i, j) for i, j in outer if 0 <= j < size]
    far = lax.ppermute(far, axis, outer)
    near = lax.ppermute(near, axis, inner)
    return near, far


def is_even(axis):
    return lax.rem(lax.axis_index(axis), 2) == 0


def gather_filters(shard, axis):
    size = lax.axis_size(axis)
    if size != 2:
        return lax.all_gather(shard, axis, axis=2, tiled=True)
    other = lax.ppermute(shard, axis, [(0, 1), (1, 0)])
    first = lax.axis_index(axis) == 0
    return jnp.concatenate(
        [jnp.where(first, shard, other), jnp.where(first, other, shard)], axis=2
    )


def sum_over(value, axis, beside=None):
    size = lax.axis_size(axis)
    if size & (size - 1):
        return lax.psum(value, axis), 0
    rounds = size.bit_length() - 1
    for step in range(rounds):
        pairs = [(i, i ^ (1 << step)) for i in range(size)]
        received = lax.ppermute(value, axis, pairs)
        value = value + received
        if beside is not None:
            value = value + beside(step)
    return value, rounds


def sum_scatter(parts, axis):
    if len(parts) == 2:
        kept, sent = parts
        return kept + lax.ppermute(sent, axis, [(0, 1), (1, 0)])
    (value,) = parts
    portion = value.shape[-1] // lax.axis_size(axis)
    total, _ = sum_over(value, axis)
    return lax.dynamic_slice_in_dim(
        total, lax.axis_index(axis) * portion, portion, value.ndim - 1
    )


def dot_taps(weights, pieces):
    total = weights[0] * pieces[0]
    for weight, piece in zip(weights[1:], pieces[1:]):
        total = total + weight * piece
    return total


def weight_rows(ref, bank, lanes):
    return [ref[lag, pl.ds(bank, 1), lanes] for lag in range(ref.shape[0])]


def lane_slice(index):
    return pl.ds(pl.multiple_of(index * LANES, LANES), LANES)


def part_slice(repeat, groups, column):
    return pl.ds(pl.multiple_of(repeat * groups + column * LANES, LANES), LANES)


class Tokens:
    def __init__(self, ref, repeats, origin=0, lead=()):
        self.ref, self.repeats, self.origin, self.lead = ref, repeats, origin, lead

    def rows(self, token, count=1):
        start = (self.origin + token) * self.repeats
        if not isinstance(start, int):
            start = pl.multiple_of(start, self.repeats)
        return pl.ds(start, count * self.repeats)

    def __getitem__(self, token):
        return self.ref[(*self.lead, self.rows(token), slice(None))]

    def __setitem__(self, token, value):
        self.ref[(*self.lead, self.rows(token), slice(None))] = value

    def strided(self, token, repeat, count):
        start = (self.origin + token) * self.repeats + repeat
        return pl.ds(start, count, stride=self.repeats)

    def put(self, token, repeat, value):
        rows = self.strided(token, repeat, value.shape[0])
        self.ref[(*self.lead, rows, slice(None))] = value

    def take(self, token, repeat, count):
        return self.ref[(*self.lead, self.strided(token, repeat, count), slice(None))]


class Halo:
    def __init__(self, ref, repeats, columns):
        self.ref, self.repeats, self.columns = ref, repeats, columns

    def put(self, token, column, repeat, value):
        start = (token * self.columns + column) * self.repeats + repeat
        rows = pl.ds(start, value.shape[0], stride=self.columns * self.repeats)
        self.ref[rows, :] = value

    def tokens(self, column):
        class View:
            def __getitem__(_, token):
                start = (token * self.columns + column) * self.repeats
                if not isinstance(start, int):
                    start = pl.multiple_of(start, self.repeats)
                return self.ref[pl.ds(start, self.repeats), :]

        return View()


def held_tokens(reach):
    wide = 2 * reach
    return (
        (0, wide, reach),
        (0, reach, wide),
        (0, reach, wide),
        (0, wide, 0),
        (0, 0, reach),
        (0, 0, reach),
        (reach, wide, reach),
        (0, 0, reach),
    )


class Held:
    def __init__(self, ref, repeats, column, span):
        self.first, self.last, self.tail = span
        self.view = Tokens(ref, repeats, 0, (column,))

    def __getitem__(self, token):
        if token < 0:
            return self.view[self.last - self.first + self.tail + token]
        return self.view[token - self.first]


class Window:
    def __init__(self, load):
        self.load, self.held = load, {}

    def __call__(self, token):
        if token not in self.held:
            self.held[token] = self.load(token)
        return self.held[token]

    def back(self, token, taps):
        return [self(token - lag) for lag in range(taps)]

    def ahead(self, token, taps):
        return [self(token + lag) for lag in range(taps)]


class Sums:
    def __init__(self, taps):
        self.taps = taps
        self.held = {}

    def add(self, bank, grad, pieces):
        for lag, piece in enumerate(pieces):
            term = grad * piece
            old = self.held.get((bank, lag))
            self.held[bank, lag] = term if old is None else old + term

    def store(self, ref, lanes):
        for (bank, lag), value in self.held.items():
            ref[bank, lag, :, lanes] += value


def pack_kernel(
    reach,
    columns,
    features_hbm,
    cotangent_hbm,
    master_hbm,
    near_ref,
    far_ref,
    rounded_ref,
    tail,
    head,
    upstream,
    master,
    b_s,
    a_s,
    sems,
):
    length = cotangent_hbm.shape[0]
    copies = [
        pltpu.make_async_copy(features_hbm.at[:, length - PAD :, :], tail, sems.at[0]),
        pltpu.make_async_copy(features_hbm.at[:, :PAD, :], head, sems.at[1]),
        pltpu.make_async_copy(cotangent_hbm.at[:PAD, :], upstream, sems.at[2]),
        pltpu.make_async_copy(master_hbm, master, sems.at[3]),
    ]
    for copy in copies:
        copy.start()
    even = is_even("ctx")
    repeats = upstream.shape[1] // (columns * LANES)
    block = reach * columns * repeats
    b_s[5 * block : 6 * block, :] = jnp.zeros((block, LANES), F32)
    last, first = Halo(b_s, repeats, columns), Halo(a_s, repeats, columns)
    wide = 2 * reach

    def place(message, parts):
        def repeat_step(repeat, carry):
            for column in range(columns):
                lanes = lane_slice(repeat * columns + column)
                for token, ref, start, stop in parts:
                    value = ref[:, lanes].astype(F32)[start:stop]
                    message.put(token, column, repeat, value)
            return carry

        lax.fori_loop(0, repeats, repeat_step, 0)

    copies[0].wait()
    place(
        last,
        (
            (0, tail.at[0], PAD - reach, PAD),
            (reach, tail.at[1], PAD - wide, PAD),
            (3 * reach, tail.at[2], PAD - wide, PAD),
        ),
    )
    for copy in copies[1:]:
        copy.wait()
    rounded_ref[...] = master[...].astype(rounded_ref.dtype)
    place(
        first,
        (
            (0, head.at[0], 0, wide),
            (wide, upstream, 0, wide),
            (2 * wide, head.at[1], 0, reach),
            (5 * reach, head.at[2], 0, reach),
        ),
    )
    ending, opening = b_s[: 6 * block, :], a_s[: 6 * block, :]
    near_ref[...] = jnp.where(even, ending, opening).astype(near_ref.dtype)
    far_ref[...] = jnp.where(even, opening, ending).astype(far_ref.dtype)


def pack(features, cotangent, master, groups):
    reach = master.shape[0] - 1
    banks, length, channels = features.shape
    kind = features.dtype
    hbm = [
        pltpu.with_memory_space_constraint(value, pltpu.HBM)
        for value in (features, cotangent, master)
    ]
    message = jax.ShapeDtypeStruct((6 * reach * channels // LANES, LANES), kind)
    room = ((6 * reach + 8) * channels // LANES, LANES)
    return pl.pallas_call(
        functools.partial(pack_kernel, reach, groups // LANES),
        out_shape=(message, message, jax.ShapeDtypeStruct(master.shape, jnp.bfloat16)),
        in_specs=[pl.BlockSpec(memory_space=pltpu.HBM)] * 3,
        out_specs=(VMEM_SPEC,) * 3,
        scratch_shapes=[
            pltpu.VMEM((banks, PAD, channels), kind),
            pltpu.VMEM((banks, PAD, channels), kind),
            pltpu.VMEM((PAD, channels), kind),
            pltpu.VMEM(master.shape, F32),
            pltpu.VMEM(room, F32),
            pltpu.VMEM(room, F32),
            pltpu.SemaphoreType.DMA((4,)),
        ],
        cost_estimate=pl.CostEstimate(flops=10**6, bytes_accessed=10**6, transcendentals=0),
        compiler_params=pltpu.CompilerParams(vmem_limit_bytes=PACK_LIMIT),
        name="pack_halos",
    )(*hbm)


def interior_kernel(
    taps,
    repeats,
    features_ref,
    cotangent_hbm,
    weights_ref,
    mixed_ref,
    gq_ref,
    gk_ref,
    gv_ref,
    *refs,
):
    *held_refs, sums_ref = refs[:9]
    *work_refs, cotangent_ref, sem = refs[9:]
    *work_refs, k_other, v_other = work_refs
    q_s, k_s, v_s, c_s, kc_s, vc_s, p_s, gm_s = work_refs
    pairs = ((k_s, v_s), (k_other, v_other))
    reach = taps - 1
    groups = weights_ref.shape[2]
    length = cotangent_ref.shape[0]
    count = length // CHUNK
    fetch = pltpu.make_async_copy(cotangent_hbm, cotangent_ref, sem)
    fetch.start()
    sums_ref[...] = jnp.zeros_like(sums_ref)

    def part_of(repeat, column):
        first = repeat * groups + column * LANES
        return slice(first, first + LANES)

    zero = jnp.zeros((reach * repeats, LANES), F32)
    for ref in (q_s, p_s, k_s, v_s, k_other, v_other):
        ref[(PAD - reach) * repeats : PAD * repeats, :] = zero
    gm_s[(PAD + length) * repeats : (PAD + length + reach) * repeats, :] = zero
    q_t, c_t, kc_t, vc_t, p_t, gm_t = (
        Tokens(ref, repeats, PAD) for ref in (q_s, c_s, kc_s, vc_s, p_s, gm_s)
    )
    columns = groups // LANES

    def put_pair(column, base, rows):
        for bank, ref in enumerate(pairs[column % 2]):
            view = Tokens(ref, repeats, PAD)
            for repeat in range(repeats):
                part = part_of(repeat, column)
                view.put(base, repeat, features_ref[1 + bank, rows, part].astype(F32))

    def chunks(body):
        def step_body(step, carry):
            base = pl.multiple_of(step * CHUNK, CHUNK)
            body(step, base, pl.ds(base, CHUNK))
            return carry

        lax.fori_loop(0, count, step_body, 0)

    chunks(lambda step, base, rows: put_pair(0, base, rows))
    for column in range(columns):
        lanes = slice(column * LANES, (column + 1) * LANES)
        m_t, gq_t, gk_t, gv_t = (
            Tokens(ref, repeats, 0, (column,)) for ref in (mixed_ref, gq_ref, gk_ref, gv_ref)
        )
        k_t, v_t = (Tokens(ref, repeats, PAD) for ref in pairs[column % 2])
        wq, wk, wv, wm = (weight_rows(weights_ref, bank, lanes) for bank in range(4))

        def products(step, base, rows):
            for repeat in range(repeats):
                part = part_of(repeat, column)
                q_t.put(base, repeat, features_ref[0, rows, part].astype(F32))
            k_w, v_w = (Window(lambda t, view=view: view[base + t]) for view in (k_t, v_t))
            for token in range(CHUNK):
                kc = dot_taps(wk, k_w.back(token, taps))
                vc = dot_taps(wv, v_w.back(token, taps))
                kc_t[base + token] = kc
                vc_t[base + token] = vc
                p_t[base + token] = kc * vc

        def forward(step, base, rows):
            for repeat in range(repeats):
                part = part_of(repeat, column)
                c_t.put(base, repeat, cotangent_ref[rows, part].astype(F32))
            if column + 1 < columns:
                put_pair(column + 1, base, rows)
            sums = Sums(taps)
            q_w, p_w = (Window(lambda t, view=view: view[base + t]) for view in (q_t, p_t))
            for token in range(CHUNK):
                up = c_t[base + token]
                sources = q_w.back(token, taps)
                inner = p_w.back(token, taps)
                qc = dot_taps(wq, sources)
                mixer = dot_taps(wm, inner)
                gq = up * mixer
                gm = up * qc
                m_t[base + token] = qc * mixer
                gm_t[base + token] = gm
                gq_t[base + token] = gq
                if token < 2 * reach:
                    gq = jnp.where(step > 0, gq, 0.0)
                    gm = jnp.where(step > 0, gm, 0.0)
                sums.add(0, gq, sources)
                sums.add(3, gm, inner)
            sums.store(sums_ref, lanes)

        def backward(step, base, rows):
            k_w, v_w, gm_w = (
                Window(lambda t, view=view: view[base + t]) for view in (k_t, v_t, gm_t)
            )
            sums = Sums(taps)
            for token in range(CHUNK):
                gp = dot_taps(wm, gm_w.ahead(token, taps))
                if token < reach:
                    gp = jnp.where(step > 0, gp, 0.0)
                if token >= CHUNK - reach:
                    gp = jnp.where(step < count - 1, gp, 0.0)
                gk = gp * vc_t[base + token]
                gv = gp * kc_t[base + token]
                gk_t[base + token] = gk
                gv_t[base + token] = gv
                sums.add(1, gk, k_w.back(token, taps))
                sums.add(2, gv, v_w.back(token, taps))
            sums.store(sums_ref, lanes)

        chunks(products)
        if column == 0:
            fetch.wait()
        chunks(forward)
        chunks(backward)
        sources = (q_s, *pairs[column % 2], c_s, kc_s, vc_s, p_s, gm_s)
        for ref, work, (first, last, tail) in zip(held_refs, sources, held_tokens(reach)):
            target, source = Tokens(ref, repeats, 0, (column,)), Tokens(work, repeats, PAD)
            for token in (*range(first, last), *range(length - tail, length)):
                row = token - first if token < last else token - length + last - first + tail
                target[row] = source[token]


def interior(features, cotangent, weights):
    length, channels = cotangent.shape
    taps, banks, groups = weights.shape
    repeats = channels // groups
    columns = groups // LANES
    work = length * channels * taps * 2
    grad = jax.ShapeDtypeStruct((columns, length * repeats, LANES), F32)
    held = [
        jax.ShapeDtypeStruct((columns, (last - first + tail) * repeats, LANES), F32)
        for first, last, tail in held_tokens(taps - 1)
    ]
    work_shape = ((length + 2 * PAD) * repeats, LANES)
    mixed, gq, gk, gv, *arrays, sums = pl.pallas_call(
        functools.partial(interior_kernel, taps, repeats),
        out_shape=(
            *[grad] * 4,
            *held,
            jax.ShapeDtypeStruct((banks, taps, repeats, groups), F32),
        ),
        in_specs=[VMEM_SPEC, pl.BlockSpec(memory_space=pltpu.HBM), VMEM_SPEC],
        out_specs=(VMEM_SPEC,) * 13,
        scratch_shapes=[pltpu.VMEM(work_shape, F32) for _ in range(10)]
        + [
            pltpu.VMEM(cotangent.shape, cotangent.dtype),
            pltpu.SemaphoreType.DMA,
        ],
        cost_estimate=pl.CostEstimate(
            flops=9 * work, bytes_accessed=22 * length * channels, transcendentals=0
        ),
        compiler_params=pltpu.CompilerParams(vmem_limit_bytes=VMEM_LIMIT),
        name="interior",
    )(features, pltpu.with_memory_space_constraint(cotangent, pltpu.HBM), weights)
    return mixed, (gq, gk, gv), arrays, sums


def edge_kernel(
    taps,
    repeats,
    weights_ref,
    near_ref,
    far_ref,
    sums_in_ref,
    q_a,
    k_a,
    v_a,
    c_a,
    kc_a,
    vc_a,
    p_a,
    gm_a,
    mixed_ref,
    ghead_ref,
    gtail_ref,
    after_ref,
    *refs,
):
    *sums_out, sums_ref, before_s, kc_s, vc_s, p_s, gm_s = refs
    reach = taps - 1
    groups = weights_ref.shape[2]
    even = is_even("ctx")
    columns = groups // LANES
    near, far = near_ref[...].astype(F32), far_ref[...].astype(F32)
    before_s[...] = jnp.where(even, far, near)
    after_ref[...] = jnp.where(even, near, far)

    for column in range(columns):
        lanes = slice(column * LANES, (column + 1) * LANES)
        kc_t, vc_t, p_t, gm_t = (
            Tokens(ref, repeats, reach, (column,)) for ref in (kc_s, vc_s, p_s, gm_s)
        )
        wq, wk, wv, wm = (weight_rows(weights_ref, bank, lanes) for bank in range(4))
        q_t, k_t, v_t, c_t, kc_i, vc_i, p_i, gm_i = (
            Held(ref, repeats, column, span)
            for ref, span in zip(
                (q_a, k_a, v_a, c_a, kc_a, vc_a, p_a, gm_a), held_tokens(reach)
            )
        )
        sums = Sums(taps)

        h_t = Halo(before_s, repeats, columns).tokens(column)
        q_w = Window(lambda t: q_t[t] if t >= 0 else h_t[reach + t])
        k_w = Window(lambda t: k_t[t] if t >= 0 else h_t[3 * reach + t])
        v_w = Window(lambda t: v_t[t] if t >= 0 else h_t[5 * reach + t])
        gq_o, gk_o, gv_o = (Tokens(ghead_ref, repeats, 0, (bank, column)) for bank in range(3))
        m_o = Tokens(mixed_ref, repeats, 0, (column,))
        for token in range(-reach, reach):
            kc = dot_taps(wk, k_w.back(token, taps))
            vc = dot_taps(wv, v_w.back(token, taps))
            p_t[token] = kc * vc
            if token >= 0:
                kc_t[token] = kc
                vc_t[token] = vc
        p_w = Window(lambda t: p_t[t] if t < reach else p_i[t])
        for token in range(2 * reach):
            up = c_t[token]
            sources = q_w.back(token, taps)
            products = p_w.back(token, taps)
            qc = dot_taps(wq, sources)
            mixer = dot_taps(wm, products)
            gq = up * mixer
            gm = up * qc
            m_o[token] = qc * mixer
            gm_t[token] = gm
            gq_o[token] = gq
            sums.add(0, gq, sources)
            sums.add(3, gm, products)
        gm_w = Window(lambda t: gm_t[t])
        for token in range(reach):
            gp = dot_taps(wm, gm_w.ahead(token, taps))
            gk = gp * vc_t[token]
            gv = gp * kc_t[token]
            gk_o[token] = gk
            gv_o[token] = gv
            sums.add(1, gk, k_w.back(token, taps))
            sums.add(2, gv, v_w.back(token, taps))

        n_t = Halo(after_ref, repeats, columns).tokens(column)
        q_w = Window(lambda t: q_t[t] if t < 0 else n_t[t])
        gk_o, gv_o = (Tokens(gtail_ref, repeats, reach, (bank, column)) for bank in range(2))
        for token in range(reach):
            gm_t[token] = n_t[2 * reach + token] * dot_taps(wq, q_w.back(token, taps))
        gm_w = Window(lambda t: gm_i[t] if t < 0 else gm_t[t])
        k_w, v_w = (Window(lambda t, view=view: view[t]) for view in (k_t, v_t))
        for token in range(-reach, 0):
            gp = dot_taps(wm, gm_w.ahead(token, taps))
            gk = gp * vc_i[token]
            gv = gp * kc_i[token]
            gk_o[token] = gk
            gv_o[token] = gv
            sums.add(1, gk, k_w.back(token, taps))
            sums.add(2, gv, v_w.back(token, taps))
        for (bank, lag), value in sums.held.items():
            total = sums_in_ref[bank, lag, :, lanes] + value
            sums_ref[lag, bank : bank + 1, lanes] = jnp.sum(total, axis=0, keepdims=True)
    if len(sums_out) == 1:
        sums_out[0][...] = sums_ref[...]
    else:
        low, high = sums_ref[:, :, : groups // 2], sums_ref[:, :, groups // 2 :]
        first = lax.axis_index("fsdp") == 0
        sums_out[0][...] = jnp.where(first, low, high)
        sums_out[1][...] = jnp.where(first, high, low)


def edge(weights, near, far, sums, arrays):
    taps, banks, groups = weights.shape
    columns = groups // LANES
    reach = taps - 1
    repeats = near.shape[0] // (6 * reach * columns)
    parts = 2 if lax.axis_size("fsdp") == 2 else 1
    return pl.pallas_call(
        functools.partial(edge_kernel, taps, repeats),
        out_shape=(
            jax.ShapeDtypeStruct((columns, 2 * reach * repeats, LANES), F32),
            jax.ShapeDtypeStruct((3, columns, 2 * reach * repeats, LANES), F32),
            jax.ShapeDtypeStruct((2, columns, reach * repeats, LANES), F32),
            jax.ShapeDtypeStruct(near.shape, F32),
            *[jax.ShapeDtypeStruct((taps, banks, groups // parts), F32)] * parts,
        ),
        in_specs=[VMEM_SPEC] * 12,
        out_specs=(VMEM_SPEC,) * (4 + parts),
        scratch_shapes=[
            pltpu.VMEM((taps, banks, groups), F32),
            pltpu.VMEM(near.shape, F32),
        ]
        + [pltpu.VMEM((columns, 3 * reach * repeats, LANES), F32) for _ in range(4)],
        cost_estimate=pl.CostEstimate(
            flops=10**7, bytes_accessed=4 * 10**6, transcendentals=0
        ),
        compiler_params=pltpu.CompilerParams(vmem_limit_bytes=VMEM_LIMIT),
        name="edge",
    )(weights, near, far, sums, *arrays)


def mixed_kernel(repeats, middle, top, out_ref, zero_ref, o_s):
    columns, rows, _ = middle.shape
    groups = columns * LANES
    ready = top.shape[1] // repeats
    zero_ref[...] = jnp.zeros_like(zero_ref)

    def column_step(column, carry):
        m_t, t_t = (Tokens(ref, repeats, 0, (column,)) for ref in (middle, top))
        o_t = Tokens(o_s, repeats)
        for token in range(CHUNK):
            o_t[token] = t_t[token] if token < ready else m_t[token]
        for repeat in range(repeats):
            part = part_slice(repeat, groups, column)
            out_ref[:CHUNK, part] = o_t.take(0, repeat, CHUNK).astype(out_ref.dtype)

        def chunk_step(chunk, carry):
            base = pl.multiple_of(chunk * CHUNK, CHUNK)
            for repeat in range(repeats):
                part = part_slice(repeat, groups, column)
                value = m_t.take(base, repeat, CHUNK)
                out_ref[pl.ds(base, CHUNK), part] = value.astype(out_ref.dtype)
            return carry

        return lax.fori_loop(1, rows // repeats // CHUNK, chunk_step, carry)

    lax.fori_loop(0, columns, column_step, 0)


def round_mixed(middle, top, cotangent, zero):
    columns, rows, _ = middle.shape
    length, channels = cotangent.shape
    repeats = rows // length
    return pl.pallas_call(
        functools.partial(mixed_kernel, repeats),
        out_shape=(jax.ShapeDtypeStruct(cotangent.shape, cotangent.dtype), zero),
        in_specs=[VMEM_SPEC] * 2,
        out_specs=(VMEM_SPEC,) * 2,
        scratch_shapes=[pltpu.VMEM((CHUNK * repeats, LANES), F32)],
        cost_estimate=pl.CostEstimate(
            flops=length * channels, bytes_accessed=6 * length * channels, transcendentals=0
        ),
        compiler_params=pltpu.CompilerParams(vmem_limit_bytes=VMEM_LIMIT),
        name="round_mixed",
    )(middle, top)


def grads_kernel(taps, repeats, first, steps, count, *refs):
    refs = list(refs)
    top, bottom = first == 0, first + steps == count

    def pop(number):
        taken, refs[:number] = refs[:number], []
        return taken

    weights_ref, gq, gk, gv, ghead, gtail = pop(6)
    if top:
        (whole,) = pop(1)
    else:
        pop(1)
    if bottom:
        after_ref, *ahead_of = pop(5)
    out_hbm, zero_ref = pop(2)
    copies = []
    out_s, o_s, sems = refs[-3:]
    reach = taps - 1
    groups = weights_ref.shape[2]
    columns = groups // LANES
    length = gq.shape[1] // repeats
    zero_ref[...] = jnp.zeros_like(zero_ref)
    if top:
        (mixed_hbm,) = pop(1)
        copies = [pltpu.make_async_copy(whole, mixed_hbm, sems.at[steps])]
        for copy in copies:
            copy.start()

    def load(bank, column, token):
        if token >= length:
            return Tokens(refs[0], repeats, 0, (bank, column))[token - length]
        if token < (reach if bank else 2 * reach):
            return Tokens(ghead, repeats, 0, (bank, column))[token]
        if bank and token >= length - reach:
            return Tokens(gtail, repeats, reach - length, (bank - 1, column))[token]
        return Tokens((gq, gk, gv)[bank], repeats, 0, (column,))[token]

    def next_shard(column, carry):
        gnext, p_s, gm_s = refs[:3]
        lanes = lane_slice(column)
        wq, wk, wv, wm = (weight_rows(weights_ref, bank, lanes) for bank in range(4))
        p_t, gm_t = (Tokens(ref, repeats) for ref in (p_s, gm_s))
        h_t = Halo(after_ref, repeats, columns).tokens(column)
        q_t, k_t, v_t, p_i = (
            Held(ref, repeats, column, held_tokens(reach)[which])
            for ref, which in zip(ahead_of, (0, 1, 2, 6))
        )
        q_w = Window(lambda t: q_t[t] if t < 0 else h_t[t])
        k_w = Window(lambda t: k_t[t] if t < 0 else h_t[4 * reach + t])
        v_w = Window(lambda t: v_t[t] if t < 0 else h_t[5 * reach + t])
        p_w = Window(lambda t: p_i[t] if t < 0 else p_t[t])
        gm_w = Window(lambda t: gm_t[t])
        next_q, next_k, next_v = (
            Tokens(gnext, repeats, 0, (bank, column)) for bank in range(3)
        )
        for token in range(2 * reach):
            gm_t[token] = h_t[2 * reach + token] * dot_taps(wq, q_w.back(token, taps))
        for token in range(reach):
            kc = dot_taps(wk, k_w.back(token, taps))
            vc = dot_taps(wv, v_w.back(token, taps))
            p_t[token] = kc * vc
            gp = dot_taps(wm, gm_w.ahead(token, taps))
            next_k[token] = gp * vc
            next_v[token] = gp * kc
            next_q[token] = h_t[2 * reach + token] * dot_taps(wm, p_w.back(token, taps))
        return carry

    def out_copy(slot):
        rows = slice((first + slot) * CHUNK, (first + slot + 1) * CHUNK)
        return pltpu.make_async_copy(out_s.at[slot], out_hbm.at[:, rows, :], sems.at[slot])

    if bottom:
        lax.fori_loop(0, columns, next_shard, 0)
    for slot in range(steps):
        base = (first + slot) * CHUNK

        def column_step(column, carry):
            lanes = lane_slice(column)
            o_t = Tokens(o_s, repeats)
            for bank in range(3):
                weights = weight_rows(weights_ref, bank, lanes)
                window = Window(lambda t: load(bank, column, base + t))
                for token in range(CHUNK):
                    o_t[token] = dot_taps(weights, window.ahead(token, taps))
                for repeat in range(repeats):
                    part = part_slice(repeat, groups, column)
                    out_s[slot, bank, :, part] = o_t.take(0, repeat, CHUNK).astype(out_s.dtype)
            return carry

        lax.fori_loop(0, columns, column_step, 0)
        out_copy(slot).start()
    for slot in range(steps):
        out_copy(slot).wait()
    for copy in copies:
        copy.wait()


def feature_gradients(
    piece, pieces, features, weights, grads, ghead, gtail, mixed, after, arrays, earlier, zero
):
    banks, length, channels = features.shape
    taps, _, groups = weights.shape
    repeats = channels // groups
    columns = groups // LANES
    reach = taps - 1
    count = length // CHUNK
    steps = count // pieces
    first = piece * steps
    operands = [weights, *grads, ghead, gtail]
    in_specs = [VMEM_SPEC] * len(operands)
    out_shape = [jax.ShapeDtypeStruct(features.shape, features.dtype), zero]
    out_specs = [ANY_SPEC, VMEM_SPEC]
    aliases = {}
    scratch = []
    if piece == 0:
        operands.append(mixed)
        in_specs.append(VMEM_SPEC)
        out_shape.append(jax.ShapeDtypeStruct(mixed.shape, mixed.dtype))
        out_specs.append(ANY_SPEC)
    else:
        aliases = {len(operands): 0}
        operands.append(earlier)
        in_specs.append(ANY_SPEC)
    if piece == pieces - 1:
        q_a, k_a, v_a, _, _, _, p_a, _ = arrays
        operands += [after, q_a, k_a, v_a, p_a]
        in_specs += [VMEM_SPEC] * 5
        scratch = [
            pltpu.VMEM((3, columns, reach * repeats, LANES), F32),
            pltpu.VMEM((reach * repeats, LANES), F32),
            pltpu.VMEM((2 * reach * repeats, LANES), F32),
        ]
    work = length * channels * taps * 2 // pieces
    return pl.pallas_call(
        functools.partial(grads_kernel, taps, repeats, first, steps, count),
        out_shape=out_shape,
        in_specs=in_specs,
        out_specs=out_specs,
        scratch_shapes=scratch
        + [
            pltpu.VMEM((steps, banks, CHUNK, channels), features.dtype),
            pltpu.VMEM((CHUNK * repeats, LANES), F32),
            pltpu.SemaphoreType.DMA((steps + 1,)),
        ],
        input_output_aliases=aliases,
        cost_estimate=pl.CostEstimate(
            flops=4 * work,
            bytes_accessed=18 * length * channels // pieces,
            transcendentals=0,
        ),
        compiler_params=pltpu.CompilerParams(vmem_limit_bytes=VMEM_LIMIT),
        name="feature_gradients",
    )(*operands)


def per_device(features, cotangent, master_filters):
    length = features.shape[1]
    near, far, rounded = pack(
        features,
        cotangent,
        jnp.transpose(master_filters, (1, 0, 2)),
        master_filters.shape[2] * lax.axis_size("fsdp"),
    )
    weights = gather_filters(rounded, "fsdp").astype(F32)
    halos = swap_pairs(near, far, "ctx")
    middle, grads, arrays, sums = interior(features, cotangent, weights)
    top, ghead, gtail, after, *sums = edge(weights, *halos, sums, arrays)
    repeats = features.shape[2] // weights.shape[2]
    pieces = PIECES if (length // CHUNK) % PIECES == 0 else 1
    zero = jax.ShapeDtypeStruct(
        (*weights.shape[:2], weights.shape[2] // lax.axis_size("fsdp")), F32
    )
    whole, nothing = round_mixed(middle, top, cotangent, zero)
    owned = sum_scatter(sums, "fsdp") + nothing
    made = {"grads": None}

    def beside(piece):
        if piece >= pieces:
            return 0.0
        made["grads"], nothing, *rest = feature_gradients(
            piece,
            pieces,
            features,
            weights,
            grads,
            ghead,
            gtail,
            whole,
            after,
            arrays,
            made["grads"],
            zero,
        )
        if rest:
            made["mixed"] = rest[0]
        return nothing

    summed, done = sum_over(owned, "ctx", beside)
    for piece in range(done, pieces):
        beside(piece)
    count_all = length * lax.axis_size("ctx") * repeats * lax.axis_size("fsdp")
    filter_grads = jnp.transpose(summed * (1.0 / math.sqrt(count_all)), (1, 0, 2))
    return (made["mixed"], made["grads"], filter_grads)


def solution(mesh):
    return jax.shard_map(
        per_device,
        mesh=mesh,
        in_specs=(P(None, "ctx", "fsdp"), P("ctx", "fsdp"), P(None, None, "fsdp")),
        out_specs=(P("ctx", "fsdp"), P(None, "ctx", "fsdp"), P(None, None, "fsdp")),
        check_vma=False,
    )
```

```python
import functools
import math

import jax
import jax.numpy as jnp
from jax import lax
from jax.experimental import pallas as pl
from jax.experimental.pallas import tpu as pltpu
from jax.sharding import PartitionSpec as P

LANES = 128
CHUNK = 16
PAD = 16
PIECES = 4
VMEM_LIMIT = 28 * 1024 * 1024
PACK_LIMIT = 16 * 1024 * 1024
F32 = jnp.float32
VMEM_SPEC = pl.BlockSpec(memory_space=pltpu.VMEM)
ANY_SPEC = pl.BlockSpec(memory_space=pl.ANY)


def swap_pairs(near, far, axis):
    size = lax.axis_size(axis)
    inner = [(i, i ^ 1) for i in range(size) if i ^ 1 < size]
    outer = [(i, i - 1 if i % 2 == 0 else i + 1) for i in range(size)]
    outer = [(i, j) for i, j in outer if 0 <= j < size]
    far = lax.ppermute(far, axis, outer)
    near = lax.ppermute(near, axis, inner)
    return near, far


def is_even(axis):
    return lax.rem(lax.axis_index(axis), 2) == 0


def gather_filters(shard, axis):
    size = lax.axis_size(axis)
    if size != 2:
        return lax.all_gather(shard, axis, axis=2, tiled=True)
    other = lax.ppermute(shard, axis, [(0, 1), (1, 0)])
    first = lax.axis_index(axis) == 0
    return jnp.concatenate(
        [jnp.where(first, shard, other), jnp.where(first, other, shard)], axis=2
    )


def sum_over(value, axis, beside=None):
    size = lax.axis_size(axis)
    if size & (size - 1):
        return lax.psum(value, axis), 0
    rounds = size.bit_length() - 1
    for step in range(rounds):
        pairs = [(i, i ^ (1 << step)) for i in range(size)]
        received = lax.ppermute(value, axis, pairs)
        value = value + received
        if beside is not None:
            value = value + beside(step)
    return value, rounds


def sum_scatter(parts, axis):
    if len(parts) == 2:
        kept, sent = parts
        return kept + lax.ppermute(sent, axis, [(0, 1), (1, 0)])
    (value,) = parts
    portion = value.shape[-1] // lax.axis_size(axis)
    total, _ = sum_over(value, axis)
    return lax.dynamic_slice_in_dim(
        total, lax.axis_index(axis) * portion, portion, value.ndim - 1
    )


def dot_taps(weights, pieces):
    total = weights[0] * pieces[0]
    for weight, piece in zip(weights[1:], pieces[1:]):
        total = total + weight * piece
    return total


def weight_rows(ref, bank, lanes):
    return [ref[lag, pl.ds(bank, 1), lanes] for lag in range(ref.shape[0])]


def lane_slice(index):
    return pl.ds(pl.multiple_of(index * LANES, LANES), LANES)


def part_slice(repeat, groups, column):
    return pl.ds(pl.multiple_of(repeat * groups + column * LANES, LANES), LANES)


class Tokens:
    def __init__(self, ref, repeats, origin=0, lead=()):
        self.ref, self.repeats, self.origin, self.lead = ref, repeats, origin, lead

    def rows(self, token, count=1):
        start = (self.origin + token) * self.repeats
        if not isinstance(start, int):
            start = pl.multiple_of(start, self.repeats)
        return pl.ds(start, count * self.repeats)

    def __getitem__(self, token):
        return self.ref[(*self.lead, self.rows(token), slice(None))]

    def __setitem__(self, token, value):
        self.ref[(*self.lead, self.rows(token), slice(None))] = value

    def strided(self, token, repeat, count):
        start = (self.origin + token) * self.repeats + repeat
        return pl.ds(start, count, stride=self.repeats)

    def put(self, token, repeat, value):
        rows = self.strided(token, repeat, value.shape[0])
        self.ref[(*self.lead, rows, slice(None))] = value

    def take(self, token, repeat, count):
        return self.ref[(*self.lead, self.strided(token, repeat, count), slice(None))]


class Halo:
    def __init__(self, ref, repeats, columns):
        self.ref, self.repeats, self.columns = ref, repeats, columns

    def put(self, token, column, repeat, value):
        start = (token * self.columns + column) * self.repeats + repeat
        rows = pl.ds(start, value.shape[0], stride=self.columns * self.repeats)
        self.ref[rows, :] = value

    def tokens(self, column):
        class View:
            def __getitem__(_, token):
                start = (token * self.columns + column) * self.repeats
                if not isinstance(start, int):
                    start = pl.multiple_of(start, self.repeats)
                return self.ref[pl.ds(start, self.repeats), :]

        return View()


def held_tokens(reach):
    wide = 2 * reach
    return (
        (0, wide, reach),
        (0, reach, wide),
        (0, reach, wide),
        (0, wide, 0),
        (0, 0, reach),
        (0, 0, reach),
        (reach, wide, reach),
        (0, 0, reach),
    )


class Held:
    def __init__(self, ref, repeats, column, span):
        self.first, self.last, self.tail = span
        self.view = Tokens(ref, repeats, 0, (column,))

    def __getitem__(self, token):
        if token < 0:
            return self.view[self.last - self.first + self.tail + token]
        return self.view[token - self.first]


class Window:
    def __init__(self, load):
        self.load, self.held = load, {}

    def __call__(self, token):
        if token not in self.held:
            self.held[token] = self.load(token)
        return self.held[token]

    def back(self, token, taps):
        return [self(token - lag) for lag in range(taps)]

    def ahead(self, token, taps):
        return [self(token + lag) for lag in range(taps)]


class Sums:
    def __init__(self, taps):
        self.taps = taps
        self.held = {}

    def add(self, bank, grad, pieces):
        for lag, piece in enumerate(pieces):
            term = grad * piece
            old = self.held.get((bank, lag))
            self.held[bank, lag] = term if old is None else old + term

    def store(self, ref, lanes):
        for (bank, lag), value in self.held.items():
            ref[bank, lag, :, lanes] += value


def pack_kernel(
    reach,
    columns,
    features_hbm,
    cotangent_hbm,
    master_hbm,
    near_ref,
    far_ref,
    rounded_ref,
    tail,
    head,
    upstream,
    master,
    b_s,
    a_s,
    sems,
):
    length = cotangent_hbm.shape[0]
    copies = [
        pltpu.make_async_copy(features_hbm.at[:, length - PAD :, :], tail, sems.at[0]),
        pltpu.make_async_copy(features_hbm.at[:, :PAD, :], head, sems.at[1]),
        pltpu.make_async_copy(cotangent_hbm.at[:PAD, :], upstream, sems.at[2]),
        pltpu.make_async_copy(master_hbm, master, sems.at[3]),
    ]
    for copy in copies:
        copy.start()
    even = is_even("ctx")
    repeats = upstream.shape[1] // (columns * LANES)
    block = reach * columns * repeats
    b_s[5 * block : 6 * block, :] = jnp.zeros((block, LANES), F32)
    last, first = Halo(b_s, repeats, columns), Halo(a_s, repeats, columns)
    wide = 2 * reach

    def place(message, parts):
        def repeat_step(repeat, carry):
            for column in range(columns):
                lanes = lane_slice(repeat * columns + column)
                for token, ref, start, stop in parts:
                    value = ref[:, lanes].astype(F32)[start:stop]
                    message.put(token, column, repeat, value)
            return carry

        lax.fori_loop(0, repeats, repeat_step, 0, unroll=True)

    copies[0].wait()
    place(
        last,
        (
            (0, tail.at[0], PAD - reach, PAD),
            (reach, tail.at[1], PAD - wide, PAD),
            (3 * reach, tail.at[2], PAD - wide, PAD),
        ),
    )
    for copy in copies[1:]:
        copy.wait()
    rounded_ref[...] = master[...].astype(rounded_ref.dtype)
    place(
        first,
        (
            (0, head.at[0], 0, wide),
            (wide, upstream, 0, wide),
            (2 * wide, head.at[1], 0, reach),
            (5 * reach, head.at[2], 0, reach),
        ),
    )
    ending, opening = b_s[: 6 * block, :], a_s[: 6 * block, :]
    near_ref[...] = jnp.where(even, ending, opening).astype(near_ref.dtype)
    far_ref[...] = jnp.where(even, opening, ending).astype(far_ref.dtype)


def pack(features, cotangent, master, groups):
    reach = master.shape[0] - 1
    banks, length, channels = features.shape
    kind = features.dtype
    hbm = [
        pltpu.with_memory_space_constraint(value, pltpu.HBM)
        for value in (features, cotangent, master)
    ]
    message = jax.ShapeDtypeStruct((6 * reach * channels // LANES, LANES), kind)
    room = ((6 * reach + 8) * channels // LANES, LANES)
    return pl.pallas_call(
        functools.partial(pack_kernel, reach, groups // LANES),
        out_shape=(message, message, jax.ShapeDtypeStruct(master.shape, jnp.bfloat16)),
        in_specs=[pl.BlockSpec(memory_space=pltpu.HBM)] * 3,
        out_specs=(VMEM_SPEC,) * 3,
        scratch_shapes=[
            pltpu.VMEM((banks, PAD, channels), kind),
            pltpu.VMEM((banks, PAD, channels), kind),
            pltpu.VMEM((PAD, channels), kind),
            pltpu.VMEM(master.shape, F32),
            pltpu.VMEM(room, F32),
            pltpu.VMEM(room, F32),
            pltpu.SemaphoreType.DMA((4,)),
        ],
        cost_estimate=pl.CostEstimate(flops=10**6, bytes_accessed=10**6, transcendentals=0),
        compiler_params=pltpu.CompilerParams(vmem_limit_bytes=PACK_LIMIT),
        name="pack_halos",
    )(*hbm)


def interior_kernel(
    taps,
    repeats,
    features_ref,
    cotangent_hbm,
    weights_ref,
    mixed_ref,
    gq_ref,
    gk_ref,
    gv_ref,
    *refs,
):
    *held_refs, sums_ref = refs[:9]
    *work_refs, cotangent_ref, sem = refs[9:]
    *work_refs, k_other, v_other = work_refs
    q_s, k_s, v_s, c_s, kc_s, vc_s, p_s, gm_s = work_refs
    pairs = ((k_s, v_s), (k_other, v_other))
    reach = taps - 1
    groups = weights_ref.shape[2]
    length = cotangent_ref.shape[0]
    count = length // CHUNK
    fetch = pltpu.make_async_copy(cotangent_hbm, cotangent_ref, sem)
    fetch.start()
    sums_ref[...] = jnp.zeros_like(sums_ref)

    def part_of(repeat, column):
        first = repeat * groups + column * LANES
        return slice(first, first + LANES)

    zero = jnp.zeros((reach * repeats, LANES), F32)
    for ref in (q_s, p_s, k_s, v_s, k_other, v_other):
        ref[(PAD - reach) * repeats : PAD * repeats, :] = zero
    gm_s[(PAD + length) * repeats : (PAD + length + reach) * repeats, :] = zero
    q_t, c_t, kc_t, vc_t, p_t, gm_t = (
        Tokens(ref, repeats, PAD) for ref in (q_s, c_s, kc_s, vc_s, p_s, gm_s)
    )
    columns = groups // LANES

    def put_pair(column, base, rows):
        for bank, ref in enumerate(pairs[column % 2]):
            view = Tokens(ref, repeats, PAD)
            for repeat in range(repeats):
                part = part_of(repeat, column)
                view.put(base, repeat, features_ref[1 + bank, rows, part].astype(F32))

    def chunks(body):
        def step_body(step, carry):
            base = pl.multiple_of(step * CHUNK, CHUNK)
            body(step, base, pl.ds(base, CHUNK))
            return carry

        lax.fori_loop(0, count, step_body, 0)

    chunks(lambda step, base, rows: put_pair(0, base, rows))
    for column in range(columns):
        lanes = slice(column * LANES, (column + 1) * LANES)
        m_t, gq_t, gk_t, gv_t = (
            Tokens(ref, repeats, 0, (column,)) for ref in (mixed_ref, gq_ref, gk_ref, gv_ref)
        )
        k_t, v_t = (Tokens(ref, repeats, PAD) for ref in pairs[column % 2])
        wq, wk, wv, wm = (weight_rows(weights_ref, bank, lanes) for bank in range(4))

        def products(step, base, rows):
            for repeat in range(repeats):
                part = part_of(repeat, column)
                q_t.put(base, repeat, features_ref[0, rows, part].astype(F32))
            k_w, v_w = (Window(lambda t, view=view: view[base + t]) for view in (k_t, v_t))
            for token in range(CHUNK):
                kc = dot_taps(wk, k_w.back(token, taps))
                vc = dot_taps(wv, v_w.back(token, taps))
                kc_t[base + token] = kc
                vc_t[base + token] = vc
                p_t[base + token] = kc * vc

        def forward(step, base, rows):
            for repeat in range(repeats):
                part = part_of(repeat, column)
                c_t.put(base, repeat, cotangent_ref[rows, part].astype(F32))
            if column + 1 < columns:
                put_pair(column + 1, base, rows)
            sums = Sums(taps)
            q_w, p_w = (Window(lambda t, view=view: view[base + t]) for view in (q_t, p_t))
            for token in range(CHUNK):
                up = c_t[base + token]
                sources = q_w.back(token, taps)
                inner = p_w.back(token, taps)
                qc = dot_taps(wq, sources)
                mixer = dot_taps(wm, inner)
                gq = up * mixer
                gm = up * qc
                m_t[base + token] = qc * mixer
                gm_t[base + token] = gm
                gq_t[base + token] = gq
                if token < 2 * reach:
                    gq = jnp.where(step > 0, gq, 0.0)
                    gm = jnp.where(step > 0, gm, 0.0)
                sums.add(0, gq, sources)
                sums.add(3, gm, inner)
            sums.store(sums_ref, lanes)

        def backward(step, base, rows):
            k_w, v_w, gm_w = (
                Window(lambda t, view=view: view[base + t]) for view in (k_t, v_t, gm_t)
            )
            sums = Sums(taps)
            for token in range(CHUNK):
                gp = dot_taps(wm, gm_w.ahead(token, taps))
                if token < reach:
                    gp = jnp.where(step > 0, gp, 0.0)
                if token >= CHUNK - reach:
                    gp = jnp.where(step < count - 1, gp, 0.0)
                gk = gp * vc_t[base + token]
                gv = gp * kc_t[base + token]
                gk_t[base + token] = gk
                gv_t[base + token] = gv
                sums.add(1, gk, k_w.back(token, taps))
                sums.add(2, gv, v_w.back(token, taps))
            sums.store(sums_ref, lanes)

        chunks(products)
        if column == 0:
            fetch.wait()
        chunks(forward)
        chunks(backward)
        sources = (q_s, *pairs[column % 2], c_s, kc_s, vc_s, p_s, gm_s)
        for ref, work, (first, last, tail) in zip(held_refs, sources, held_tokens(reach)):
            target, source = Tokens(ref, repeats, 0, (column,)), Tokens(work, repeats, PAD)
            for token in (*range(first, last), *range(length - tail, length)):
                row = token - first if token < last else token - length + last - first + tail
                target[row] = source[token]


def interior(features, cotangent, weights):
    length, channels = cotangent.shape
    taps, banks, groups = weights.shape
    repeats = channels // groups
    columns = groups // LANES
    work = length * channels * taps * 2
    grad = jax.ShapeDtypeStruct((columns, length * repeats, LANES), F32)
    held = [
        jax.ShapeDtypeStruct((columns, (last - first + tail) * repeats, LANES), F32)
        for first, last, tail in held_tokens(taps - 1)
    ]
    work_shape = ((length + 2 * PAD) * repeats, LANES)
    mixed, gq, gk, gv, *arrays, sums = pl.pallas_call(
        functools.partial(interior_kernel, taps, repeats),
        out_shape=(
            *[grad] * 4,
            *held,
            jax.ShapeDtypeStruct((banks, taps, repeats, groups), F32),
        ),
        in_specs=[VMEM_SPEC, pl.BlockSpec(memory_space=pltpu.HBM), VMEM_SPEC],
        out_specs=(VMEM_SPEC,) * 13,
        scratch_shapes=[pltpu.VMEM(work_shape, F32) for _ in range(10)]
        + [
            pltpu.VMEM(cotangent.shape, cotangent.dtype),
            pltpu.SemaphoreType.DMA,
        ],
        cost_estimate=pl.CostEstimate(
            flops=9 * work, bytes_accessed=22 * length * channels, transcendentals=0
        ),
        compiler_params=pltpu.CompilerParams(vmem_limit_bytes=VMEM_LIMIT),
        name="interior",
    )(features, pltpu.with_memory_space_constraint(cotangent, pltpu.HBM), weights)
    return mixed, (gq, gk, gv), arrays, sums


def edge_kernel(
    taps,
    repeats,
    weights_ref,
    near_ref,
    far_ref,
    sums_in_ref,
    q_a,
    k_a,
    v_a,
    c_a,
    kc_a,
    vc_a,
    p_a,
    gm_a,
    mixed_ref,
    ghead_ref,
    gtail_ref,
    after_ref,
    *refs,
):
    *sums_out, sums_ref, before_s, kc_s, vc_s, p_s, gm_s = refs
    reach = taps - 1
    groups = weights_ref.shape[2]
    even = is_even("ctx")
    columns = groups // LANES
    near, far = near_ref[...].astype(F32), far_ref[...].astype(F32)
    before_s[...] = jnp.where(even, far, near)
    after_ref[...] = jnp.where(even, near, far)

    for column in range(columns):
        lanes = slice(column * LANES, (column + 1) * LANES)
        kc_t, vc_t, p_t, gm_t = (
            Tokens(ref, repeats, reach, (column,)) for ref in (kc_s, vc_s, p_s, gm_s)
        )
        wq, wk, wv, wm = (weight_rows(weights_ref, bank, lanes) for bank in range(4))
        q_t, k_t, v_t, c_t, kc_i, vc_i, p_i, gm_i = (
            Held(ref, repeats, column, span)
            for ref, span in zip(
                (q_a, k_a, v_a, c_a, kc_a, vc_a, p_a, gm_a), held_tokens(reach)
            )
        )
        sums = Sums(taps)

        h_t = Halo(before_s, repeats, columns).tokens(column)
        q_w = Window(lambda t: q_t[t] if t >= 0 else h_t[reach + t])
        k_w = Window(lambda t: k_t[t] if t >= 0 else h_t[3 * reach + t])
        v_w = Window(lambda t: v_t[t] if t >= 0 else h_t[5 * reach + t])
        gq_o, gk_o, gv_o = (Tokens(ghead_ref, repeats, 0, (bank, column)) for bank in range(3))
        m_o = Tokens(mixed_ref, repeats, 0, (column,))
        for token in range(-reach, reach):
            kc = dot_taps(wk, k_w.back(token, taps))
            vc = dot_taps(wv, v_w.back(token, taps))
            p_t[token] = kc * vc
            if token >= 0:
                kc_t[token] = kc
                vc_t[token] = vc
        p_w = Window(lambda t: p_t[t] if t < reach else p_i[t])
        for token in range(2 * reach):
            up = c_t[token]
            sources = q_w.back(token, taps)
            products = p_w.back(token, taps)
            qc = dot_taps(wq, sources)
            mixer = dot_taps(wm, products)
            gq = up * mixer
            gm = up * qc
            m_o[token] = qc * mixer
            gm_t[token] = gm
            gq_o[token] = gq
            sums.add(0, gq, sources)
            sums.add(3, gm, products)
        gm_w = Window(lambda t: gm_t[t])
        for token in range(reach):
            gp = dot_taps(wm, gm_w.ahead(token, taps))
            gk = gp * vc_t[token]
            gv = gp * kc_t[token]
            gk_o[token] = gk
            gv_o[token] = gv
            sums.add(1, gk, k_w.back(token, taps))
            sums.add(2, gv, v_w.back(token, taps))

        n_t = Halo(after_ref, repeats, columns).tokens(column)
        q_w = Window(lambda t: q_t[t] if t < 0 else n_t[t])
        gk_o, gv_o = (Tokens(gtail_ref, repeats, reach, (bank, column)) for bank in range(2))
        for token in range(reach):
            gm_t[token] = n_t[2 * reach + token] * dot_taps(wq, q_w.back(token, taps))
        gm_w = Window(lambda t: gm_i[t] if t < 0 else gm_t[t])
        k_w, v_w = (Window(lambda t, view=view: view[t]) for view in (k_t, v_t))
        for token in range(-reach, 0):
            gp = dot_taps(wm, gm_w.ahead(token, taps))
            gk = gp * vc_i[token]
            gv = gp * kc_i[token]
            gk_o[token] = gk
            gv_o[token] = gv
            sums.add(1, gk, k_w.back(token, taps))
            sums.add(2, gv, v_w.back(token, taps))
        for (bank, lag), value in sums.held.items():
            total = sums_in_ref[bank, lag, :, lanes] + value
            sums_ref[lag, bank : bank + 1, lanes] = jnp.sum(total, axis=0, keepdims=True)
    if len(sums_out) == 1:
        sums_out[0][...] = sums_ref[...]
    else:
        low, high = sums_ref[:, :, : groups // 2], sums_ref[:, :, groups // 2 :]
        first = lax.axis_index("fsdp") == 0
        sums_out[0][...] = jnp.where(first, low, high)
        sums_out[1][...] = jnp.where(first, high, low)


def edge(weights, near, far, sums, arrays):
    taps, banks, groups = weights.shape
    columns = groups // LANES
    reach = taps - 1
    repeats = near.shape[0] // (6 * reach * columns)
    parts = 2 if lax.axis_size("fsdp") == 2 else 1
    return pl.pallas_call(
        functools.partial(edge_kernel, taps, repeats),
        out_shape=(
            jax.ShapeDtypeStruct((columns, 2 * reach * repeats, LANES), F32),
            jax.ShapeDtypeStruct((3, columns, 2 * reach * repeats, LANES), F32),
            jax.ShapeDtypeStruct((2, columns, reach * repeats, LANES), F32),
            jax.ShapeDtypeStruct(near.shape, F32),
            *[jax.ShapeDtypeStruct((taps, banks, groups // parts), F32)] * parts,
        ),
        in_specs=[VMEM_SPEC] * 12,
        out_specs=(VMEM_SPEC,) * (4 + parts),
        scratch_shapes=[
            pltpu.VMEM((taps, banks, groups), F32),
            pltpu.VMEM(near.shape, F32),
        ]
        + [pltpu.VMEM((columns, 3 * reach * repeats, LANES), F32) for _ in range(4)],
        cost_estimate=pl.CostEstimate(
            flops=10**7, bytes_accessed=4 * 10**6, transcendentals=0
        ),
        compiler_params=pltpu.CompilerParams(vmem_limit_bytes=VMEM_LIMIT),
        name="edge",
    )(weights, near, far, sums, *arrays)


def mixed_kernel(repeats, middle, top, out_ref, zero_ref, o_s):
    columns, rows, _ = middle.shape
    groups = columns * LANES
    ready = top.shape[1] // repeats
    zero_ref[...] = jnp.zeros_like(zero_ref)

    def column_step(column, carry):
        m_t, t_t = (Tokens(ref, repeats, 0, (column,)) for ref in (middle, top))
        o_t = Tokens(o_s, repeats)
        for token in range(CHUNK):
            o_t[token] = t_t[token] if token < ready else m_t[token]
        for repeat in range(repeats):
            part = part_slice(repeat, groups, column)
            out_ref[:CHUNK, part] = o_t.take(0, repeat, CHUNK).astype(out_ref.dtype)

        def chunk_step(chunk, carry):
            base = pl.multiple_of(chunk * CHUNK, CHUNK)
            for repeat in range(repeats):
                part = part_slice(repeat, groups, column)
                value = m_t.take(base, repeat, CHUNK)
                out_ref[pl.ds(base, CHUNK), part] = value.astype(out_ref.dtype)
            return carry

        return lax.fori_loop(1, rows // repeats // CHUNK, chunk_step, carry)

    lax.fori_loop(0, columns, column_step, 0)


def round_mixed(middle, top, cotangent, zero):
    columns, rows, _ = middle.shape
    length, channels = cotangent.shape
    repeats = rows // length
    return pl.pallas_call(
        functools.partial(mixed_kernel, repeats),
        out_shape=(jax.ShapeDtypeStruct(cotangent.shape, cotangent.dtype), zero),
        in_specs=[VMEM_SPEC] * 2,
        out_specs=(VMEM_SPEC,) * 2,
        scratch_shapes=[pltpu.VMEM((CHUNK * repeats, LANES), F32)],
        cost_estimate=pl.CostEstimate(
            flops=length * channels, bytes_accessed=6 * length * channels, transcendentals=0
        ),
        compiler_params=pltpu.CompilerParams(vmem_limit_bytes=VMEM_LIMIT),
        name="round_mixed",
    )(middle, top)


def grads_kernel(taps, repeats, first, steps, count, *refs):
    refs = list(refs)
    top, bottom = first == 0, first + steps == count

    def pop(number):
        taken, refs[:number] = refs[:number], []
        return taken

    weights_ref, gq, gk, gv, ghead, gtail = pop(6)
    if top:
        (whole,) = pop(1)
    else:
        pop(1)
    if bottom:
        after_ref, *ahead_of = pop(5)
    out_hbm, zero_ref = pop(2)
    copies = []
    out_s, o_s, sems = refs[-3:]
    reach = taps - 1
    groups = weights_ref.shape[2]
    columns = groups // LANES
    length = gq.shape[1] // repeats
    zero_ref[...] = jnp.zeros_like(zero_ref)
    if top:
        (mixed_hbm,) = pop(1)
        copies = [pltpu.make_async_copy(whole, mixed_hbm, sems.at[steps])]
        for copy in copies:
            copy.start()

    def load(bank, column, token):
        if token >= length:
            return Tokens(refs[0], repeats, 0, (bank, column))[token - length]
        if token < (reach if bank else 2 * reach):
            return Tokens(ghead, repeats, 0, (bank, column))[token]
        if bank and token >= length - reach:
            return Tokens(gtail, repeats, reach - length, (bank - 1, column))[token]
        return Tokens((gq, gk, gv)[bank], repeats, 0, (column,))[token]

    def next_shard(column, carry):
        gnext, p_s, gm_s = refs[:3]
        lanes = lane_slice(column)
        wq, wk, wv, wm = (weight_rows(weights_ref, bank, lanes) for bank in range(4))
        p_t, gm_t = (Tokens(ref, repeats) for ref in (p_s, gm_s))
        h_t = Halo(after_ref, repeats, columns).tokens(column)
        q_t, k_t, v_t, p_i = (
            Held(ref, repeats, column, held_tokens(reach)[which])
            for ref, which in zip(ahead_of, (0, 1, 2, 6))
        )
        q_w = Window(lambda t: q_t[t] if t < 0 else h_t[t])
        k_w = Window(lambda t: k_t[t] if t < 0 else h_t[4 * reach + t])
        v_w = Window(lambda t: v_t[t] if t < 0 else h_t[5 * reach + t])
        p_w = Window(lambda t: p_i[t] if t < 0 else p_t[t])
        gm_w = Window(lambda t: gm_t[t])
        next_q, next_k, next_v = (
            Tokens(gnext, repeats, 0, (bank, column)) for bank in range(3)
        )
        for token in range(2 * reach):
            gm_t[token] = h_t[2 * reach + token] * dot_taps(wq, q_w.back(token, taps))
        for token in range(reach):
            kc = dot_taps(wk, k_w.back(token, taps))
            vc = dot_taps(wv, v_w.back(token, taps))
            p_t[token] = kc * vc
            gp = dot_taps(wm, gm_w.ahead(token, taps))
            next_k[token] = gp * vc
            next_v[token] = gp * kc
            next_q[token] = h_t[2 * reach + token] * dot_taps(wm, p_w.back(token, taps))
        return carry

    def out_copy(slot):
        rows = slice((first + slot) * CHUNK, (first + slot + 1) * CHUNK)
        return pltpu.make_async_copy(out_s.at[slot], out_hbm.at[:, rows, :], sems.at[slot])

    if bottom:
        lax.fori_loop(0, columns, next_shard, 0)
    for slot in range(steps):
        base = (first + slot) * CHUNK

        def column_step(column, carry):
            lanes = lane_slice(column)
            o_t = Tokens(o_s, repeats)
            for bank in range(3):
                weights = weight_rows(weights_ref, bank, lanes)
                window = Window(lambda t: load(bank, column, base + t))
                for token in range(CHUNK):
                    o_t[token] = dot_taps(weights, window.ahead(token, taps))
                for repeat in range(repeats):
                    part = part_slice(repeat, groups, column)
                    out_s[slot, bank, :, part] = o_t.take(0, repeat, CHUNK).astype(out_s.dtype)
            return carry

        lax.fori_loop(0, columns, column_step, 0)
        out_copy(slot).start()
    for slot in range(steps):
        out_copy(slot).wait()
    for copy in copies:
        copy.wait()


def feature_gradients(
    piece, pieces, features, weights, grads, ghead, gtail, mixed, after, arrays, earlier, zero
):
    banks, length, channels = features.shape
    taps, _, groups = weights.shape
    repeats = channels // groups
    columns = groups // LANES
    reach = taps - 1
    count = length // CHUNK
    steps = count // pieces
    first = piece * steps
    operands = [weights, *grads, ghead, gtail]
    in_specs = [VMEM_SPEC] * len(operands)
    out_shape = [jax.ShapeDtypeStruct(features.shape, features.dtype), zero]
    out_specs = [ANY_SPEC, VMEM_SPEC]
    aliases = {}
    scratch = []
    if piece == 0:
        operands.append(mixed)
        in_specs.append(VMEM_SPEC)
        out_shape.append(jax.ShapeDtypeStruct(mixed.shape, mixed.dtype))
        out_specs.append(ANY_SPEC)
    else:
        aliases = {len(operands): 0}
        operands.append(earlier)
        in_specs.append(ANY_SPEC)
    if piece == pieces - 1:
        q_a, k_a, v_a, _, _, _, p_a, _ = arrays
        operands += [after, q_a, k_a, v_a, p_a]
        in_specs += [VMEM_SPEC] * 5
        scratch = [
            pltpu.VMEM((3, columns, reach * repeats, LANES), F32),
            pltpu.VMEM((reach * repeats, LANES), F32),
            pltpu.VMEM((2 * reach * repeats, LANES), F32),
        ]
    work = length * channels * taps * 2 // pieces
    return pl.pallas_call(
        functools.partial(grads_kernel, taps, repeats, first, steps, count),
        out_shape=out_shape,
        in_specs=in_specs,
        out_specs=out_specs,
        scratch_shapes=scratch
        + [
            pltpu.VMEM((steps, banks, CHUNK, channels), features.dtype),
            pltpu.VMEM((CHUNK * repeats, LANES), F32),
            pltpu.SemaphoreType.DMA((steps + 1,)),
        ],
        input_output_aliases=aliases,
        cost_estimate=pl.CostEstimate(
            flops=4 * work,
            bytes_accessed=18 * length * channels // pieces,
            transcendentals=0,
        ),
        compiler_params=pltpu.CompilerParams(vmem_limit_bytes=VMEM_LIMIT),
        name="feature_gradients",
    )(*operands)


def per_device(features, cotangent, master_filters):
    length = features.shape[1]
    near, far, rounded = pack(
        features,
        cotangent,
        jnp.transpose(master_filters, (1, 0, 2)),
        master_filters.shape[2] * lax.axis_size("fsdp"),
    )
    weights = gather_filters(rounded, "fsdp").astype(F32)
    halos = swap_pairs(near, far, "ctx")
    middle, grads, arrays, sums = interior(features, cotangent, weights)
    top, ghead, gtail, after, *sums = edge(weights, *halos, sums, arrays)
    repeats = features.shape[2] // weights.shape[2]
    pieces = PIECES if (length // CHUNK) % PIECES == 0 else 1
    zero = jax.ShapeDtypeStruct(
        (*weights.shape[:2], weights.shape[2] // lax.axis_size("fsdp")), F32
    )
    whole, nothing = round_mixed(middle, top, cotangent, zero)
    owned = sum_scatter(sums, "fsdp") + nothing
    made = {"grads": None}

    def beside(piece):
        if piece >= pieces:
            return 0.0
        made["grads"], nothing, *rest = feature_gradients(
            piece,
            pieces,
            features,
            weights,
            grads,
            ghead,
            gtail,
            whole,
            after,
            arrays,
            made["grads"],
            zero,
        )
        if rest:
            made["mixed"] = rest[0]
        return nothing

    summed, done = sum_over(owned, "ctx", beside)
    for piece in range(done, pieces):
        beside(piece)
    count_all = length * lax.axis_size("ctx") * repeats * lax.axis_size("fsdp")
    filter_grads = jnp.transpose(summed * (1.0 / math.sqrt(count_all)), (1, 0, 2))
    return (made["mixed"], made["grads"], filter_grads)


def solution(mesh):
    return jax.shard_map(
        per_device,
        mesh=mesh,
        in_specs=(P(None, "ctx", "fsdp"), P("ctx", "fsdp"), P(None, None, "fsdp")),
        out_specs=(P("ctx", "fsdp"), P(None, "ctx", "fsdp"), P(None, None, "fsdp")),
        check_vma=False,
    )
```
